128 devices in a mesh: gx: 16 (over z, y), gy: 8 (over x, core).
Axes of the slice: x: 4, y: 4, z: 4, core: 2. Of those that a mesh axis runs over, the one named last changes fastest.
Arguments:
- field: float32 [256, 1024, 512], P('gx', 'gy'), may hold values from -6144 to 6144
- conduct: float32 [256, 1024, 512], P('gx', 'gy'), may hold values from 0.2 to 4
- seg_cell: int32 [128, 128, 4], P(('gx', 'gy')), may hold values from 0 to 1048575
- seg_count: int32 [128, 128], P(('gx', 'gy')), may hold values from 1 to 4, as said below
- currents: float32 [128, 128, 4], P(('gx', 'gy')), may hold values from -6 to 6
- coupling: bfloat16 [128, 512, 512], P(('gx', 'gy')), may hold values from -0.0048828125 to 0.0048828125
Outputs:
- field_next: float32 [256, 1024, 512], P('gx', 'gy')
- currents_next: float32 [128, 128, 4], P(('gx', 'gy'))
The draws below stay inside these ranges and needn't reach their ends.
Inputs may be any that keep to these rules, and one draw needn't show every extreme that they name: `seg_cell`: A flat cell index within the sending device's block. `seg_count`: every count is 1 to 4; for one owner drawn from the seed every sender's count is 4.
All inputs are finite; a program needn't handle non-finite values.
Results may differ from the reference program's by a relative error of at most 0.002.
Values sent between devices are 32-bit elements; how exact they have to be, the bound alone decides.
A program may use at most 256 MiB of HBM per device.

```python
import math
import jax
import jax.numpy as jnp
from jax import lax

CX = 16
CY = 128
NZ = 512
CAP = 4
NX = 256
NY = 1024
NODES = 128
WIRE = 512
N_GY = 8


def draw_seg_count(key, part):
    counts = jax.random.randint(jax.random.fold_in(key, 11), (NODES, NODES), 1, CAP + 1)
    owner = jax.random.randint(jax.random.fold_in(key, 12), (), 0, NODES)
    column = jnp.arange(NODES)[None, :] == owner
    return jnp.where(column, CAP, counts).astype(jnp.int32)


def touch_ends(result, key, low, high):
    longest = result.shape.index(max(result.shape))
    spots = []
    for shift in (0, 1):
        where = [jax.random.randint(jax.random.fold_in(key, axis), (), 0, length) for axis, length in enumerate(result.shape)]
        where[longest] = (where[longest] + shift) % result.shape[longest]
        spots.append(tuple(where))
    return result.at[spots[0]].set(low).at[spots[1]].set(high)


def levels(stream_key, shape, pieces, least, top_value):
    def one(dim, shards_of):
        draws = jax.random.uniform(jax.random.fold_in(jax.random.fold_in(stream_key, 6), dim), (shards_of,), jnp.float32, least / len(pieces), top_value / len(pieces))
        return jnp.repeat(jnp.exp(draws), shape[dim] // shards_of).reshape((-1,) + (1,) * (len(shape) - dim - 1))

    level = one(*pieces[0])
    for cut in pieces[1:]:
        level = level * one(*cut)
    return level


def centred(key, shape, deviation, limit, split=(), kind=jnp.bfloat16):
    values = jax.random.normal(key, shape, jnp.float32) * deviation
    if len(split) > 0:
        values = levels(key, shape, split, -0.22, 0.18) * values
    return jnp.clip(values, min=-limit, max=limit).astype(kind)


def setup_inputs(seed: int = 0) -> dict:
    key_list = jax.random.split(jax.random.key(seed), 7)
    field = centred(key_list[0], (NX, NY, NZ), (CX * CY // 2), 6144.0, ((0, 16), (1, 8)), jnp.float32)
    conduct = jnp.clip(jnp.exp(math.log(4.0) - 2.9957323 * jax.random.uniform(key_list[1], (NX, NY, NZ), jnp.float32) ** levels(key_list[1], (NX, NY, NZ), ((0, 16), (1, 8)), -0.2, 0.2)), 0.2, 4.0)
    seg_cell = touch_ends(jax.random.randint(key_list[2], (NODES, NODES, CAP), 0, CX * CY * NZ), jax.random.fold_in(key_list[2], 1), 0, (CX * CY * NZ) - 1).astype(jnp.int32)
    seg_count = draw_seg_count(jax.random.fold_in(key_list[6], 71), 0)
    currents = centred(key_list[4], (NODES, NODES, CAP), 1.0, 6.0, ((0, 128),), jnp.float32)
    coupling = centred(key_list[5], (NODES, WIRE, WIRE), (WIRE * CX * CY * CY // 100) ** -0.5, 0.0048828125, ((0, 128),))
    return dict(field=field, conduct=conduct, seg_cell=seg_cell, seg_count=seg_count, currents=currents, coupling=coupling)


def thomas(diagonal, rhs, coupled):
    def forward(state_pair, step_item):
        c_prev, d_prev = state_pair
        diag_now, rhs_now = step_item
        divisor = diag_now + coupled * c_prev
        c_new = -coupled / divisor
        d_new = (rhs_now + coupled * d_prev) / divisor[None]
        return (c_new, d_new), (c_new, d_new)

    start = (jnp.zeros_like(diagonal[0]), jnp.zeros_like(rhs[0]))
    _, (c_all, d_all) = lax.scan(forward, start, (diagonal, rhs))

    def backward(value_next, step_item):
        c_now, d_now = step_item
        value_now = d_now - c_now[None] * value_next
        return value_now, value_now

    _, solved = lax.scan(backward, jnp.zeros_like(rhs[0]), (c_all, d_all), reverse=True)
    return solved


def reference(field, conduct, seg_cell, seg_count, currents, coupling):
    coef_x = 8.0 * CX * CX
    coef_y = 8.0 * CY * CY
    coef_z = 0.25
    inject = 4.0 * (coef_y ** 0.5)
    diag_x = 1.0 + 0.5 * conduct + 2.0 * coef_x
    diag_y = 1.0 + 0.5 * conduct + 2.0 * coef_y
    padded = jnp.pad(field, ((0, 0), (0, 0), (1, 1)))
    first_rhs = field + coef_z * (padded[:, :, 2:] + padded[:, :, :-2] - 2.0 * field)
    half_step = thomas(diag_x, first_rhs[:, None], coef_x)[:, 0]
    source_ids = jnp.arange(NODES, dtype=jnp.int32)[:, None, None]
    pos_x = (source_ids // N_GY) * CX + seg_cell // (CY * NZ)
    pos_y = (source_ids % N_GY) * CY + (seg_cell // NZ) % CY
    pos_z = seg_cell % NZ
    filled = jnp.arange(CAP, dtype=jnp.int32)[None, None, :] < seg_count[:, :, None]
    samples = jnp.where(filled, half_step[pos_x, pos_y, pos_z], 0.0)
    gathered = jnp.transpose(samples, (1, 0, 2)).reshape(NODES, WIRE)
    change = jnp.einsum("omn,on->om", coupling.astype(jnp.float32), gathered, precision=lax.Precision.HIGHEST)
    currents_next = 0.5 * currents.reshape(NODES, WIRE) + change
    currents_next = currents_next.reshape(NODES, NODES, CAP)
    returned = jnp.transpose(currents_next, (1, 0, 2))
    injected = jnp.where(filled, returned, 0.0) * inject
    second_rhs = half_step.at[pos_x, pos_y, pos_z].add(injected)
    swapped = jnp.swapaxes(second_rhs, 0, 1)
    solved = thomas(jnp.swapaxes(diag_y, 0, 1), swapped[:, None], coef_y)[:, 0]
    field_next = jnp.swapaxes(solved, 0, 1)
    return field_next, currents_next
```

```python
import functools

import jax
import jax.numpy as jnp
from jax import lax
from jax.experimental import pallas as pl
from jax.experimental.pallas import tpu as pltpu
from jax.sharding import PartitionSpec as P

MESH = pl.DeviceIdType.MESH
F32 = jnp.float32
BF16 = jnp.bfloat16

CX, CY, NZ, CAP = 16, 128, 512, 4
GX, GY = 16, 8
WIRE = 512
KX = 8.0 * CX * CX
KY = 8.0 * CY * CY
INJECT = 4.0 * KY**0.5
PLANE = CY * CX


def inverse(value):
    return 1.0 / value


def split3(value):
    high = value.astype(BF16).astype(F32)
    rest = value - high
    middle = rest.astype(BF16).astype(F32)
    return high, middle, rest - middle


def kernel(
    field,
    conduct,
    cell_s,
    cell_v,
    count_v,
    cur_v,
    coupling,
    out,
    cur_out,
    fb,
    cb,
    mx,
    ax,
    xs,
    xr,
    xw,
    vs,
    vr,
    ht,
    my,
    ay,
    cw,
    hot,
    bh,
    bl,
    samp,
    zcol,
    p1s,
    p1r,
    p2s,
    p2r,
    ys,
    ga,
    gat,
    gb,
    ycs,
    ycr,
    yrs,
    yrr,
    yvs,
    yvr,
    fsem,
    csem,
    wsem,
    xsem,
    vsem,
    s1,
    s2,
    sa,
    sb,
    syc,
    syr,
    syv,
    osem,
):
    me_x = lax.axis_index("gx")
    me_y = lax.axis_index("gy")

    def peer_x(step):
        return lax.rem(me_x + step, GX)

    def peer_y(step):
        return lax.rem(me_y + step, GY)

    def chunk(d):
        return pl.ds(pl.multiple_of(d * 8, 8), 8)

    def quarter(q):
        return slice(128 * q, 128 * q + 128)

    def in_copies(d):
        copies = []
        for q in range(4):
            for src, dst, sem in ((conduct, cb, csem), (field, fb, fsem)):
                copies.append(
                    pltpu.make_async_copy(
                        src.at[:, chunk(d), quarter(q)], dst.at[q, :, chunk(d), :], sem.at[d, q]
                    )
                )
        return copies

    def load4(ref, x, rows):
        return jnp.concatenate([ref[q, x, rows, :] for q in range(4)], axis=1)

    def order(t):
        u = 15 - t
        return lax.rem(me_x // 4 + u // 4, 4) * 4 + lax.rem(me_x + lax.rem(u, 4), 4)

    def start_in(t, carry):
        for copy in in_copies(order(t)):
            copy.start()
        return carry

    lax.fori_loop(0, GX, start_in, 0)
    weights = pltpu.make_async_copy(coupling, cw, wsem)
    weights.start()

    barrier = pltpu.get_barrier_semaphore()

    def greet_x(t, carry):
        pl.semaphore_signal(barrier, inc=1, device_id=(peer_x(t), me_y), device_id_type=MESH)
        return carry

    def greet_y(t, carry):
        pl.semaphore_signal(barrier, inc=1, device_id=(me_x, peer_y(t)), device_id_type=MESH)
        return carry

    lax.fori_loop(1, GX, greet_x, 0)
    lax.fori_loop(1, GY, greet_y, 0)
    pl.semaphore_wait(barrier, GX - 1 + GY - 1)

    def copy_x(src, dst, sems, slot, to, who):
        return pltpu.make_async_remote_copy(
            src_ref=src, dst_ref=dst, send_sem=sems.at[0, slot], recv_sem=sems.at[1, who],
            device_id=(to, me_y), device_id_type=MESH,
        )

    def copy_y(src, dst, sems, slot, to, who):
        return pltpu.make_async_remote_copy(
            src_ref=src, dst_ref=dst, send_sem=sems.at[0, slot], recv_sem=sems.at[1, who],
            device_id=(me_x, to), device_id_type=MESH,
        )

    def each(count, body, start=1):
        def run(t, carry):
            body(t)
            return carry

        lax.fori_loop(start, count, run, 0)

    lane_z = lax.broadcasted_iota(jnp.int32, (8, NZ), 1)
    scale_f = 1.0 / (KX * KY)

    def eliminate(t, carry):
        d = order(t)
        for copy in in_copies(d):
            copy.wait()
        rows = chunk(d)

        def ground(x):
            return (1.0 / KX) + (0.5 / KX) * load4(cb, x, rows)

        def source(x):
            value = load4(fb, x, rows)
            up = jnp.where(lane_z == NZ - 1, 0.0, pltpu.roll(value, NZ - 1, 1))
            down = jnp.where(lane_z == 0, 0.0, pltpu.roll(value, 1, 1))
            return (0.5 * scale_f) * value + (0.25 * scale_f) * (up + down)

        a = jnp.ones((8, NZ), F32)
        g = ground(0)
        f = source(0)
        gp = jnp.zeros((8, NZ), F32)
        fp = jnp.zeros((8, NZ), F32)
        for x in range(CX - 1):
            m = inverse(a + g + 1.0)
            am = a * m
            b = f * m
            mx[x, rows, :] = m
            ax[x, rows, :] = am
            gp = gp + am * g
            fp = fp + am * f
            f = source(x + 1) + b
            for q in range(4):
                fb[q, x, rows, :] = b[:, quarter(q)]
            g = ground(x + 1) + g * m
            a = am
        for slot, value in enumerate((a, g, f, gp, fp)):
            xs[d, slot] = value

        @pl.when(t < GX - 1)
        def _():
            copy_x(xs.at[d], xr.at[me_x], xsem, d, d, me_x).start()

        return carry

    lax.fori_loop(0, GX, eliminate, 0)
    xr[me_x] = xs[me_x]

    cb2 = cb.reshape(4 * PLANE, 128)

    def ground_y(y):
        return [(1.0 / KY) + (0.5 / KY) * cb2[pl.ds(q * PLANE + y, CX, stride=CY), :] for q in range(4)]

    def at_y(y, q):
        return pl.ds(pl.multiple_of(q * PLANE + y * CX, CX), CX)

    def factor(y, state):
        a, g, gp = state
        after = ground_y(y + 1)
        a_new, g_new, gp_new = [], [], []
        for q in range(4):
            m = inverse(a[q] + g[q] + 1.0)
            am = a[q] * m
            my[at_y(y, q), :] = m
            ay[at_y(y, q), :] = am
            gp_new.append(gp[q] + am * g[q])
            g_new.append(after[q] + g[q] * m)
            a_new.append(am)
        return a_new, g_new, gp_new

    ones = [jnp.ones((CX, 128), F32) for _ in range(4)]
    zeros = [jnp.zeros((CX, 128), F32) for _ in range(4)]
    a_y, g_y, gp_y = lax.fori_loop(0, CY - 1, factor, (ones, ground_y(0), zeros))
    for q in range(4):
        for h in range(2):
            for slot, value in enumerate((a_y, g_y, gp_y)):
                ycs[2 * q + h, slot] = value[q][8 * h : 8 * h + 8]

    def send_yc(t):
        to = peer_y(t)
        copy_y(ycs.at[to], ycr.at[me_y], syc, to, to, me_y).start()

    each(GY, send_yc)
    ycr[me_y] = ycs[me_y]

    cells = cell_v[...]
    slot_of = lax.broadcasted_iota(jnp.int32, (CAP, 128), 0)
    filled = slot_of < count_v[...]
    place_z = jnp.where(filled, cells & (NZ - 1), -1)
    place_r = ((cells >> 9) & (CY - 1)) * CX + (cells >> 16)
    zcol[...] = jnp.concatenate([place_z, jnp.full((128 - CAP, 128), -1, jnp.int32)], axis=0).T

    def build_hot(n, carry):
        base = n * 128
        rows = lax.broadcasted_iota(jnp.int32, (128, 128), 0) + base
        for k in range(CAP):
            match = jnp.where(rows == place_r[k : k + 1, :], 1.0, 0.0)
            hot[pl.ds(pl.multiple_of(base, 128), 128), 128 * k : 128 * k + 128] = match.astype(BF16)
        return carry

    lax.fori_loop(0, PLANE // 128, build_hot, 0)

    row_m = lax.broadcasted_iota(jnp.int32, (128, WIRE), 0)
    lane_m = lax.broadcasted_iota(jnp.int32, (128, WIRE), 1)
    spread = [jnp.where(lane_m == row_m * CAP + k, 1.0, 0.0).astype(BF16) for k in range(CAP)]

    def three_rows(row):
        high, middle, low = split3(row)
        index = lax.broadcasted_iota(jnp.int32, (16, row.shape[1]), 0)
        stack = jnp.where(index == 0, high, jnp.where(index == 1, middle, jnp.where(index == 2, low, 0.0)))
        return stack.astype(BF16)

    def exact_dot(row, matrix, dims):
        product = lax.dot_general(three_rows(row), matrix, (dims, ((), ())), preferred_element_type=F32)
        return (product[2:3] + product[1:2]) + product[0:1]

    cur_row = jnp.zeros((1, WIRE), F32)
    for k in range(CAP):
        cur_row = cur_row + exact_dot(cur_v[k : k + 1, :], spread[k], ((1,), (0,)))
    p2s[...] = jnp.zeros_like(p2s)
    ys[...] = jnp.zeros_like(ys)

    def arrive_x(t):
        frm = peer_x(t)
        copy_x(xs.at[frm], xr.at[frm], xsem, frm, frm, frm).wait_recv()

    each(GX, arrive_x)

    def forward_x(r, state):
        q, phi = state
        more_g = jnp.where(r < GX - 1, xr[jnp.minimum(r + 1, GX - 1), 3], 1.0)
        more_f = jnp.where(r < GX - 1, xr[jnp.minimum(r + 1, GX - 1), 4], 0.0)
        a = xr[r, 0]
        m = inverse(a + q)
        am = jnp.where(r == 0, 0.0, a * m)
        q_new = xr[r, 1] + more_g + jnp.where(r == 0, a, am * q)
        phi_new = xr[r, 2] + more_f + am * phi
        xw[r, 0] = am
        xw[r, 1] = m * phi
        return q_new, phi_new

    blank = jnp.zeros((8, NZ), F32)
    q_x, phi_x = lax.fori_loop(0, GX, forward_x, (blank, blank))

    def backward_x(n, value):
        r = GX - 1 - n
        vs[r, 1] = value
        west = xw[r, 1] + xw[r, 0] * value
        west = jnp.where(r == 0, 0.0, west)
        vs[r, 0] = west
        return west

    lax.fori_loop(0, GX, backward_x, phi_x * inverse(q_x))

    def send_v(t):
        to = peer_x(t)
        copy_x(vs.at[to], vr.at[me_x], vsem, to, to, me_x).start()

    each(GX, send_v)
    vr[me_x] = vs[me_x]

    def substitute(t, carry):
        d = peer_x(t)

        @pl.when(t > 0)
        def _():
            copy_x(vs.at[d], vr.at[d], vsem, d, d, d).wait_recv()

        rows = chunk(d)
        west = vr[d, 0]
        value = vr[d, 1]
        for x in range(CX - 1, -1, -1):
            if x < CX - 1:
                value = load4(fb, x, rows) + ax[x, rows, :] * west + mx[x, rows, :] * value
            for q in range(4):
                ht[pl.ds(q * PLANE + d * (8 * CX) + x, 8, stride=CX), :] = value[:, 128 * q : 128 * q + 128]
        return carry

    lax.fori_loop(0, GX, substitute, 0)

    def take(o, carry):
        for k in range(CAP):
            c = cell_s[k, o]
            row = ((c >> 7) & 3) * PLANE + ((c >> 9) & (CY - 1)) * CX + (c >> 16)
            samp[pl.ds(k * 128 + o, 1), :] = ht[pl.ds(row, 1), :]
        return carry

    lax.fori_loop(0, 128, take, 0)

    lanes = lax.broadcasted_iota(jnp.int32, (128, 128), 1)
    mine = lax.rem(me_x, 4) * 32 + me_y * CAP
    placed = jnp.zeros((128, 128), F32)
    for k in range(CAP):
        z = zcol[:, k : k + 1]
        hit = ((z & 127) == lanes) & (z >= 0)
        value = jnp.sum(jnp.where(hit, samp[128 * k : 128 * k + 128, :], 0.0), axis=1, keepdims=True) * KY
        placed = jnp.where(lanes == mine + k, value, placed)
    p1s[...] = placed.reshape(GX, GY, 128)

    def send_1(t):
        to = peer_x(t)
        copy_x(p1s.at[to], p1r.at[me_x], s1, to, to, me_x).start()

    def arrive_1(t):
        frm = peer_x(t)
        copy_x(p1s.at[frm], p1r.at[frm], s1, frm, frm, frm).wait_recv()

    each(GX, send_1)
    p1r[me_x] = p1s[me_x]
    each(GX, arrive_1)
    for a in range(4):
        total = (p1r[4 * a] + p1r[4 * a + 1]) + (p1r[4 * a + 2] + p1r[4 * a + 3])
        for j in range(GY):
            p2s[j, a : a + 1, :] = total[j : j + 1, :]

    def send_2(t):
        to = peer_y(t)
        copy_y(p2s.at[to], p2r.at[me_y], s2, to, to, me_y).start()

    def arrive_2(t):
        frm = peer_y(t)
        copy_y(p2s.at[frm], p2r.at[frm], s2, frm, frm, frm).wait_recv()

    each(GY, send_2)
    p2r[me_y] = p2s[me_y]
    each(GY, arrive_2)
    gathered = p2r[0]
    for j in range(1, GY):
        gathered = gathered + p2r[j]
    row = jnp.concatenate([gathered[a : a + 1, :] for a in range(4)], axis=1)
    weights.wait()
    new_row = 0.5 * cur_row + exact_dot(row, cw[...], ((1,), (1,)))
    for a in range(4):
        ys[a : a + 1, :] = new_row[:, 128 * a : 128 * a + 128]

    def send_a(t):
        to = peer_y(t)
        copy_y(ys, ga.at[me_y], sa, to, to, me_y).start()

    def arrive_a(t):
        frm = peer_y(t)
        copy_y(ys, ga.at[frm], sa, frm, frm, frm).wait_recv()

    each(GY, send_a)
    ga[me_y] = ys[...]
    for k in range(CAP):
        cur_out[k : k + 1, :] = exact_dot(new_row, spread[k], ((1,), (1,)))
    each(GY, arrive_a)
    for j in range(GY):
        part = ga[j]
        for a in range(4):
            gat[a, j : j + 1, :] = part[a : a + 1, :]

    def send_b(t):
        to = peer_x(t)
        copy_x(gat.at[to // 4], gb.at[me_x], sb, to, to, me_x).start()

    def arrive_b(t):
        frm = peer_x(t)
        copy_x(gat.at[0], gb.at[frm], sb, frm, frm, frm).wait_recv()

    each(GX, send_b)
    gb[me_x] = gat[me_x // 4]
    each(GX, arrive_b)

    back = gb[...].reshape(128, 128)
    lane_k = lax.broadcasted_iota(jnp.int32, (128, NZ), 1)
    for k in range(CAP):
        value = jnp.sum(jnp.where(lanes == mine + k, back, 0.0), axis=1, keepdims=True) * (INJECT / KY)
        spot = jnp.where(lane_k == zcol[:, k : k + 1], value, 0.0)
        high = spot.astype(BF16)
        bh[128 * k : 128 * k + 128, :] = high
        bl[128 * k : 128 * k + 128, :] = (spot - high.astype(F32)).astype(BF16)

    def scatter(n, carry):
        rows = pl.ds(pl.multiple_of(n * 256, 256), 256)
        part = hot[rows, :]
        added = jnp.dot(part, bh[...], preferred_element_type=F32) + jnp.dot(part, bl[...], preferred_element_type=F32)
        for q in range(4):
            where = pl.ds(pl.multiple_of(q * PLANE + n * 256, 256), 256)
            ht[where, :] = ht[where, :] + added[:, 128 * q : 128 * q + 128]
        return carry

    lax.fori_loop(0, PLANE // 256, scatter, 0)

    def forward_y(y, state):
        f, fp = state
        f_new, fp_new = [], []
        for q in range(4):
            b = f[q] * my[at_y(y, q), :]
            fp_new.append(fp[q] + ay[at_y(y, q), :] * f[q])
            f_new.append(ht[at_y(y + 1, q), :] + b)
            ht[at_y(y, q), :] = b
        return f_new, fp_new

    first = [ht[at_y(0, q), :] for q in range(4)]
    f_y, fp_y = lax.fori_loop(0, CY - 1, forward_y, (first, zeros))
    for q in range(4):
        for h in range(2):
            for slot, value in enumerate((f_y, fp_y)):
                yrs[2 * q + h, slot] = value[q][8 * h : 8 * h + 8]

    def send_yr(t):
        to = peer_y(t)
        copy_y(yrs.at[to], yrr.at[me_y], syr, to, to, me_y).start()

    def arrive_yr(t):
        frm = peer_y(t)
        copy_y(yrs.at[frm], yrr.at[frm], syr, frm, frm, frm).wait_recv()

    def arrive_yc(t):
        frm = peer_y(t)
        copy_y(ycs.at[frm], ycr.at[frm], syc, frm, frm, frm).wait_recv()

    each(GY, send_yr)
    yrr[me_y] = yrs[me_y]
    each(GY, arrive_yc)
    m_list = [None]
    q_y = ycr[0, 0] + ycr[0, 1] + ycr[1, 2]
    for r in range(1, GY):
        a = ycr[r, 0]
        m = inverse(a + q_y)
        m_list.append((a * m, m))
        more = ycr[r + 1, 2] if r < GY - 1 else 1.0
        q_y = ycr[r, 1] + more + a * m * q_y
    last = inverse(q_y)
    each(GY, arrive_yr)
    phi = yrr[0, 0] + yrr[1, 1]
    phis = [phi]
    for r in range(1, GY):
        more = yrr[r + 1, 1] if r < GY - 1 else 0.0
        phi = yrr[r, 0] + more + m_list[r][0] * phi
        phis.append(phi)
    value = phi * last
    for r in range(GY - 1, 0, -1):
        yvs[r, 1] = value
        value = m_list[r][1] * phis[r - 1] + m_list[r][0] * value
        yvs[r, 0] = value
    yvs[0, 1] = value
    yvs[0, 0] = jnp.zeros((8, 128), F32)

    def send_yv(t):
        to = peer_y(t)
        copy_y(yvs.at[to], yvr.at[me_y], syv, to, to, me_y).start()

    def arrive_yv(t):
        frm = peer_y(t)
        copy_y(yvs.at[frm], yvr.at[frm], syv, frm, frm, frm).wait_recv()

    each(GY, send_yv)
    yvr[me_y] = yvs[me_y]
    each(GY, arrive_yv)

    west_y = [jnp.concatenate([yvr[2 * q, 0], yvr[2 * q + 1, 0]], axis=0) for q in range(4)]
    east_y = [jnp.concatenate([yvr[2 * q, 1], yvr[2 * q + 1, 1]], axis=0) for q in range(4)]
    ob2 = fb.reshape(4 * PLANE, 128)

    def put(y, value):
        for q in range(4):
            ob2[pl.ds(q * PLANE + y, CX, stride=CY), :] = value[q]

    def out_copies(c):
        return [
            pltpu.make_async_copy(fb.at[q, :, chunk(c), :], out.at[:, chunk(c), quarter(q)], osem.at[c, q])
            for q in range(4)
        ]

    def finish(n, value):
        c = CY // 8 - 1 - n
        for back_step in range(8):
            y = c * 8 + 7 - back_step
            new = []
            for q in range(4):
                new.append(ht[at_y(y, q), :] + ay[at_y(y, q), :] * west_y[q] + my[at_y(y, q), :] * value[q])
            value = new
            put(y, value)
        for copy in out_copies(c):
            copy.start()
        return value

    for q in range(4):
        ht[at_y(CY - 1, q), :] = jnp.zeros((CX, 128), F32)
        ay[at_y(CY - 1, q), :] = jnp.zeros((CX, 128), F32)
        my[at_y(CY - 1, q), :] = jnp.ones((CX, 128), F32)
    lax.fori_loop(0, CY // 8, finish, east_y)

    def drain_x(t):
        to = peer_x(t)
        copy_x(xs.at[to], xr.at[me_x], xsem, to, to, me_x).wait_send()
        copy_x(vs.at[to], vr.at[me_x], vsem, to, to, me_x).wait_send()
        copy_x(p1s.at[to], p1r.at[me_x], s1, to, to, me_x).wait_send()
        copy_x(gat.at[0], gb.at[me_x], sb, to, to, me_x).wait_send()

    def drain_y(t):
        to = peer_y(t)
        copy_y(p2s.at[to], p2r.at[me_y], s2, to, to, me_y).wait_send()
        copy_y(ys, ga.at[me_y], sa, to, to, me_y).wait_send()
        copy_y(ycs.at[to], ycr.at[me_y], syc, to, to, me_y).wait_send()
        copy_y(yrs.at[to], yrr.at[me_y], syr, to, to, me_y).wait_send()
        copy_y(yvs.at[to], yvr.at[me_y], syv, to, to, me_y).wait_send()

    each(GX, drain_x)
    each(GY, drain_y)

    def drain_out(c):
        for copy in out_copies(c):
            copy.wait()

    each(CY // 8, drain_out, 0)


def local(field, conduct, seg_cell, seg_count, currents, coupling):
    hbm = pl.BlockSpec(memory_space=pltpu.HBM)
    vmem = pl.BlockSpec(memory_space=pltpu.VMEM)
    smem = pl.BlockSpec(memory_space=pltpu.SMEM)
    cells = seg_cell[0].T
    block = lambda *shape: pltpu.VMEM(shape, F32)
    sems = lambda count: pltpu.SemaphoreType.DMA((2, count))
    scratch = [
        block(4, CX, CY, 128),
        block(4, CX, CY, 128),
        block(CX - 1, CY, NZ),
        block(CX - 1, CY, NZ),
        block(GX, 5, 8, NZ),
        block(GX, 5, 8, NZ),
        block(GX, 2, 8, NZ),
        block(GX, 2, 8, NZ),
        block(GX, 2, 8, NZ),
        block(4 * PLANE, 128),
        block(4 * PLANE, 128),
        block(4 * PLANE, 128),
        pltpu.VMEM((WIRE, WIRE), BF16),
        pltpu.VMEM((PLANE, WIRE), BF16),
        pltpu.VMEM((WIRE, NZ), BF16),
        pltpu.VMEM((WIRE, NZ), BF16),
        block(WIRE, 128),
        pltpu.VMEM((128, 128), jnp.int32),
        block(GX, 8, 128),
        block(GX, 8, 128),
        block(GY, 8, 128),
        block(GY, 8, 128),
        block(8, 128),
        block(GY, 8, 128),
        block(4, 8, 128),
        block(GX, 8, 128),
        block(GY, 3, 8, 128),
        block(GY, 3, 8, 128),
        block(GY, 2, 8, 128),
        block(GY, 2, 8, 128),
        block(GY, 2, 8, 128),
        block(GY, 2, 8, 128),
        pltpu.SemaphoreType.DMA((GX, 4)),
        pltpu.SemaphoreType.DMA((GX, 4)),
        pltpu.SemaphoreType.DMA,
        sems(GX),
        sems(GX),
        sems(GX),
        sems(GY),
        sems(GY),
        sems(GX),
        sems(GY),
        sems(GY),
        sems(GY),
        pltpu.SemaphoreType.DMA((CY // 8, 4)),
    ]
    field_next, currents_next = pl.pallas_call(
        kernel,
        out_shape=(
            jax.ShapeDtypeStruct((CX, CY, NZ), F32),
            jax.ShapeDtypeStruct((CAP, 128), F32),
        ),
        in_specs=[hbm, hbm, smem, vmem, vmem, vmem, hbm],
        out_specs=(hbm, vmem),
        scratch_shapes=scratch,
        compiler_params=pltpu.CompilerParams(
            collective_id=0, has_side_effects=True, vmem_limit_bytes=56 * 1024 * 1024
        ),
    )(field, conduct, cells, cells, seg_count, currents[0].T, coupling[0])
    return field_next, currents_next.T[None]


def solution(mesh):
    placed = (
        P("gx", "gy", None),
        P("gx", "gy", None),
        P(("gx", "gy"), None, None),
        P(("gx", "gy"), None),
        P(("gx", "gy"), None, None),
        P(("gx", "gy"), None, None),
    )
    return jax.shard_map(
        local,
        mesh=mesh,
        in_specs=placed,
        out_specs=(P("gx", "gy", None), P(("gx", "gy"), None, None)),
        check_vma=False,
    )
```

```python
import functools

import jax
import jax.numpy as jnp
from jax import lax
from jax.experimental import pallas as pl
from jax.experimental.pallas import tpu as pltpu
from jax.sharding import PartitionSpec as P

MESH = pl.DeviceIdType.MESH
F32 = jnp.float32
BF16 = jnp.bfloat16

CX, CY, NZ, CAP = 16, 128, 512, 4
GX, GY = 16, 8
WIRE = 512
KX = 8.0 * CX * CX
KY = 8.0 * CY * CY
INJECT = 4.0 * KY**0.5
PLANE = CY * CX
UNITS = 8
EARLY = 8


def inverse(value):
    return pl.reciprocal(value, approx=True)


def split3(value):
    high = value.astype(BF16).astype(F32)
    rest = value - high
    middle = rest.astype(BF16).astype(F32)
    return high, middle, rest - middle


def kernel(
    field,
    conduct,
    cell_s,
    cell_v,
    count_v,
    cur_v,
    coupling,
    ob,
    cur_out,
    fb,
    cb,
    mx,
    ax,
    xs,
    xr,
    vs,
    vr,
    ht,
    my,
    ay,
    cw,
    hot,
    bh,
    bl,
    samp,
    zcol,
    rows_s,
    p1s,
    p1r,
    p2s,
    p2r,
    ys,
    ga,
    gat,
    gb,
    ycs,
    ycr,
    yrs,
    yrr,
    yvs,
    yvr,
    fsem,
    csem,
    wsem,
    xsem,
    vsem,
    s1,
    s2,
    sa,
    sb,
    syc,
    syr,
    syv,
):
    me_x = lax.axis_index("gx")
    me_y = lax.axis_index("gy")

    def peer_x(step):
        return lax.rem(me_x + step, GX)

    def peer_y(step):
        return lax.rem(me_y + step, GY)

    def each(count, body, start=1):
        def run(t, carry):
            body(t)
            return carry

        lax.fori_loop(start, count, run, 0)

    def chunk(d):
        return pl.ds(pl.multiple_of(d * 8, 8), 8)

    def quarter(q):
        return slice(128 * q, 128 * q + 128)

    def in_copies(d):
        copies = []
        for q in range(4):
            for src, dst, sem in ((conduct, cb, csem), (field, fb, fsem)):
                copies.append(
                    pltpu.make_async_copy(src.at[:, chunk(d), quarter(q)], dst.at[q, d], sem.at[d, q])
                )
        return copies

    def load4(ref, d, x):
        return jnp.concatenate([ref[q, d, x] for q in range(4)], axis=1)

    def order(t):
        u = 15 - t
        return lax.rem(me_x // 4 + u // 4, 4) * 4 + lax.rem(me_x + lax.rem(u, 4), 4)

    def start_in(t, carry):
        for copy in in_copies(order(t)):
            copy.start()
        return carry

    lax.fori_loop(0, GX, start_in, 0)
    weights = pltpu.make_async_copy(coupling, cw, wsem)
    weights.start()

    barrier = pltpu.get_barrier_semaphore()

    def greet_x(t, carry):
        pl.semaphore_signal(barrier, inc=1, device_id=(peer_x(t), me_y), device_id_type=MESH)
        return carry

    def greet_y(t, carry):
        pl.semaphore_signal(barrier, inc=1, device_id=(me_x, peer_y(t)), device_id_type=MESH)
        return carry

    lax.fori_loop(1, GX, greet_x, 0)
    lax.fori_loop(1, GY, greet_y, 0)
    def copy_x(src, dst, sems, slot, to, who):
        return pltpu.make_async_remote_copy(
            src_ref=src, dst_ref=dst, send_sem=sems.at[0, slot], recv_sem=sems.at[1, who],
            device_id=(to, me_y), device_id_type=MESH,
        )

    def copy_y(src, dst, sems, slot, to, who):
        return pltpu.make_async_remote_copy(
            src_ref=src, dst_ref=dst, send_sem=sems.at[0, slot], recv_sem=sems.at[1, who],
            device_id=(me_x, to), device_id_type=MESH,
        )

    lane_z = lax.broadcasted_iota(jnp.int32, (8, NZ), 1)
    scale_f = 1.0 / (KX * KY)

    def eliminate(d):
        for copy in in_copies(d):
            copy.wait()

        def ground(x):
            return (1.0 / KX) + (0.5 / KX) * load4(cb, d, x)

        def source(x):
            value = load4(fb, d, x)
            up = jnp.where(lane_z == NZ - 1, 0.0, pltpu.roll(value, NZ - 1, 1))
            down = jnp.where(lane_z == 0, 0.0, pltpu.roll(value, 1, 1))
            return (0.5 * scale_f) * value + (0.25 * scale_f) * (up + down)

        a = jnp.ones((8, NZ), F32)
        g = ground(0)
        f = source(0)
        gp = jnp.zeros((8, NZ), F32)
        fp = jnp.zeros((8, NZ), F32)
        for x in range(CX - 1):
            m = inverse(a + g + 1.0)
            am = a * m
            b = f * m
            gp = gp + am * g
            fp = fp + am * f
            f = source(x + 1) + b
            for q in range(4):
                mx[q, d, x] = m[:, quarter(q)]
                ax[q, d, x] = am[:, quarter(q)]
                fb[q, d, x] = b[:, quarter(q)]
            g = ground(x + 1) + g * m
            a = am
        for slot, value in enumerate((a, g, f, gp, fp)):
            for q in range(4):
                xs[q, d, slot] = value[:, quarter(q)]

    def send_x(q, d):
        copy_x(xs.at[q, d], xr.at[q, me_x], xsem.at[q], d, d, me_x).start()

    def eliminate_and_send(t):
        d = order(t)
        eliminate(d)

        @pl.when(t < GX - 1)
        def _():
            send_x(0, d)

    each(EARLY, lambda t: eliminate(order(t)), 0)
    pl.semaphore_wait(barrier, GX - 1 + GY - 1)
    each(EARLY, lambda t: send_x(0, order(t)), 0)
    each(GX, eliminate_and_send, EARLY)
    for q in range(1, 4):
        each(GX - 1, lambda t, q=q: send_x(q, order(t)), 0)
    for q in range(4):
        xr[q, me_x] = xs[q, me_x]

    cb2 = cb.reshape(4 * PLANE, 128)

    def spread_rows(y, u):
        return pl.ds((u // 2) * PLANE + (y // 8) * (8 * CX) + (u % 2) * 64 + lax.rem(y, 8), 8, stride=8)

    def ground_y(y):
        return [(1.0 / KY) + (0.5 / KY) * cb2[spread_rows(y, u), :] for u in range(UNITS)]

    def at_y(y, u):
        return pl.ds(pl.multiple_of(u * (8 * CY) + y * 8, 8), 8)

    def factor(y, state):
        a, g, gp = state
        after = ground_y(y + 1)
        a_new, g_new, gp_new = [], [], []
        for u in range(UNITS):
            m = inverse(a[u] + g[u] + 1.0)
            am = a[u] * m
            my[at_y(y, u), :] = m
            ay[at_y(y, u), :] = am
            gp_new.append(gp[u] + am * g[u])
            g_new.append(after[u] + g[u] * m)
            a_new.append(am)
        return a_new, g_new, gp_new

    ones = [jnp.ones((8, 128), F32) for _ in range(UNITS)]
    zeros = [jnp.zeros((8, 128), F32) for _ in range(UNITS)]
    a_y, g_y, gp_y = lax.fori_loop(0, CY - 1, factor, (ones, ground_y(0), zeros))
    for u in range(UNITS):
        for slot, value in enumerate((a_y, g_y, gp_y)):
            ycs[u, slot] = value[u]

    def send_yc(t):
        to = peer_y(t)
        copy_y(ycs.at[to], ycr.at[me_y], syc, to, to, me_y).start()

    each(GY, send_yc)
    ycr[me_y] = ycs[me_y]

    cells = cell_v[...]
    slot_of = lax.broadcasted_iota(jnp.int32, (CAP, 128), 0)
    filled = slot_of < count_v[...]
    place_z = jnp.where(filled, cells & (NZ - 1), -1)
    place_r = (cells >> 19) * (8 * CY) + ((cells >> 9) & (CY - 1)) * 8 + ((cells >> 16) & 7)
    zcol[...] = jnp.concatenate([place_z, jnp.full((128 - CAP, 128), -1, jnp.int32)], axis=0).T

    def find(o):
        for k in range(CAP):
            c = cell_s[k, o]
            row = ((c >> 7) & 3) * PLANE + (c >> 19) * (8 * CY) + ((c >> 9) & (CY - 1)) * 8 + ((c >> 16) & 7)
            rows_s[k * 128 + o] = row

    each(128, find, 0)

    def build_hot(n, carry):
        base = n * 128
        rows = lax.broadcasted_iota(jnp.int32, (128, 128), 0) + base
        for k in range(CAP):
            match = jnp.where(rows == place_r[k : k + 1, :], 1.0, 0.0)
            hot[pl.ds(pl.multiple_of(base, 128), 128), 128 * k : 128 * k + 128] = match.astype(BF16)
        return carry

    lax.fori_loop(0, PLANE // 128, build_hot, 0)

    row_m = lax.broadcasted_iota(jnp.int32, (128, WIRE), 0)
    lane_m = lax.broadcasted_iota(jnp.int32, (128, WIRE), 1)
    spread = [jnp.where(lane_m == row_m * CAP + k, 1.0, 0.0).astype(BF16) for k in range(CAP)]

    def three_rows(row):
        high, middle, low = split3(row)
        index = lax.broadcasted_iota(jnp.int32, (16, row.shape[1]), 0)
        stack = jnp.where(index == 0, high, jnp.where(index == 1, middle, jnp.where(index == 2, low, 0.0)))
        return stack.astype(BF16)

    def exact_dot(row, matrix, dims):
        product = lax.dot_general(three_rows(row), matrix, (dims, ((), ())), preferred_element_type=F32)
        return (product[2:3] + product[1:2]) + product[0:1]

    cur_row = jnp.zeros((1, WIRE), F32)
    for k in range(CAP):
        cur_row = cur_row + exact_dot(cur_v[k : k + 1, :], spread[k], ((1,), (0,)))
    p2s[...] = jnp.zeros_like(p2s)
    ys[...] = jnp.zeros_like(ys)

    blank = jnp.zeros((8, 128), F32)

    def reduce_x(q):
        def arrive(t):
            frm = peer_x(t)
            copy_x(xs.at[q, frm], xr.at[q, frm], xsem.at[q], frm, frm, frm).wait_recv()

        each(GX, arrive)
        q_x = xr[q, 0, 0] + xr[q, 0, 1] + xr[q, 1, 3]
        phi = xr[q, 0, 2] + xr[q, 1, 4]
        kept = [None]
        for r in range(1, GX):
            a = xr[q, r, 0]
            m = inverse(a + q_x)
            am = a * m
            kept.append((am, m * phi))
            more_g, more_f = (xr[q, r + 1, 3], xr[q, r + 1, 4]) if r < GX - 1 else (1.0, 0.0)
            q_x = xr[q, r, 1] + more_g + am * q_x
            phi = xr[q, r, 2] + more_f + am * phi
        value = phi * inverse(q_x)
        for r in range(GX - 1, 0, -1):
            vs[q, r, 1] = value
            value = kept[r][1] + kept[r][0] * value
            vs[q, r, 0] = value
        vs[q, 0, 1] = value
        vs[q, 0, 0] = blank

        def send(t):
            to = peer_x(t)
            copy_x(vs.at[q, to], vr.at[q, me_x], vsem.at[q], to, to, me_x).start()

        each(GX, send)
        vr[q, me_x] = vs[q, me_x]

    for q in range(4):
        reduce_x(q)

    def substitute(q):
        def arrive(t):
            frm = peer_x(t)
            copy_x(vs.at[q, frm], vr.at[q, frm], vsem.at[q], frm, frm, frm).wait_recv()

        def group(n):
            ds = [n * 4 + i for i in range(4)]
            west = [vr[q, d, 0] for d in ds]
            value = [vr[q, d, 1] for d in ds]
            for x in range(CX - 1, -1, -1):
                if x < CX - 1:
                    value = [
                        (fb[q, d, x] + ax[q, d, x] * west[i]) + mx[q, d, x] * value[i] for i, d in enumerate(ds)
                    ]
                for i, d in enumerate(ds):
                    ht[pl.ds((2 * q + x // 8) * (8 * CY) + d * 64 + x % 8, 8, stride=8), :] = value[i]

        each(GX, arrive)
        each(4, group, 0)

    for q in range(4):
        substitute(q)

    def take(n):
        for i in range(16):
            samp[pl.ds(n * 16 + i, 1), :] = ht[pl.ds(rows_s[n * 16 + i], 1), :]

    each(WIRE // 16, take, 0)

    lanes = lax.broadcasted_iota(jnp.int32, (128, 128), 1)
    mine = lax.rem(me_x, 4) * 32 + me_y * CAP
    placed = jnp.zeros((128, 128), F32)
    for k in range(CAP):
        z = zcol[:, k : k + 1]
        hit = ((z & 127) == lanes) & (z >= 0)
        value = jnp.sum(jnp.where(hit, samp[128 * k : 128 * k + 128, :], 0.0), axis=1, keepdims=True) * KY
        placed = jnp.where(lanes == mine + k, value, placed)
    p1s[...] = placed.reshape(GX, GY, 128)

    def send_1(t):
        to = peer_x(t)
        copy_x(p1s.at[to], p1r.at[me_x], s1, to, to, me_x).start()

    def arrive_1(t):
        frm = peer_x(t)
        copy_x(p1s.at[frm], p1r.at[frm], s1, frm, frm, frm).wait_recv()

    each(GX, send_1)
    p1r[me_x] = p1s[me_x]
    each(GX, arrive_1)
    for a in range(4):
        total = (p1r[4 * a] + p1r[4 * a + 1]) + (p1r[4 * a + 2] + p1r[4 * a + 3])
        for j in range(GY):
            p2s[j, a : a + 1, :] = total[j : j + 1, :]

    def send_2(t):
        to = peer_y(t)
        copy_y(p2s.at[to], p2r.at[me_y], s2, to, to, me_y).start()

    def arrive_2(t):
        frm = peer_y(t)
        copy_y(p2s.at[frm], p2r.at[frm], s2, frm, frm, frm).wait_recv()

    each(GY, send_2)
    p2r[me_y] = p2s[me_y]
    each(GY, arrive_2)
    gathered = p2r[0]
    for j in range(1, GY):
        gathered = gathered + p2r[j]
    row = jnp.concatenate([gathered[a : a + 1, :] for a in range(4)], axis=1)
    weights.wait()
    new_row = 0.5 * cur_row + exact_dot(row, cw[...], ((1,), (1,)))
    for a in range(4):
        ys[a : a + 1, :] = new_row[:, 128 * a : 128 * a + 128]

    def send_a(t):
        to = peer_y(t)
        copy_y(ys, ga.at[me_y], sa, to, to, me_y).start()

    def arrive_a(t):
        frm = peer_y(t)
        copy_y(ys, ga.at[frm], sa, frm, frm, frm).wait_recv()

    each(GY, send_a)
    ga[me_y] = ys[...]
    for k in range(CAP):
        cur_out[k : k + 1, :] = exact_dot(new_row, spread[k], ((1,), (1,)))
    each(GY, arrive_a)
    for j in range(GY):
        part = ga[j]
        for a in range(4):
            gat[a, j : j + 1, :] = part[a : a + 1, :]

    def send_b(t):
        to = peer_x(t)
        copy_x(gat.at[to // 4], gb.at[me_x], sb, to, to, me_x).start()

    def arrive_b(t):
        frm = peer_x(t)
        copy_x(gat.at[0], gb.at[frm], sb, frm, frm, frm).wait_recv()

    each(GX, send_b)
    gb[me_x] = gat[me_x // 4]
    each(GX, arrive_b)

    back = gb[...].reshape(128, 128)
    lane_k = lax.broadcasted_iota(jnp.int32, (128, NZ), 1)
    for k in range(CAP):
        value = jnp.sum(jnp.where(lanes == mine + k, back, 0.0), axis=1, keepdims=True) * (INJECT / KY)
        spot = jnp.where(lane_k == zcol[:, k : k + 1], value, 0.0)
        high = spot.astype(BF16)
        bh[128 * k : 128 * k + 128, :] = high
        bl[128 * k : 128 * k + 128, :] = (spot - high.astype(F32)).astype(BF16)

    def scatter(n, carry):
        rows = pl.ds(pl.multiple_of(n * 256, 256), 256)
        part = hot[rows, :]
        added = jnp.dot(part, bh[...], preferred_element_type=F32) + jnp.dot(part, bl[...], preferred_element_type=F32)
        for q in range(4):
            where = pl.ds(pl.multiple_of(q * PLANE + n * 256, 256), 256)
            ht[where, :] = ht[where, :] + added[:, 128 * q : 128 * q + 128]
        return carry

    lax.fori_loop(0, PLANE // 256, scatter, 0)

    def forward_y(y, state):
        f, fp = state
        f_new, fp_new = [], []
        for u in range(UNITS):
            b = f[u] * my[at_y(y, u), :]
            fp_new.append(fp[u] + ay[at_y(y, u), :] * f[u])
            f_new.append(ht[at_y(y + 1, u), :] + b)
            ht[at_y(y, u), :] = b
        return f_new, fp_new

    first = [ht[at_y(0, u), :] for u in range(UNITS)]
    f_y, fp_y = lax.fori_loop(0, CY - 1, forward_y, (first, zeros))
    for u in range(UNITS):
        for slot, value in enumerate((f_y, fp_y)):
            yrs[u, slot] = value[u]

    def send_yr(t):
        to = peer_y(t)
        copy_y(yrs.at[to], yrr.at[me_y], syr, to, to, me_y).start()

    def arrive_yr(t):
        frm = peer_y(t)
        copy_y(yrs.at[frm], yrr.at[frm], syr, frm, frm, frm).wait_recv()

    def arrive_yc(t):
        frm = peer_y(t)
        copy_y(ycs.at[frm], ycr.at[frm], syc, frm, frm, frm).wait_recv()

    each(GY, send_yr)
    yrr[me_y] = yrs[me_y]
    each(GY, arrive_yc)
    m_list = [None]
    q_y = ycr[0, 0] + ycr[0, 1] + ycr[1, 2]
    for r in range(1, GY):
        a = ycr[r, 0]
        m = inverse(a + q_y)
        m_list.append((a * m, m))
        more = ycr[r + 1, 2] if r < GY - 1 else 1.0
        q_y = ycr[r, 1] + more + a * m * q_y
    last = inverse(q_y)
    each(GY, arrive_yr)
    phi = yrr[0, 0] + yrr[1, 1]
    phis = [phi]
    for r in range(1, GY):
        more = yrr[r + 1, 1] if r < GY - 1 else 0.0
        phi = yrr[r, 0] + more + m_list[r][0] * phi
        phis.append(phi)
    value = phi * last
    for r in range(GY - 1, 0, -1):
        yvs[r, 1] = value
        value = m_list[r][1] * phis[r - 1] + m_list[r][0] * value
        yvs[r, 0] = value
    yvs[0, 1] = value
    yvs[0, 0] = jnp.zeros((8, 128), F32)

    def send_yv(t):
        to = peer_y(t)
        copy_y(yvs.at[to], yvr.at[me_y], syv, to, to, me_y).start()

    def arrive_yv(t):
        frm = peer_y(t)
        copy_y(yvs.at[frm], yvr.at[frm], syv, frm, frm, frm).wait_recv()

    each(GY, send_yv)
    yvr[me_y] = yvs[me_y]
    each(GY, arrive_yv)

    west_y = [yvr[u, 0] for u in range(UNITS)]
    east_y = [yvr[u, 1] for u in range(UNITS)]
    ob2 = ob.reshape(4 * PLANE, 128)

    def finish(n, value):
        c = CY // 8 - 1 - n
        for back_step in range(8):
            y = c * 8 + 7 - back_step
            value = [
                (ht[at_y(y, u), :] + ay[at_y(y, u), :] * west_y[u]) + my[at_y(y, u), :] * value[u]
                for u in range(UNITS)
            ]
            for u in range(UNITS):
                ob2[spread_rows(y, u), :] = value[u]
        return value

    for u in range(UNITS):
        ht[at_y(CY - 1, u), :] = jnp.zeros((8, 128), F32)
        ay[at_y(CY - 1, u), :] = jnp.zeros((8, 128), F32)
        my[at_y(CY - 1, u), :] = jnp.ones((8, 128), F32)
    lax.fori_loop(0, CY // 8, finish, east_y)

    def drain_x(t):
        to = peer_x(t)
        for q in range(4):
            copy_x(xs.at[q, to], xr.at[q, me_x], xsem.at[q], to, to, me_x).wait_send()
            copy_x(vs.at[q, to], vr.at[q, me_x], vsem.at[q], to, to, me_x).wait_send()
        copy_x(p1s.at[to], p1r.at[me_x], s1, to, to, me_x).wait_send()
        copy_x(gat.at[0], gb.at[me_x], sb, to, to, me_x).wait_send()

    def drain_y(t):
        to = peer_y(t)
        copy_y(p2s.at[to], p2r.at[me_y], s2, to, to, me_y).wait_send()
        copy_y(ys, ga.at[me_y], sa, to, to, me_y).wait_send()
        copy_y(ycs.at[to], ycr.at[me_y], syc, to, to, me_y).wait_send()
        copy_y(yrs.at[to], yrr.at[me_y], syr, to, to, me_y).wait_send()
        copy_y(yvs.at[to], yvr.at[me_y], syv, to, to, me_y).wait_send()

    each(GX, drain_x)
    each(GY, drain_y)


def deliver(staged, cur_in, out, cur_out, sems):
    def copy(d, q):
        return pltpu.make_async_copy(
            staged.at[q, d], out.at[:, pl.ds(pl.multiple_of(d * 8, 8), 8), 128 * q : 128 * q + 128], sems.at[q, d]
        )

    def start(d, carry):
        for q in range(4):
            copy(d, q).start()
        return carry

    def wait(d, carry):
        for q in range(4):
            copy(d, q).wait()
        return carry

    lax.fori_loop(0, GX, start, 0)
    cur_out[...] = cur_in[...]
    lax.fori_loop(0, GX, wait, 0)


def local(field, conduct, seg_cell, seg_count, currents, coupling):
    hbm = pl.BlockSpec(memory_space=pltpu.HBM)
    vmem = pl.BlockSpec(memory_space=pltpu.VMEM)
    smem = pl.BlockSpec(memory_space=pltpu.SMEM)
    cells = seg_cell[0].T
    block = lambda *shape: pltpu.VMEM(shape, F32)
    sems = lambda count: pltpu.SemaphoreType.DMA((2, count))
    scratch = [
        block(4, GX, CX, 8, 128),
        block(4, GX, CX, 8, 128),
        block(4, GX, CX, 8, 128),
        block(4, GX, CX, 8, 128),
        block(4, GX, 5, 8, 128),
        block(4, GX, 5, 8, 128),
        block(4, GX, 2, 8, 128),
        block(4, GX, 2, 8, 128),
        block(4 * PLANE, 128),
        block(4 * PLANE, 128),
        block(4 * PLANE, 128),
        pltpu.VMEM((WIRE, WIRE), BF16),
        pltpu.VMEM((PLANE, WIRE), BF16),
        pltpu.VMEM((WIRE, NZ), BF16),
        pltpu.VMEM((WIRE, NZ), BF16),
        block(WIRE, 128),
        pltpu.VMEM((128, 128), jnp.int32),
        pltpu.SMEM((WIRE,), jnp.int32),
        block(GX, 8, 128),
        block(GX, 8, 128),
        block(GY, 8, 128),
        block(GY, 8, 128),
        block(8, 128),
        block(GY, 8, 128),
        block(4, 8, 128),
        block(GX, 8, 128),
        block(GY, 3, 8, 128),
        block(GY, 3, 8, 128),
        block(GY, 2, 8, 128),
        block(GY, 2, 8, 128),
        block(GY, 2, 8, 128),
        block(GY, 2, 8, 128),
        pltpu.SemaphoreType.DMA((GX, 4)),
        pltpu.SemaphoreType.DMA((GX, 4)),
        pltpu.SemaphoreType.DMA,
        pltpu.SemaphoreType.DMA((4, 2, GX)),
        pltpu.SemaphoreType.DMA((4, 2, GX)),
        sems(GX),
        sems(GY),
        sems(GY),
        sems(GX),
        sems(GY),
        sems(GY),
        sems(GY),
    ]
    staged, currents_next = pl.pallas_call(
        kernel,
        out_shape=(
            pltpu.VMEM((4, GX, CX, 8, 128), F32),
            pltpu.VMEM((CAP, 128), F32),
        ),
        in_specs=[hbm, hbm, smem, vmem, vmem, vmem, hbm],
        out_specs=(vmem, vmem),
        scratch_shapes=scratch,
        compiler_params=pltpu.CompilerParams(
            collective_id=0, has_side_effects=True, vmem_limit_bytes=57 * 1024 * 1024
        ),
    )(field, conduct, cells, cells, seg_count, currents[0].T, coupling[0])
    field_next, currents_next = pl.pallas_call(
        deliver,
        out_shape=(
            jax.ShapeDtypeStruct((CX, CY, NZ), F32),
            jax.ShapeDtypeStruct((CAP, 128), F32),
        ),
        in_specs=[pl.BlockSpec(memory_space=pl.ANY), vmem],
        out_specs=(hbm, vmem),
        scratch_shapes=[pltpu.SemaphoreType.DMA((4, GX))],
        compiler_params=pltpu.CompilerParams(vmem_limit_bytes=4 * 1024 * 1024),
    )(staged, currents_next)
    return field_next, currents_next.T[None]


def solution(mesh):
    placed = (
        P("gx", "gy", None),
        P("gx", "gy", None),
        P(("gx", "gy"), None, None),
        P(("gx", "gy"), None),
        P(("gx", "gy"), None, None),
        P(("gx", "gy"), None, None),
    )
    return jax.shard_map(
        local,
        mesh=mesh,
        in_specs=placed,
        out_specs=(P("gx", "gy", None), P(("gx", "gy"), None, None)),
        check_vma=False,
    )
```

```python
import functools

import jax
import jax.numpy as jnp
from jax import lax
from jax.experimental import pallas as pl
from jax.experimental.pallas import tpu as pltpu
from jax.sharding import PartitionSpec as P

MESH = pl.DeviceIdType.MESH
F32 = jnp.float32
BF16 = jnp.bfloat16

CX, CY, NZ, CAP = 16, 128, 512, 4
GX, GY = 16, 8
WIRE = 512
KX = 8.0 * CX * CX
KY = 8.0 * CY * CY
INJECT = 4.0 * KY**0.5
PLANE = CY * CX
UNITS = 8
EARLY = 2


def inverse(value):
    return pl.reciprocal(value, approx=True)


def split3(value):
    high = value.astype(BF16).astype(F32)
    rest = value - high
    middle = rest.astype(BF16).astype(F32)
    return high, middle, rest - middle


def kernel(
    field,
    conduct,
    cell_h,
    count_h,
    cur_h,
    coupling,
    ob,
    cur_out,
    fb,
    cb,
    mx,
    ax,
    xs,
    xr,
    vs,
    vr,
    ht,
    my,
    ay,
    cw,
    hot,
    bhl,
    samp,
    zcol,
    cell_v,
    count_v,
    cur_v,
    rows_v,
    rows_s,
    wv,
    wp,
    samp2,
    pks,
    pkr,
    zhot,
    xmask,
    gbt,
    yk,
    added0,
    added1,
    p1s,
    p1r,
    p2s,
    p2r,
    ys,
    ga,
    gat,
    gb,
    ycs,
    ycr,
    yrs,
    yrr,
    yvs,
    yvr,
    fsem,
    csem,
    wsem,
    xsem,
    vsem,
    s1,
    s2,
    sa,
    sb,
    syc,
    syr,
    syv,
    spk,
    small,
    rsem,
):
    me_x = lax.axis_index("gx")
    me_y = lax.axis_index("gy")

    def peer_x(step):
        return lax.rem(me_x + step, GX)

    def peer_y(step):
        return lax.rem(me_y + step, GY)

    def each(count, body, start=1):
        def run(t, carry):
            body(t)
            return carry

        lax.fori_loop(start, count, run, 0)

    def chunk(d):
        return pl.ds(pl.multiple_of(d * 8, 8), 8)

    def quarter(q):
        return slice(128 * q, 128 * q + 128)

    def in_copies(d):
        copies = []
        for q in range(4):
            for src, dst, sem in ((conduct, cb, csem), (field, fb, fsem)):
                copies.append(
                    pltpu.make_async_copy(src.at[:, chunk(d), quarter(q)], dst.at[q, d], sem.at[d, q])
                )
        return copies

    def load4(ref, d, x):
        return jnp.concatenate([ref[q, d, x] for q in range(4)], axis=1)

    def order(t):
        u = 15 - t
        return lax.rem(me_x // 4 + u // 4, 4) * 4 + lax.rem(me_x + lax.rem(u, 4), 4)

    def start_in(t, carry):
        for copy in in_copies(order(t)):
            copy.start()
        return carry

    barrier = pltpu.get_barrier_semaphore()

    def greet_x(t, carry):
        pl.semaphore_signal(barrier, inc=1, device_id=(peer_x(t), me_y), device_id_type=MESH)
        return carry

    def greet_y(t, carry):
        pl.semaphore_signal(barrier, inc=1, device_id=(me_x, peer_y(t)), device_id_type=MESH)
        return carry

    lax.fori_loop(1, GX, greet_x, 0)
    lax.fori_loop(1, GY, greet_y, 0)
    lax.fori_loop(0, GX, start_in, 0)
    weights = pltpu.make_async_copy(coupling, cw, wsem)
    weights.start()
    smalls = [
        pltpu.make_async_copy(src, dst, small.at[i])
        for i, (src, dst) in enumerate(((cell_h, cell_v), (count_h, count_v), (cur_h, cur_v)))
    ]
    for copy in smalls:
        copy.start()

    def copy_x(src, dst, sems, slot, to, who):
        return pltpu.make_async_remote_copy(
            src_ref=src, dst_ref=dst, send_sem=sems.at[0, slot], recv_sem=sems.at[1, who],
            device_id=(to, me_y), device_id_type=MESH,
        )

    def copy_y(src, dst, sems, slot, to, who):
        return pltpu.make_async_remote_copy(
            src_ref=src, dst_ref=dst, send_sem=sems.at[0, slot], recv_sem=sems.at[1, who],
            device_id=(me_x, to), device_id_type=MESH,
        )

    lane_z = lax.broadcasted_iota(jnp.int32, (8, NZ), 1)
    scale_f = 1.0 / (KX * KY)

    def eliminate(d):
        for copy in in_copies(d):
            copy.wait()

        def ground(x):
            return (1.0 / KX) + (0.5 / KX) * load4(cb, d, x)

        def source(x):
            value = load4(fb, d, x)
            up = jnp.where(lane_z == NZ - 1, 0.0, pltpu.roll(value, NZ - 1, 1))
            down = jnp.where(lane_z == 0, 0.0, pltpu.roll(value, 1, 1))
            return (0.5 * scale_f) * value + (0.25 * scale_f) * (up + down)

        a = jnp.ones((8, NZ), F32)
        g = ground(0)
        f = source(0)
        gp = jnp.zeros((8, NZ), F32)
        fp = jnp.zeros((8, NZ), F32)
        for x in range(CX - 1):
            m = inverse(a + g + 1.0)
            am = a * m
            b = f * m
            gp = gp + am * g
            fp = fp + am * f
            f = source(x + 1) + b
            for q in range(4):
                mx[q, d, x] = m[:, quarter(q)]
                ax[q, d, x] = am[:, quarter(q)]
                fb[q, d, x] = b[:, quarter(q)]
            g = ground(x + 1) + g * m
            a = am
        for slot, value in enumerate((a, g, f, gp, fp)):
            for q in range(4):
                xs[q, d, slot] = value[:, quarter(q)]

    def send_x(q, d):
        copy_x(xs.at[q, d], xr.at[q, me_x], xsem.at[q], d, d, me_x).start()

    def eliminate_and_send(t):
        d = order(t)
        eliminate(d)

        @pl.when(t < GX - 1)
        def _():
            send_x(0, d)

    each(EARLY, lambda t: eliminate(order(t)), 0)
    pl.semaphore_wait(barrier, GX - 1 + GY - 1)
    each(EARLY, lambda t: send_x(0, order(t)), 0)
    each(GX, eliminate_and_send, EARLY)
    for q in range(1, 4):
        each(GX - 1, lambda t, q=q: send_x(q, order(t)), 0)
    for q in range(4):
        xr[q, me_x] = xs[q, me_x]

    cb2 = cb.reshape(4 * PLANE, 128)

    def spread_rows(y, u):
        return pl.ds((u // 2) * PLANE + (y // 8) * (8 * CX) + (u % 2) * 64 + lax.rem(y, 8), 8, stride=8)

    def ground_y(y):
        return [(1.0 / KY) + (0.5 / KY) * cb2[spread_rows(y, u), :] for u in range(UNITS)]

    def at_y(y, u):
        return pl.ds(pl.multiple_of(u * (8 * CY) + y * 8, 8), 8)

    def factor(y, state):
        a, g, gp = state
        after = ground_y(y + 1)
        a_new, g_new, gp_new = [], [], []
        for u in range(UNITS):
            m = inverse(a[u] + g[u] + 1.0)
            am = a[u] * m
            my[at_y(y, u), :] = m
            ay[at_y(y, u), :] = am
            gp_new.append(gp[u] + am * g[u])
            g_new.append(after[u] + g[u] * m)
            a_new.append(am)
        return a_new, g_new, gp_new

    ones = [jnp.ones((8, 128), F32) for _ in range(UNITS)]
    zeros = [jnp.zeros((8, 128), F32) for _ in range(UNITS)]
    a_y, g_y, gp_y = lax.fori_loop(0, CY - 1, factor, (ones, ground_y(0), zeros))
    for u in range(UNITS):
        for slot, value in enumerate((a_y, g_y, gp_y)):
            ycs[u, slot] = value[u]

    for u in range(UNITS):
        my[at_y(CY - 1, u), :] = jnp.ones((8, 128), F32)
        ay[at_y(CY - 1, u), :] = jnp.zeros((8, 128), F32)
        wv[at_y(CY - 1, u), :] = jnp.ones((8, 128), F32)
        wp[at_y(CY - 1, u), :] = jnp.zeros((8, 128), F32)

    def send_yc(t):
        to = peer_y(t)
        copy_y(ycs.at[to], ycr.at[me_y], syc, to, to, me_y).start()

    each(GY, send_yc)
    ycr[me_y] = ycs[me_y]

    def weigh(n, state):
        y = CY - 2 - n
        to_last, to_west = state
        last_new, west_new = [], []
        for u in range(UNITS):
            m = my[at_y(y, u), :]
            last_new.append(m * to_last[u])
            west_new.append(ay[at_y(y, u), :] + m * to_west[u])
            wv[at_y(y, u), :] = last_new[u]
            wp[at_y(y, u), :] = west_new[u]
        return last_new, west_new

    lax.fori_loop(0, CY - 1, weigh, (ones, zeros))

    for copy in smalls:
        copy.wait()
    cells = cell_v[...]
    slot_of = lax.broadcasted_iota(jnp.int32, (CAP, 128), 0)
    filled = slot_of < count_v[...]
    at_x = cells >> 16
    place_z = jnp.where(filled, cells & (NZ - 1), -1)
    place_r = ((cells >> 9) & (CY - 1)) * CX + at_x
    rows_v[...] = ((cells >> 7) & 3) * PLANE + (at_x >> 3) * (8 * CY) + ((cells >> 9) & (CY - 1)) * 8 + (at_x & 7)
    rows_copy = pltpu.make_async_copy(rows_v, rows_s, rsem)
    rows_copy.start()
    zcol[...] = jnp.concatenate([place_z, jnp.full((128 - CAP, 128), -1, jnp.int32)], axis=0).T
    lanes = lax.broadcasted_iota(jnp.int32, (128, 128), 1)

    def hit_of(k):
        z = zcol[:, k : k + 1]
        return ((z & 127) == lanes) & (z >= 0)

    def pick(pairs):
        def run(n):
            for i in range(16):
                o = n * 16 + i
                for k in range(CAP):
                    row = rows_s[k, o]
                    for src, dst in pairs:
                        dst[pl.ds(k * 128 + o, 1), :] = src[pl.ds(row, 1), :]

        each(128 // 16, run, 0)

    rows_copy.wait()
    pick(((wv, samp), (wp, samp2)))
    for k in range(CAP):
        hit = hit_of(k)
        rows = slice(128 * k, 128 * k + 128)
        for slot, ref in enumerate((samp, samp2)):
            chosen = jnp.where(hit, ref[rows, :], 0.0) * (INJECT / KY)
            pks[slot * CAP + k : slot * CAP + k + 1, :] = jnp.sum(chosen.T, axis=0, keepdims=True)
    pks[2 * CAP : 3 * CAP, :] = at_x.astype(F32)
    pks[3 * CAP : 4 * CAP, :] = place_z.astype(F32)

    def send_pk(t):
        to = peer_y(t)
        copy_y(pks, pkr.at[me_y], spk, to, to, me_y).start()

    each(GY, send_pk)
    pkr[me_y] = pks[...]

    def build_hot(n, carry):
        base = n * 128
        rows = lax.broadcasted_iota(jnp.int32, (128, 128), 0) + base
        for k in range(CAP):
            match = jnp.where(rows == place_r[k : k + 1, :], 1.0, 0.0)
            hot[pl.ds(pl.multiple_of(base, 128), 128), 128 * k : 128 * k + 128] = match.astype(BF16)
        return carry

    lax.fori_loop(0, PLANE // 128, build_hot, 0)

    row_m = lax.broadcasted_iota(jnp.int32, (128, WIRE), 0)
    lane_m = lax.broadcasted_iota(jnp.int32, (128, WIRE), 1)
    spread = [jnp.where(lane_m == row_m * CAP + k, 1.0, 0.0).astype(BF16) for k in range(CAP)]

    def three_rows(row):
        high, middle, low = split3(row)
        index = lax.broadcasted_iota(jnp.int32, (16, row.shape[1]), 0)
        stack = jnp.where(index == 0, high, jnp.where(index == 1, middle, jnp.where(index == 2, low, 0.0)))
        return stack.astype(BF16)

    def exact_dot(row, matrix, dims):
        product = lax.dot_general(three_rows(row), matrix, (dims, ((), ())), preferred_element_type=F32)
        return (product[2:3] + product[1:2]) + product[0:1]

    cur_row = jnp.zeros((1, WIRE), F32)
    for k in range(CAP):
        cur_row = cur_row + exact_dot(cur_v[k : k + 1, :], spread[k], ((1,), (0,)))
    p2s[...] = jnp.zeros_like(p2s)
    ys[...] = jnp.zeros_like(ys)

    blank = jnp.zeros((8, 128), F32)

    def reduce_x(q):
        def arrive(t):
            frm = peer_x(t)
            copy_x(xs.at[q, frm], xr.at[q, frm], xsem.at[q], frm, frm, frm).wait_recv()

        each(GX, arrive)
        q_x = xr[q, 0, 0] + xr[q, 0, 1] + xr[q, 1, 3]
        phi = xr[q, 0, 2] + xr[q, 1, 4]
        kept = [None]
        for r in range(1, GX):
            a = xr[q, r, 0]
            m = inverse(a + q_x)
            am = a * m
            kept.append((am, m * phi))
            more_g, more_f = (xr[q, r + 1, 3], xr[q, r + 1, 4]) if r < GX - 1 else (1.0, 0.0)
            q_x = xr[q, r, 1] + more_g + am * q_x
            phi = xr[q, r, 2] + more_f + am * phi
        value = phi * inverse(q_x)
        for r in range(GX - 1, 0, -1):
            vs[q, r, 1] = value
            value = kept[r][1] + kept[r][0] * value
            vs[q, r, 0] = value
        vs[q, 0, 1] = value
        vs[q, 0, 0] = blank

        def send(t):
            to = peer_x(t)
            copy_x(vs.at[q, to], vr.at[q, me_x], vsem.at[q], to, to, me_x).start()

        each(GX, send)
        vr[q, me_x] = vs[q, me_x]

    for q in range(4):
        reduce_x(q)

    def substitute(q):
        def arrive(t):
            frm = peer_x(t)
            copy_x(vs.at[q, frm], vr.at[q, frm], vsem.at[q], frm, frm, frm).wait_recv()

        def group(n):
            ds = [n * 4 + i for i in range(4)]
            west = [vr[q, d, 0] for d in ds]
            value = [vr[q, d, 1] for d in ds]
            for x in range(CX - 1, -1, -1):
                if x < CX - 1:
                    value = [
                        (fb[q, d, x] + ax[q, d, x] * west[i]) + mx[q, d, x] * value[i] for i, d in enumerate(ds)
                    ]
                for i, d in enumerate(ds):
                    ht[pl.ds((2 * q + x // 8) * (8 * CY) + d * 64 + x % 8, 8, stride=8), :] = value[i]

        each(GX, arrive)
        each(4, group, 0)

    for q in range(4):
        substitute(q)

    pick(((ht, samp),))

    mine = lax.rem(me_x, 4) * 32 + me_y * CAP
    placed = jnp.zeros((128, 128), F32)
    for k in range(CAP):
        value = jnp.sum(jnp.where(hit_of(k), samp[128 * k : 128 * k + 128, :], 0.0), axis=1, keepdims=True) * KY
        placed = jnp.where(lanes == mine + k, value, placed)
    p1s[...] = placed.reshape(GX, GY, 128)

    def send_1(t):
        to = peer_x(t)
        copy_x(p1s.at[to], p1r.at[me_x], s1, to, to, me_x).start()

    def arrive_1(t):
        frm = peer_x(t)
        copy_x(p1s.at[frm], p1r.at[frm], s1, frm, frm, frm).wait_recv()

    each(GX, send_1)
    p1r[me_x] = p1s[me_x]
    def sum_up(y, state):
        f, fp = state
        f_new, fp_new = [], []
        for u in range(UNITS):
            fp_new.append(fp[u] + ay[at_y(y, u), :] * f[u])
            f_new.append(ht[at_y(y + 1, u), :] + f[u] * my[at_y(y, u), :])
        return f_new, fp_new

    first = [ht[at_y(0, u), :] for u in range(UNITS)]
    f_y, fp_y = lax.fori_loop(0, CY - 1, sum_up, (first, zeros))
    for u in range(UNITS):
        for slot, value in enumerate((f_y, fp_y)):
            yrs[u, slot] = value[u]

    def send_yr(t):
        to = peer_y(t)
        copy_y(yrs.at[to], yrr.at[me_y], syr, to, to, me_y).start()

    each(GY, send_yr)
    yrr[me_y] = yrs[me_y]
    each(GX, arrive_1)
    for a in range(4):
        total = (p1r[4 * a] + p1r[4 * a + 1]) + (p1r[4 * a + 2] + p1r[4 * a + 3])
        for j in range(GY):
            p2s[j, a : a + 1, :] = total[j : j + 1, :]

    def send_2(t):
        to = peer_y(t)
        copy_y(p2s.at[to], p2r.at[me_y], s2, to, to, me_y).start()

    def arrive_2(t):
        frm = peer_y(t)
        copy_y(p2s.at[frm], p2r.at[frm], s2, frm, frm, frm).wait_recv()

    each(GY, send_2)
    p2r[me_y] = p2s[me_y]
    def arrive_pk(t):
        frm = peer_y(t)
        copy_y(pks, pkr.at[frm], spk, frm, frm, frm).wait_recv()

    def arrive_yc(t):
        frm = peer_y(t)
        copy_y(ycs.at[frm], ycr.at[frm], syc, frm, frm, frm).wait_recv()

    each(GY, arrive_pk)
    each(GY, arrive_yc)
    share_z = ((me_y // 2) * 128 + lax.broadcasted_iota(jnp.int32, (128, 128), 0)).astype(F32)
    share_x = (lax.rem(me_y, 2) * 8 + lax.broadcasted_iota(jnp.int32, (8, 128), 0)).astype(F32)

    def build_share(r):
        info = pkr[r]
        for k in range(CAP):
            zhot[r, :, 128 * k : 128 * k + 128] = jnp.where(share_z == info[12 + k : 13 + k, :], 1.0, 0.0).astype(BF16)
            match = share_x == info[8 + k : 9 + k, :]
            for slot in range(2):
                weight = info[4 * slot + k : 4 * slot + k + 1, :]
                xmask[r, slot, :, 128 * k : 128 * k + 128] = jnp.where(match, weight, 0.0)

    each(GY, build_share, 0)
    q_y = ycr[0, 0] + ycr[0, 1] + ycr[1, 2]
    for r in range(1, GY):
        a = ycr[r, 0]
        m = inverse(a + q_y)
        yk[r, 0] = a * m
        yk[r, 1] = m
        more = ycr[r + 1, 2] if r < GY - 1 else 1.0
        q_y = ycr[r, 1] + more + a * m * q_y
    yk[0, 0] = inverse(q_y)
    each(GY, arrive_2)
    gathered = p2r[0]
    for j in range(1, GY):
        gathered = gathered + p2r[j]
    row = jnp.concatenate([gathered[a : a + 1, :] for a in range(4)], axis=1)
    weights.wait()
    new_row = 0.5 * cur_row + exact_dot(row, cw[...], ((1,), (1,)))
    for a in range(4):
        ys[a : a + 1, :] = new_row[:, 128 * a : 128 * a + 128]

    def send_a(t):
        to = peer_y(t)
        copy_y(ys, ga.at[me_y], sa, to, to, me_y).start()

    def arrive_a(t):
        frm = peer_y(t)
        copy_y(ys, ga.at[frm], sa, frm, frm, frm).wait_recv()

    each(GY, send_a)
    ga[me_y] = ys[...]
    for k in range(CAP):
        cur_out[k : k + 1, :] = exact_dot(new_row, spread[k], ((1,), (1,)))
    each(GY, arrive_a)
    for j in range(GY):
        part = ga[j]
        for a in range(4):
            gat[a, j : j + 1, :] = part[a : a + 1, :]

    def send_b(t):
        to = peer_x(t)
        copy_x(gat.at[to // 4], gb.at[me_x], sb, to, to, me_x).start()

    def arrive_b(t):
        frm = peer_x(t)
        copy_x(gat.at[0], gb.at[frm], sb, frm, frm, frm).wait_recv()

    each(GX, send_b)
    gb[me_x] = gat[me_x // 4]
    def drain_x(t):
        to = peer_x(t)
        for q in range(4):
            copy_x(xs.at[q, to], xr.at[q, me_x], xsem.at[q], to, to, me_x).wait_send()
            copy_x(vs.at[q, to], vr.at[q, me_x], vsem.at[q], to, to, me_x).wait_send()
        copy_x(p1s.at[to], p1r.at[me_x], s1, to, to, me_x).wait_send()

    def drain_y(t):
        to = peer_y(t)
        copy_y(p2s.at[to], p2r.at[me_y], s2, to, to, me_y).wait_send()
        copy_y(ycs.at[to], ycr.at[me_y], syc, to, to, me_y).wait_send()
        copy_y(yrs.at[to], yrr.at[me_y], syr, to, to, me_y).wait_send()
        copy_y(pks, pkr.at[me_y], spk, to, to, me_y).wait_send()

    each(GX, drain_x)
    each(GY, drain_y)
    each(GX, arrive_b)

    back = gb[...].reshape(128, 128)
    gbt[...] = back.T
    mine_rows = gbt[pl.ds(pl.multiple_of(lax.rem(me_x, 4) * 32, 32), 32), :]
    extra = []
    for r in range(GY):
        values = jnp.concatenate([mine_rows[CAP * r + k : CAP * r + k + 1, :] for k in range(CAP)], axis=1)
        parts = jnp.concatenate([xmask[r, 0] * values, xmask[r, 1] * values], axis=0)
        high = parts.astype(BF16)
        low = (parts - high.astype(F32)).astype(BF16)
        product = lax.dot_general(
            jnp.concatenate([high, low], axis=0), zhot[r], (((1,), (1,)), ((), ())), preferred_element_type=F32
        )
        extra.append((product[0:8] + product[16:24], product[8:16] + product[24:32]))

    def arrive_yr(t):
        frm = peer_y(t)
        copy_y(yrs.at[frm], yrr.at[frm], syr, frm, frm, frm).wait_recv()

    each(GY, arrive_yr)
    phi = (yrr[0, 0] + extra[0][0]) + (yrr[1, 1] + extra[1][1])
    phis = [phi]
    for r in range(1, GY):
        phi = (yrr[r, 0] + extra[r][0]) + yk[r, 0] * phi
        if r < GY - 1:
            phi = phi + (yrr[r + 1, 1] + extra[r + 1][1])
        phis.append(phi)
    value = phi * yk[0, 0]
    for r in range(GY - 1, 0, -1):
        yvs[r, 1] = value
        value = yk[r, 1] * phis[r - 1] + yk[r, 0] * value
        yvs[r, 0] = value
    yvs[0, 1] = value
    yvs[0, 0] = jnp.zeros((8, 128), F32)

    def send_yv(t):
        to = peer_y(t)
        copy_y(yvs.at[to], yvr.at[me_y], syv, to, to, me_y).start()

    def arrive_yv(t):
        frm = peer_y(t)
        copy_y(yvs.at[frm], yvr.at[frm], syv, frm, frm, frm).wait_recv()

    each(GY, send_yv)
    yvr[me_y] = yvs[me_y]

    lane_k = lax.broadcasted_iota(jnp.int32, (128, NZ), 1)
    for k in range(CAP):
        value = jnp.sum(jnp.where(lanes == mine + k, back, 0.0), axis=1, keepdims=True) * (INJECT / KY)
        spot = jnp.where(lane_k == zcol[:, k : k + 1], value, 0.0)
        high = spot.astype(BF16)
        bhl[128 * k : 128 * k + 128, :] = high
        bhl[WIRE + 128 * k : WIRE + 128 * k + 128, :] = (spot - high.astype(F32)).astype(BF16)

    def scatter(n, added):
        part = hot[pl.ds(pl.multiple_of(n * 256, 256), 256), :]
        added[...] = jnp.dot(jnp.concatenate([part, part], axis=1), bhl[...], preferred_element_type=F32)

    def eliminate_y(n, added, state):
        for step in range(16):
            y = n * 16 + step
            new = []
            for u in range(UNITS):
                row = step * CX + (u % 2) * 8
                more = added[row : row + 8, quarter(u // 2)]
                b = ((ht[at_y(y, u), :] + more) + state[u]) * my[at_y(y, u), :]
                ht[at_y(y, u), :] = b
                new.append(b)
            state = new
        return state

    def forward_y(n, state):
        scatter(2 * n + 1, added1)
        state = eliminate_y(2 * n, added0, state)
        scatter(jnp.minimum(2 * n + 2, CY // 16 - 1), added0)
        return eliminate_y(2 * n + 1, added1, state)

    scatter(0, added0)
    lax.fori_loop(0, CY // 32, forward_y, zeros)
    each(GY, arrive_yv)

    west_y = [yvr[u, 0] for u in range(UNITS)]
    east_y = [yvr[u, 1] for u in range(UNITS)]
    ob2 = ob.reshape(4 * PLANE, 128)

    def finish(n, value):
        c = CY // 8 - 1 - n
        for back_step in range(8):
            y = c * 8 + 7 - back_step
            value = [
                (ht[at_y(y, u), :] + ay[at_y(y, u), :] * west_y[u]) + my[at_y(y, u), :] * value[u]
                for u in range(UNITS)
            ]
            for u in range(UNITS):
                ob2[spread_rows(y, u), :] = value[u]
        return value

    for u in range(UNITS):
        ht[at_y(CY - 1, u), :] = jnp.zeros((8, 128), F32)
    lax.fori_loop(0, CY // 8, finish, east_y)

    def drain_late_x(t):
        copy_x(gat.at[0], gb.at[me_x], sb, peer_x(t), peer_x(t), me_x).wait_send()

    def drain_late_y(t):
        to = peer_y(t)
        copy_y(ys, ga.at[me_y], sa, to, to, me_y).wait_send()
        copy_y(yvs.at[to], yvr.at[me_y], syv, to, to, me_y).wait_send()

    each(GX, drain_late_x)
    each(GY, drain_late_y)


def deliver(staged, cur_in, out, cur_out, sems):
    def copy(d, q):
        return pltpu.make_async_copy(
            staged.at[q, d], out.at[:, pl.ds(pl.multiple_of(d * 8, 8), 8), 128 * q : 128 * q + 128], sems.at[q, d]
        )

    def start(d, carry):
        for q in range(4):
            copy(d, q).start()
        return carry

    def wait(d, carry):
        for q in range(4):
            copy(d, q).wait()
        return carry

    lax.fori_loop(0, GX, start, 0)
    cur_out[...] = cur_in[...]
    lax.fori_loop(0, GX, wait, 0)


def local(field, conduct, seg_cell, seg_count, currents, coupling):
    hbm = pl.BlockSpec(memory_space=pltpu.HBM)
    vmem = pl.BlockSpec(memory_space=pltpu.VMEM)
    cells = seg_cell[0].T
    block = lambda *shape: pltpu.VMEM(shape, F32)
    sems = lambda count: pltpu.SemaphoreType.DMA((2, count))
    scratch = [
        block(4, GX, CX, 8, 128),
        block(4, GX, CX, 8, 128),
        block(4, GX, CX, 8, 128),
        block(4, GX, CX, 8, 128),
        block(4, GX, 5, 8, 128),
        block(4, GX, 5, 8, 128),
        block(4, GX, 2, 8, 128),
        block(4, GX, 2, 8, 128),
        block(4 * PLANE, 128),
        block(4 * PLANE, 128),
        block(4 * PLANE, 128),
        pltpu.VMEM((WIRE, WIRE), BF16),
        pltpu.VMEM((PLANE, WIRE), BF16),
        pltpu.VMEM((2 * WIRE, NZ), BF16),
        block(WIRE, 128),
        pltpu.VMEM((128, 128), jnp.int32),
        pltpu.VMEM((CAP, 128), jnp.int32),
        pltpu.VMEM((1, 128), jnp.int32),
        block(CAP, 128),
        pltpu.VMEM((CAP, 128), jnp.int32),
        pltpu.SMEM((CAP, 128), jnp.int32),
        block(4 * PLANE, 128),
        block(4 * PLANE, 128),
        block(WIRE, 128),
        block(16, 128),
        block(GY, 16, 128),
        pltpu.VMEM((GY, 128, WIRE), BF16),
        block(GY, 2, 8, WIRE),
        block(128, 128),
        block(GY, 2, 8, 128),
        block(256, NZ),
        block(256, NZ),
        block(GX, 8, 128),
        block(GX, 8, 128),
        block(GY, 8, 128),
        block(GY, 8, 128),
        block(8, 128),
        block(GY, 8, 128),
        block(4, 8, 128),
        block(GX, 8, 128),
        block(GY, 3, 8, 128),
        block(GY, 3, 8, 128),
        block(GY, 2, 8, 128),
        block(GY, 2, 8, 128),
        block(GY, 2, 8, 128),
        block(GY, 2, 8, 128),
        pltpu.SemaphoreType.DMA((GX, 4)),
        pltpu.SemaphoreType.DMA((GX, 4)),
        pltpu.SemaphoreType.DMA,
        pltpu.SemaphoreType.DMA((4, 2, GX)),
        pltpu.SemaphoreType.DMA((4, 2, GX)),
        sems(GX),
        sems(GY),
        sems(GY),
        sems(GX),
        sems(GY),
        sems(GY),
        sems(GY),
        sems(GY),
        pltpu.SemaphoreType.DMA((3,)),
        pltpu.SemaphoreType.DMA,
    ]
    staged, currents_next = pl.pallas_call(
        kernel,
        out_shape=(
            pltpu.VMEM((4, GX, CX, 8, 128), F32),
            pltpu.VMEM((CAP, 128), F32),
        ),
        in_specs=[hbm] * 6,
        out_specs=(vmem, vmem),
        scratch_shapes=scratch,
        compiler_params=pltpu.CompilerParams(
            collective_id=0, has_side_effects=True, vmem_limit_bytes=57 * 1024 * 1024
        ),
    )(field, conduct, cells, seg_count, currents[0].T, coupling[0])
    field_next, currents_next = pl.pallas_call(
        deliver,
        out_shape=(
            jax.ShapeDtypeStruct((CX, CY, NZ), F32),
            jax.ShapeDtypeStruct((CAP, 128), F32),
        ),
        in_specs=[pl.BlockSpec(memory_space=pl.ANY), vmem],
        out_specs=(hbm, vmem),
        scratch_shapes=[pltpu.SemaphoreType.DMA((4, GX))],
        compiler_params=pltpu.CompilerParams(vmem_limit_bytes=4 * 1024 * 1024),
    )(staged, currents_next)
    return field_next, currents_next.T[None]


def solution(mesh):
    placed = (
        P("gx", "gy", None),
        P("gx", "gy", None),
        P(("gx", "gy"), None, None),
        P(("gx", "gy"), None),
        P(("gx", "gy"), None, None),
        P(("gx", "gy"), None, None),
    )
    return jax.shard_map(
        local,
        mesh=mesh,
        in_specs=placed,
        out_specs=(P("gx", "gy", None), P(("gx", "gy"), None, None)),
        check_vma=False,
    )
```

```python
import functools

import jax
import jax.numpy as jnp
from jax import lax
from jax.experimental import pallas as pl
from jax.experimental.pallas import tpu as pltpu
from jax.sharding import PartitionSpec as P

MESH = pl.DeviceIdType.MESH
F32 = jnp.float32
BF16 = jnp.bfloat16

CX, CY, NZ, CAP = 16, 128, 512, 4
GX, GY = 16, 8
WIRE = 512
KX = 8.0 * CX * CX
KY = 8.0 * CY * CY
INJECT = 4.0 * KY**0.5
PLANE = CY * CX
UNITS = 8
EARLY = 2


def inverse(value):
    return pl.reciprocal(value, approx=True)


def split3(value):
    high = value.astype(BF16).astype(F32)
    rest = value - high
    middle = rest.astype(BF16).astype(F32)
    return high, middle, rest - middle


def kernel(
    field,
    conduct,
    cell_h,
    count_h,
    cur_h,
    coupling,
    ob,
    cur_out,
    fb,
    cb,
    mx,
    ax,
    xs,
    xr,
    vs,
    vr,
    ht,
    my,
    ay,
    cw,
    hot,
    bhl,
    samp,
    zcol,
    cell_v,
    count_v,
    cur_v,
    rows_v,
    rows_s,
    rows_n,
    rows_t,
    samp3,
    pas,
    par,
    lines,
    acc,
    tmat,
    cw2,
    wv,
    wp,
    samp2,
    pks,
    pkr,
    zhot,
    xmask,
    gbt,
    yk,
    added0,
    added1,
    p1s,
    p1r,
    p2s,
    p2r,
    ys,
    ga,
    gat,
    gb,
    ycs,
    ycr,
    yrs,
    yrr,
    yvs,
    yvr,
    fsem,
    csem,
    wsem,
    xsem,
    vsem,
    s1,
    s2,
    sa,
    sb,
    syc,
    syr,
    syv,
    spk,
    spa,
    small,
    rsem,
):
    me_x = lax.axis_index("gx")
    me_y = lax.axis_index("gy")

    def peer_x(step):
        return lax.rem(me_x + step, GX)

    def peer_y(step):
        return lax.rem(me_y + step, GY)

    def each(count, body, start=1):
        def run(t, carry):
            body(t)
            return carry

        lax.fori_loop(start, count, run, 0)

    def chunk(d):
        return pl.ds(pl.multiple_of(d * 8, 8), 8)

    def quarter(q):
        return slice(128 * q, 128 * q + 128)

    def in_copies(d):
        copies = []
        for q in range(4):
            for src, dst, sem in ((conduct, cb, csem), (field, fb, fsem)):
                copies.append(
                    pltpu.make_async_copy(src.at[:, chunk(d), quarter(q)], dst.at[q, d], sem.at[d, q])
                )
        return copies

    def load4(ref, d, x):
        return jnp.concatenate([ref[q, d, x] for q in range(4)], axis=1)

    def order(t):
        u = 15 - t
        return lax.rem(me_x // 4 + u // 4, 4) * 4 + lax.rem(me_x + lax.rem(u, 4), 4)

    def start_in(t, carry):
        for copy in in_copies(order(t)):
            copy.start()
        return carry

    barrier = pltpu.get_barrier_semaphore()

    def greet_x(t, carry):
        pl.semaphore_signal(barrier, inc=1, device_id=(peer_x(t), me_y), device_id_type=MESH)
        return carry

    def greet_y(t, carry):
        pl.semaphore_signal(barrier, inc=1, device_id=(me_x, peer_y(t)), device_id_type=MESH)
        return carry

    lax.fori_loop(1, GX, greet_x, 0)
    lax.fori_loop(1, GY, greet_y, 0)
    lax.fori_loop(0, GX, start_in, 0)
    weights = pltpu.make_async_copy(coupling, cw, wsem)
    weights.start()
    smalls = [
        pltpu.make_async_copy(src, dst, small.at[i])
        for i, (src, dst) in enumerate(((cell_h, cell_v), (count_h, count_v), (cur_h, cur_v)))
    ]
    for copy in smalls:
        copy.start()

    def copy_x(src, dst, sems, slot, to, who):
        return pltpu.make_async_remote_copy(
            src_ref=src, dst_ref=dst, send_sem=sems.at[0, slot], recv_sem=sems.at[1, who],
            device_id=(to, me_y), device_id_type=MESH,
        )

    def copy_y(src, dst, sems, slot, to, who):
        return pltpu.make_async_remote_copy(
            src_ref=src, dst_ref=dst, send_sem=sems.at[0, slot], recv_sem=sems.at[1, who],
            device_id=(me_x, to), device_id_type=MESH,
        )

    lane_z = lax.broadcasted_iota(jnp.int32, (8, NZ), 1)
    scale_f = 1.0 / (KX * KY)

    def eliminate(ds):
        for d in ds:
            for copy in in_copies(d):
                copy.wait()

        def ground(d, x):
            return (1.0 / KX) + (0.5 / KX) * load4(cb, d, x)

        def source(d, x):
            value = load4(fb, d, x)
            up = jnp.where(lane_z == NZ - 1, 0.0, pltpu.roll(value, NZ - 1, 1))
            down = jnp.where(lane_z == 0, 0.0, pltpu.roll(value, 1, 1))
            return (0.5 * scale_f) * value + (0.25 * scale_f) * (up + down)

        blank4 = jnp.zeros((8, NZ), F32)
        states = [(jnp.ones((8, NZ), F32), ground(d, 0), source(d, 0), blank4, blank4) for d in ds]
        for x in range(CX - 1):
            for n, d in enumerate(ds):
                a, g, f, gp, fp = states[n]
                m = inverse(a + g + 1.0)
                am = a * m
                b = f * m
                gp = gp + am * g
                fp = fp + am * f
                f = source(d, x + 1) + b
                for q in range(4):
                    mx[q, d, x] = m[:, quarter(q)]
                    ax[q, d, x] = am[:, quarter(q)]
                    fb[q, d, x] = b[:, quarter(q)]
                states[n] = (am, ground(d, x + 1) + g * m, f, gp, fp)
        for n, d in enumerate(ds):
            for slot, value in enumerate(states[n]):
                for q in range(4):
                    xs[q, d, slot] = value[:, quarter(q)]

    def send_x(q, d):
        copy_x(xs.at[q, d], xr.at[q, me_x], xsem.at[q], d, d, me_x).start()

    def eliminate_and_send(t):
        d = order(t)
        eliminate([d])

        @pl.when(t < GX - 1)
        def _():
            send_x(0, d)

    each(EARLY, lambda t: eliminate([order(t)]), 0)
    pl.semaphore_wait(barrier, GX - 1 + GY - 1)
    each(EARLY, lambda t: send_x(0, order(t)), 0)
    each(GX, eliminate_and_send, EARLY)
    for q in range(1, 3):
        each(GX - 1, lambda t, q=q: send_x(q, order(t)), 0)
    for q in range(4):
        xr[q, me_x] = xs[q, me_x]

    def respond(d):
        own = jnp.zeros((8, NZ), F32)
        west = jnp.zeros((8, NZ), F32)
        last = jnp.ones((8, NZ), F32)
        for x in range(CX - 1, -1, -1):
            if x < CX - 1:
                m = load4(mx, d, x)
                own = load4(fb, d, x) + m * own
                west = load4(ax, d, x) + m * west
                last = m * last
            for q in range(4):
                fb[q, d, x] = own[:, quarter(q)]
                ax[q, d, x] = west[:, quarter(q)]
                mx[q, d, x] = last[:, quarter(q)]

    each(GX, respond, 0)

    for copy in smalls:
        copy.wait()
    cells = cell_v[...]
    slot_of = lax.broadcasted_iota(jnp.int32, (CAP, 128), 0)
    filled = slot_of < count_v[...]
    at_x = cells >> 16
    place_z = jnp.where(filled, cells & (NZ - 1), -1)
    place_r = ((cells >> 9) & (CY - 1)) * CX + at_x
    rows_v[...] = ((cells >> 7) & 3) * PLANE + (at_x >> 3) * (8 * CY) + ((cells >> 9) & (CY - 1)) * 8 + (at_x & 7)
    rows_n[...] = ((cells >> 7) & 3) * PLANE + ((cells >> 12) & 15) * 128 + at_x * 8 + ((cells >> 9) & 7)
    rows_copies = [
        pltpu.make_async_copy(rows_n, rows_t, rsem.at[0]),
        pltpu.make_async_copy(rows_v, rows_s, rsem.at[1]),
    ]
    for copy in rows_copies:
        copy.start()
    zcol[...] = jnp.concatenate([place_z, jnp.full((128 - CAP, 128), -1, jnp.int32)], axis=0).T
    lanes = lax.broadcasted_iota(jnp.int32, (128, 128), 1)

    def hit_of(k):
        z = zcol[:, k : k + 1]
        return ((z & 127) == lanes) & (z >= 0)

    def pick(table, pairs):
        def run(n):
            for i in range(16):
                o = n * 16 + i
                for k in range(CAP):
                    row = table[k, o]
                    for src, dst in pairs:
                        dst[pl.ds(k * 128 + o, 1), :] = src[pl.ds(row, 1), :]

        each(128 // 16, run, 0)

    rows_copies[0].wait()
    pick(rows_t, [(ref.reshape(4 * PLANE, 128), dst) for ref, dst in ((fb, samp), (ax, samp2), (mx, samp3))])
    for k in range(CAP):
        hit = hit_of(k)
        rows = slice(128 * k, 128 * k + 128)
        for slot, ref in enumerate((samp, samp2, samp3)):
            chosen = jnp.where(hit, ref[rows, :], 0.0) * KY
            pas[slot * CAP + k : slot * CAP + k + 1, :] = jnp.sum(chosen.T, axis=0, keepdims=True)
    key = ((cells >> 12) & 15) * 32 + ((cells >> 7) & 3) * 8 + ((cells >> 9) & 7)
    pas[3 * CAP : 4 * CAP, :] = (key * 128 + (cells & 127)).astype(F32)

    def send_pa(t):
        to = order(t)
        copy_x(pas, par.at[me_x], spa, to, to, me_x).start()

    each(GX - 1, send_pa, 0)
    par[me_x] = pas[...]
    each(GX - 1, lambda t: send_x(3, order(t)), 0)

    cb2 = cb.reshape(4 * PLANE, 128)

    def spread_rows(y, u):
        return pl.ds((u // 2) * PLANE + (y // 8) * (8 * CX) + (u % 2) * 64 + lax.rem(y, 8), 8, stride=8)

    def ground_y(y):
        return [(1.0 / KY) + (0.5 / KY) * cb2[spread_rows(y, u), :] for u in range(UNITS)]

    def at_y(y, u):
        return pl.ds(pl.multiple_of(u * (8 * CY) + y * 8, 8), 8)

    row_16 = lax.broadcasted_iota(jnp.int32, (CX, 128), 0)

    def build_hot(y):
        rows = row_16 + y * CX
        for k in range(CAP):
            match = jnp.where(rows == place_r[k : k + 1, :], 1.0, 0.0)
            hot[pl.ds(pl.multiple_of(y * CX, CX), CX), quarter(k)] = match.astype(BF16)

    def factor(y, state):
        a, g, gp = state
        build_hot(y)
        after = ground_y(y + 1)
        a_new, g_new, gp_new = [], [], []
        for u in range(UNITS):
            m = inverse(a[u] + g[u] + 1.0)
            am = a[u] * m
            my[at_y(y, u), :] = m
            ay[at_y(y, u), :] = am
            gp_new.append(gp[u] + am * g[u])
            g_new.append(after[u] + g[u] * m)
            a_new.append(am)
        return a_new, g_new, gp_new

    ones = [jnp.ones((8, 128), F32) for _ in range(UNITS)]
    zeros = [jnp.zeros((8, 128), F32) for _ in range(UNITS)]
    a_y, g_y, gp_y = lax.fori_loop(0, CY - 1, factor, (ones, ground_y(0), zeros))
    build_hot(CY - 1)
    for u in range(UNITS):
        for slot, value in enumerate((a_y, g_y, gp_y)):
            ycs[u, slot] = value[u]

    for u in range(UNITS):
        my[at_y(CY - 1, u), :] = jnp.ones((8, 128), F32)
        ay[at_y(CY - 1, u), :] = jnp.zeros((8, 128), F32)
        wv[at_y(CY - 1, u), :] = jnp.ones((8, 128), F32)
        wp[at_y(CY - 1, u), :] = jnp.zeros((8, 128), F32)

    def send_yc(t):
        to = peer_y(t)
        copy_y(ycs.at[to], ycr.at[me_y], syc, to, to, me_y).start()

    each(GY, send_yc)
    ycr[me_y] = ycs[me_y]

    def weigh(n, state):
        y = CY - 2 - n
        to_last, to_west = state
        last_new, west_new = [], []
        for u in range(UNITS):
            m = my[at_y(y, u), :]
            last_new.append(m * to_last[u])
            west_new.append(ay[at_y(y, u), :] + m * to_west[u])
            wv[at_y(y, u), :] = last_new[u]
            wp[at_y(y, u), :] = west_new[u]
        return last_new, west_new

    lax.fori_loop(0, CY - 1, weigh, (ones, zeros))

    rows_copies[1].wait()
    pick(rows_s, [(wv, samp), (wp, samp2)])
    for k in range(CAP):
        hit = hit_of(k)
        rows = slice(128 * k, 128 * k + 128)
        for slot, ref in enumerate((samp, samp2)):
            chosen = jnp.where(hit, ref[rows, :], 0.0) * (INJECT / KY)
            pks[slot * CAP + k : slot * CAP + k + 1, :] = jnp.sum(chosen.T, axis=0, keepdims=True)
    pks[2 * CAP : 3 * CAP, :] = at_x.astype(F32)
    pks[3 * CAP : 4 * CAP, :] = place_z.astype(F32)

    def send_pk(t):
        to = peer_y(t)
        copy_y(pks, pkr.at[me_y], spk, to, to, me_y).start()

    each(GY, send_pk)
    pkr[me_y] = pks[...]

    blank = jnp.zeros((8, 128), F32)

    def reduce_x(q):
        def arrive(t):
            frm = peer_x(t)
            copy_x(xs.at[q, frm], xr.at[q, frm], xsem.at[q], frm, frm, frm).wait_recv()

        each(GX, arrive)
        q_x = xr[q, 0, 0] + xr[q, 0, 1] + xr[q, 1, 3]
        phi = xr[q, 0, 2] + xr[q, 1, 4]
        kept = [None]
        for r in range(1, GX):
            a = xr[q, r, 0]
            m = inverse(a + q_x)
            am = a * m
            kept.append((am, m * phi))
            more_g, more_f = (xr[q, r + 1, 3], xr[q, r + 1, 4]) if r < GX - 1 else (1.0, 0.0)
            q_x = xr[q, r, 1] + more_g + am * q_x
            phi = xr[q, r, 2] + more_f + am * phi
        value = phi * inverse(q_x)
        for r in range(GX - 1, 0, -1):
            vs[q, r, 1] = value
            value = kept[r][1] + kept[r][0] * value
            vs[q, r, 0] = value
        vs[q, 0, 1] = value
        vs[q, 0, 0] = blank

    def send_back(q):
        def send(t):
            to = peer_x(t)
            copy_x(vs.at[q, to], vr.at[q, me_x], vsem.at[q], to, to, me_x).start()

        each(GX, send)
        vr[q, me_x] = vs[q, me_x]

    row_8 = lax.broadcasted_iota(jnp.int32, (8, 128), 0)
    row_128 = lax.broadcasted_iota(jnp.int32, (128, 128), 0)

    def build_lines(r):
        code = par[r, 3 * CAP : 4 * CAP, :].astype(jnp.int32)
        for k in range(CAP):
            match = jnp.where(row_128 == (code[k : k + 1, :] & 127), 1.0, 0.0)
            lines[r, :, quarter(k)] = match.astype(BF16)

    def gather_x(quarters, first):
        def one(r):
            info = par[r]
            code = info[3 * CAP : 4 * CAP, :].astype(jnp.int32)
            parts = []
            for q in quarters:
                value = vs[q, r].reshape(16, 128)
                high = value.astype(BF16).astype(F32)
                parts.extend((high, value - high))
            product = jnp.dot(jnp.concatenate(parts, axis=0).astype(BF16), lines[r], preferred_element_type=F32)
            for k in range(CAP):
                total = jnp.zeros((8, 128), F32) if first else acc[r, :, quarter(k)]
                for n, q in enumerate(quarters):
                    solved = product[32 * n : 32 * n + 16, quarter(k)] + product[32 * n + 16 : 32 * n + 32, quarter(k)]
                    match = (code[k : k + 1, :] >> 7) == me_x * 32 + q * 8 + row_8
                    value = (
                        info[k : k + 1, :]
                        + info[CAP + k : CAP + k + 1, :] * solved[0:8]
                        + info[2 * CAP + k : 2 * CAP + k + 1, :] * solved[8:16]
                    )
                    total = total + jnp.where(match, value, 0.0)
                acc[r, :, quarter(k)] = total

        def four(n):
            for i in range(4):
                one(n * 4 + i)

        each(4, four, 0)

    reduce_x(0)
    send_back(0)
    reduce_x(1)
    send_back(1)

    def arrive_pa(t):
        frm = peer_x(t)
        copy_x(pas, par.at[frm], spa, frm, frm, frm).wait_recv()

    each(GX, arrive_pa)
    each(GX, build_lines, 0)
    reduce_x(2)
    send_back(2)
    gather_x((0, 1, 2), True)
    reduce_x(3)
    gather_x((3,), False)

    tmat[...] = jnp.zeros_like(tmat)
    p2s[...] = jnp.zeros_like(p2s)
    ys[...] = jnp.zeros_like(ys)
    mine = lax.rem(me_x, 4) * 32 + me_y * CAP
    for r in range(GX):
        total = jnp.sum(acc[r], axis=0, keepdims=True)
        for k in range(CAP):
            tmat[pl.ds(lax.rem(me_y, 2) * 64 + CAP * r + k, 1), :] = total[:, quarter(k)]
    p1s[...] = tmat[...].T.reshape(GX, GY, 128)

    def send_1(t):
        to = peer_x(t)
        copy_x(p1s.at[to], p1r.at[me_x], s1, to, to, me_x).start()

    def arrive_1(t):
        frm = peer_x(t)
        copy_x(p1s.at[frm], p1r.at[frm], s1, frm, frm, frm).wait_recv()

    each(GX, send_1)
    p1r[me_x] = p1s[me_x]
    send_back(3)

    row_m = lax.broadcasted_iota(jnp.int32, (128, WIRE), 0)
    lane_m = lax.broadcasted_iota(jnp.int32, (128, WIRE), 1)
    spread = [jnp.where(lane_m == row_m * CAP + k, 1.0, 0.0).astype(BF16) for k in range(CAP)]

    def three_rows(row):
        high, middle, low = split3(row)
        index = lax.broadcasted_iota(jnp.int32, (16, row.shape[1]), 0)
        stack = jnp.where(index == 0, high, jnp.where(index == 1, middle, jnp.where(index == 2, low, 0.0)))
        return stack.astype(BF16)

    def exact_dot(row, matrix, dims):
        product = lax.dot_general(three_rows(row), matrix, (dims, ((), ())), preferred_element_type=F32)
        return (product[2:3] + product[1:2]) + product[0:1]

    cur_row = jnp.zeros((1, WIRE), F32)
    for k in range(CAP):
        cur_row = cur_row + exact_dot(cur_v[k : k + 1, :], spread[k], ((1,), (0,)))
    lane_n = lax.broadcasted_iota(jnp.int32, (WIRE, WIRE), 1)
    source_n = ((lane_n >> 2) & 15) * 32 + (lane_n >> 6) * CAP + (lane_n & 3)
    shuffle = jnp.where(lax.broadcasted_iota(jnp.int32, (WIRE, WIRE), 0) == source_n, 1.0, 0.0).astype(BF16)
    weights.wait()
    cw2[...] = jnp.dot(cw[...], shuffle, preferred_element_type=F32).astype(BF16)

    def substitute(q):
        def arrive(t):
            frm = peer_x(t)
            copy_x(vs.at[q, frm], vr.at[q, frm], vsem.at[q], frm, frm, frm).wait_recv()

        def group(n):
            ds = [n * 4 + i for i in range(4)]
            west = [vr[q, d, 0] for d in ds]
            last = [vr[q, d, 1] for d in ds]
            for x in range(CX):
                value = [
                    (fb[q, d, x] + ax[q, d, x] * west[i]) + mx[q, d, x] * last[i] for i, d in enumerate(ds)
                ]
                for i, d in enumerate(ds):
                    ht[pl.ds((2 * q + x // 8) * (8 * CY) + d * 64 + x % 8, 8, stride=8), :] = value[i]

        each(GX, arrive)
        each(4, group, 0)

    substitute(0)
    substitute(1)
    each(GX, arrive_1)
    total = p1r[0]
    for i in range(1, GX):
        total = total + p1r[i]
    for j in range(GY):
        p2s[j, 0:1, :] = total[j : j + 1, :]

    def send_2(t):
        to = peer_y(t)
        copy_y(p2s.at[to], p2r.at[me_y], s2, to, to, me_y).start()

    def arrive_2(t):
        frm = peer_y(t)
        copy_y(p2s.at[frm], p2r.at[frm], s2, frm, frm, frm).wait_recv()

    each(GY, send_2)
    p2r[me_y] = p2s[me_y]
    def arrive_pk(t):
        frm = peer_y(t)
        copy_y(pks, pkr.at[frm], spk, frm, frm, frm).wait_recv()

    def arrive_yc(t):
        frm = peer_y(t)
        copy_y(ycs.at[frm], ycr.at[frm], syc, frm, frm, frm).wait_recv()

    each(GY, arrive_pk)
    each(GY, arrive_yc)
    share_z = ((me_y // 2) * 128 + lax.broadcasted_iota(jnp.int32, (128, 128), 0)).astype(F32)
    share_x = (lax.rem(me_y, 2) * 8 + lax.broadcasted_iota(jnp.int32, (8, 128), 0)).astype(F32)

    def build_share(r):
        info = pkr[r]
        for k in range(CAP):
            zhot[r, :, 128 * k : 128 * k + 128] = jnp.where(share_z == info[12 + k : 13 + k, :], 1.0, 0.0).astype(BF16)
            match = share_x == info[8 + k : 9 + k, :]
            for slot in range(2):
                weight = info[4 * slot + k : 4 * slot + k + 1, :]
                xmask[r, slot, :, 128 * k : 128 * k + 128] = jnp.where(match, weight, 0.0)

    each(GY, build_share, 0)
    q_y = ycr[0, 0] + ycr[0, 1] + ycr[1, 2]
    for r in range(1, GY):
        a = ycr[r, 0]
        m = inverse(a + q_y)
        yk[r, 0] = a * m
        yk[r, 1] = m
        more = ycr[r + 1, 2] if r < GY - 1 else 1.0
        q_y = ycr[r, 1] + more + a * m * q_y
    yk[0, 0] = inverse(q_y)
    substitute(2)
    each(GY, arrive_2)
    row = jnp.concatenate([p2r[2 * j, 0:1, :] + p2r[2 * j + 1, 0:1, :] for j in range(4)], axis=1)
    new_row = 0.5 * cur_row + exact_dot(row, cw2[...], ((1,), (1,)))
    for a in range(4):
        ys[a : a + 1, :] = new_row[:, 128 * a : 128 * a + 128]

    def send_a(t):
        to = peer_y(t)
        copy_y(ys, ga.at[me_y], sa, to, to, me_y).start()

    def arrive_a(t):
        frm = peer_y(t)
        copy_y(ys, ga.at[frm], sa, frm, frm, frm).wait_recv()

    each(GY, send_a)
    ga[me_y] = ys[...]
    for k in range(CAP):
        cur_out[k : k + 1, :] = exact_dot(new_row, spread[k], ((1,), (1,)))
    substitute(3)
    def sum_up(y, state):
        f, fp = state
        f_new, fp_new = [], []
        for u in range(UNITS):
            fp_new.append(fp[u] + ay[at_y(y, u), :] * f[u])
            f_new.append(ht[at_y(y + 1, u), :] + f[u] * my[at_y(y, u), :])
        return f_new, fp_new

    first = [ht[at_y(0, u), :] for u in range(UNITS)]
    f_y, fp_y = lax.fori_loop(0, CY - 1, sum_up, (first, zeros))
    for u in range(UNITS):
        for slot, value in enumerate((f_y, fp_y)):
            yrs[u, slot] = value[u]

    def send_yr(t):
        to = peer_y(t)
        copy_y(yrs.at[to], yrr.at[me_y], syr, to, to, me_y).start()

    each(GY, send_yr)
    yrr[me_y] = yrs[me_y]
    each(GY, arrive_a)
    for j in range(GY):
        part = ga[j]
        for a in range(4):
            gat[a, j : j + 1, :] = part[a : a + 1, :]

    def send_b(t):
        to = peer_x(t)
        copy_x(gat.at[to // 4], gb.at[me_x], sb, to, to, me_x).start()

    def arrive_b(t):
        frm = peer_x(t)
        copy_x(gat.at[0], gb.at[frm], sb, frm, frm, frm).wait_recv()

    each(GX, send_b)
    gb[me_x] = gat[me_x // 4]
    def drain_x(t):
        to = peer_x(t)
        for q in range(4):
            copy_x(xs.at[q, to], xr.at[q, me_x], xsem.at[q], to, to, me_x).wait_send()
            copy_x(vs.at[q, to], vr.at[q, me_x], vsem.at[q], to, to, me_x).wait_send()
        copy_x(p1s.at[to], p1r.at[me_x], s1, to, to, me_x).wait_send()
        copy_x(pas, par.at[me_x], spa, to, to, me_x).wait_send()

    def drain_y(t):
        to = peer_y(t)
        copy_y(p2s.at[to], p2r.at[me_y], s2, to, to, me_y).wait_send()
        copy_y(ycs.at[to], ycr.at[me_y], syc, to, to, me_y).wait_send()
        copy_y(yrs.at[to], yrr.at[me_y], syr, to, to, me_y).wait_send()
        copy_y(pks, pkr.at[me_y], spk, to, to, me_y).wait_send()

    each(GX, drain_x)
    each(GY, drain_y)
    each(GX, arrive_b)

    back = gb[...].reshape(128, 128)
    gbt[...] = back.T
    mine_rows = gbt[pl.ds(pl.multiple_of(lax.rem(me_x, 4) * 32, 32), 32), :]
    extra = []
    for r in range(GY):
        values = jnp.concatenate([mine_rows[CAP * r + k : CAP * r + k + 1, :] for k in range(CAP)], axis=1)
        parts = jnp.concatenate([xmask[r, 0] * values, xmask[r, 1] * values], axis=0)
        high = parts.astype(BF16)
        low = (parts - high.astype(F32)).astype(BF16)
        product = lax.dot_general(
            jnp.concatenate([high, low], axis=0), zhot[r], (((1,), (1,)), ((), ())), preferred_element_type=F32
        )
        extra.append((product[0:8] + product[16:24], product[8:16] + product[24:32]))

    def arrive_yr(t):
        frm = peer_y(t)
        copy_y(yrs.at[frm], yrr.at[frm], syr, frm, frm, frm).wait_recv()

    each(GY, arrive_yr)
    phi = (yrr[0, 0] + extra[0][0]) + (yrr[1, 1] + extra[1][1])
    phis = [phi]
    for r in range(1, GY):
        phi = (yrr[r, 0] + extra[r][0]) + yk[r, 0] * phi
        if r < GY - 1:
            phi = phi + (yrr[r + 1, 1] + extra[r + 1][1])
        phis.append(phi)
    value = phi * yk[0, 0]
    for r in range(GY - 1, 0, -1):
        yvs[r, 1] = value
        value = yk[r, 1] * phis[r - 1] + yk[r, 0] * value
        yvs[r, 0] = value
    yvs[0, 1] = value
    yvs[0, 0] = jnp.zeros((8, 128), F32)

    def send_yv(t):
        to = peer_y(t)
        copy_y(yvs.at[to], yvr.at[me_y], syv, to, to, me_y).start()

    def arrive_yv(t):
        frm = peer_y(t)
        copy_y(yvs.at[frm], yvr.at[frm], syv, frm, frm, frm).wait_recv()

    each(GY, send_yv)
    yvr[me_y] = yvs[me_y]

    lane_k = lax.broadcasted_iota(jnp.int32, (128, NZ), 1)
    for k in range(CAP):
        value = jnp.sum(jnp.where(lanes == mine + k, back, 0.0), axis=1, keepdims=True) * (INJECT / KY)
        spot = jnp.where(lane_k == zcol[:, k : k + 1], value, 0.0)
        high = spot.astype(BF16)
        bhl[128 * k : 128 * k + 128, :] = high
        bhl[WIRE + 128 * k : WIRE + 128 * k + 128, :] = (spot - high.astype(F32)).astype(BF16)

    def scatter(n, added):
        part = hot[pl.ds(pl.multiple_of(n * 256, 256), 256), :]
        added[...] = jnp.dot(jnp.concatenate([part, part], axis=1), bhl[...], preferred_element_type=F32)

    def eliminate_y(n, added, state):
        for step in range(16):
            y = n * 16 + step
            new = []
            for u in range(UNITS):
                row = step * CX + (u % 2) * 8
                more = added[row : row + 8, quarter(u // 2)]
                b = ((ht[at_y(y, u), :] + more) + state[u]) * my[at_y(y, u), :]
                ht[at_y(y, u), :] = b
                new.append(b)
            state = new
        return state

    def forward_y(n, state):
        scatter(2 * n + 1, added1)
        state = eliminate_y(2 * n, added0, state)
        scatter(jnp.minimum(2 * n + 2, CY // 16 - 1), added0)
        return eliminate_y(2 * n + 1, added1, state)

    scatter(0, added0)
    lax.fori_loop(0, CY // 32, forward_y, zeros)
    each(GY, arrive_yv)

    west_y = [yvr[u, 0] for u in range(UNITS)]
    east_y = [yvr[u, 1] for u in range(UNITS)]
    ob2 = ob.reshape(4 * PLANE, 128)

    def finish(n, value):
        c = CY // 8 - 1 - n
        for back_step in range(8):
            y = c * 8 + 7 - back_step
            value = [
                (ht[at_y(y, u), :] + ay[at_y(y, u), :] * west_y[u]) + my[at_y(y, u), :] * value[u]
                for u in range(UNITS)
            ]
            for u in range(UNITS):
                ob2[spread_rows(y, u), :] = value[u]
        return value

    for u in range(UNITS):
        ht[at_y(CY - 1, u), :] = jnp.zeros((8, 128), F32)
    lax.fori_loop(0, CY // 8, finish, east_y)

    def drain_late_x(t):
        copy_x(gat.at[0], gb.at[me_x], sb, peer_x(t), peer_x(t), me_x).wait_send()

    def drain_late_y(t):
        to = peer_y(t)
        copy_y(ys, ga.at[me_y], sa, to, to, me_y).wait_send()
        copy_y(yvs.at[to], yvr.at[me_y], syv, to, to, me_y).wait_send()

    each(GX, drain_late_x)
    each(GY, drain_late_y)


def deliver(staged, cur_in, out, cur_out, sems):
    def copy(d, q):
        return pltpu.make_async_copy(
            staged.at[q, d], out.at[:, pl.ds(pl.multiple_of(d * 8, 8), 8), 128 * q : 128 * q + 128], sems.at[q, d]
        )

    def start(d, carry):
        for q in range(4):
            copy(d, q).start()
        return carry

    def wait(d, carry):
        for q in range(4):
            copy(d, q).wait()
        return carry

    lax.fori_loop(0, GX, start, 0)
    cur_out[...] = cur_in[...]
    lax.fori_loop(0, GX, wait, 0)


def local(field, conduct, seg_cell, seg_count, currents, coupling):
    hbm = pl.BlockSpec(memory_space=pltpu.HBM)
    vmem = pl.BlockSpec(memory_space=pltpu.VMEM)
    cells = seg_cell[0].T
    block = lambda *shape: pltpu.VMEM(shape, F32)
    sems = lambda count: pltpu.SemaphoreType.DMA((2, count))
    scratch = [
        block(4, GX, CX, 8, 128),
        block(4, GX, CX, 8, 128),
        block(4, GX, CX, 8, 128),
        block(4, GX, CX, 8, 128),
        block(4, GX, 5, 8, 128),
        block(4, GX, 5, 8, 128),
        block(4, GX, 2, 8, 128),
        block(4, GX, 2, 8, 128),
        block(4 * PLANE, 128),
        block(4 * PLANE, 128),
        block(4 * PLANE, 128),
        pltpu.VMEM((WIRE, WIRE), BF16),
        pltpu.VMEM((PLANE, WIRE), BF16),
        pltpu.VMEM((2 * WIRE, NZ), BF16),
        block(WIRE, 128),
        pltpu.VMEM((128, 128), jnp.int32),
        pltpu.VMEM((CAP, 128), jnp.int32),
        pltpu.VMEM((1, 128), jnp.int32),
        block(CAP, 128),
        pltpu.VMEM((CAP, 128), jnp.int32),
        pltpu.SMEM((CAP, 128), jnp.int32),
        pltpu.VMEM((CAP, 128), jnp.int32),
        pltpu.SMEM((CAP, 128), jnp.int32),
        block(WIRE, 128),
        block(16, 128),
        block(GX, 16, 128),
        pltpu.VMEM((GX, 128, WIRE), BF16),
        block(GX, 8, WIRE),
        block(128, 128),
        pltpu.VMEM((WIRE, WIRE), BF16),
        block(4 * PLANE, 128),
        block(4 * PLANE, 128),
        block(WIRE, 128),
        block(16, 128),
        block(GY, 16, 128),
        pltpu.VMEM((GY, 128, WIRE), BF16),
        block(GY, 2, 8, WIRE),
        block(128, 128),
        block(GY, 2, 8, 128),
        block(256, NZ),
        block(256, NZ),
        block(GX, 8, 128),
        block(GX, 8, 128),
        block(GY, 8, 128),
        block(GY, 8, 128),
        block(8, 128),
        block(GY, 8, 128),
        block(4, 8, 128),
        block(GX, 8, 128),
        block(GY, 3, 8, 128),
        block(GY, 3, 8, 128),
        block(GY, 2, 8, 128),
        block(GY, 2, 8, 128),
        block(GY, 2, 8, 128),
        block(GY, 2, 8, 128),
        pltpu.SemaphoreType.DMA((GX, 4)),
        pltpu.SemaphoreType.DMA((GX, 4)),
        pltpu.SemaphoreType.DMA,
        pltpu.SemaphoreType.DMA((4, 2, GX)),
        pltpu.SemaphoreType.DMA((4, 2, GX)),
        sems(GX),
        sems(GY),
        sems(GY),
        sems(GX),
        sems(GY),
        sems(GY),
        sems(GY),
        sems(GY),
        sems(GX),
        pltpu.SemaphoreType.DMA((3,)),
        pltpu.SemaphoreType.DMA((2,)),
    ]
    staged, currents_next = pl.pallas_call(
        kernel,
        out_shape=(
            pltpu.VMEM((4, GX, CX, 8, 128), F32),
            pltpu.VMEM((CAP, 128), F32),
        ),
        in_specs=[hbm] * 6,
        out_specs=(vmem, vmem),
        scratch_shapes=scratch,
        compiler_params=pltpu.CompilerParams(
            collective_id=0, has_side_effects=True, vmem_limit_bytes=57 * 1024 * 1024
        ),
    )(field, conduct, cells, seg_count, currents[0].T, coupling[0])
    field_next, currents_next = pl.pallas_call(
        deliver,
        out_shape=(
            jax.ShapeDtypeStruct((CX, CY, NZ), F32),
            jax.ShapeDtypeStruct((CAP, 128), F32),
        ),
        in_specs=[pl.BlockSpec(memory_space=pl.ANY), vmem],
        out_specs=(hbm, vmem),
        scratch_shapes=[pltpu.SemaphoreType.DMA((4, GX))],
        compiler_params=pltpu.CompilerParams(vmem_limit_bytes=4 * 1024 * 1024),
    )(staged, currents_next)
    return field_next, currents_next.T[None]


def solution(mesh):
    placed = (
        P("gx", "gy", None),
        P("gx", "gy", None),
        P(("gx", "gy"), None, None),
        P(("gx", "gy"), None),
        P(("gx", "gy"), None, None),
        P(("gx", "gy"), None, None),
    )
    return jax.shard_map(
        local,
        mesh=mesh,
        in_specs=placed,
        out_specs=(P("gx", "gy", None), P(("gx", "gy"), None, None)),
        check_vma=False,
    )
```

```python
import functools

import jax
import jax.numpy as jnp
from jax import lax
from jax.experimental import pallas as pl
from jax.experimental.pallas import tpu as pltpu
from jax.sharding import PartitionSpec as P

MESH = pl.DeviceIdType.MESH
F32 = jnp.float32
BF16 = jnp.bfloat16

CX, CY, NZ, CAP = 16, 128, 512, 4
GX, GY = 16, 8
WIRE = 512
KX = 8.0 * CX * CX
KY = 8.0 * CY * CY
INJECT = 4.0 * KY**0.5
PLANE = CY * CX
UNITS = 8
EARLY = 2
AHEAD = 5


def inverse(value):
    return pl.reciprocal(value, approx=True)


def split3(value):
    high = value.astype(BF16).astype(F32)
    rest = value - high
    middle = rest.astype(BF16).astype(F32)
    return high, middle, rest - middle


def kernel(
    field,
    conduct,
    cell_h,
    count_h,
    cur_h,
    coupling,
    ht,
    my,
    ay,
    ends,
    cur_out,
    fb,
    cb,
    mx,
    ax,
    xs,
    xr,
    vs,
    vr,
    cw,
    hot,
    bhl,
    samp,
    zcol,
    cell_v,
    count_v,
    cur_v,
    rows_v,
    rows_s,
    rows_n,
    rows_t,
    samp3,
    pas,
    par,
    lines,
    acc,
    tmat,
    cw2,
    wv,
    wp,
    samp2,
    pks,
    pkr,
    zhot,
    xmask,
    gbt,
    yk,
    added0,
    added1,
    p1s,
    p1r,
    p2s,
    p2r,
    ys,
    ga,
    gat,
    gb,
    ycs,
    ycr,
    yrs,
    yrr,
    yvs,
    yvr,
    fsem,
    csem,
    wsem,
    xsem,
    vsem,
    s1,
    s2,
    sa,
    sb,
    syc,
    syr,
    syv,
    spk,
    spa,
    small,
    rsem,
):
    me_x = lax.axis_index("gx")
    me_y = lax.axis_index("gy")

    def peer_x(step):
        return lax.rem(me_x + step, GX)

    def peer_y(step):
        return lax.rem(me_y + step, GY)

    def each(count, body, start=1):
        def run(t, carry):
            body(t)
            return carry

        lax.fori_loop(start, count, run, 0)

    def chunk(d):
        return pl.ds(pl.multiple_of(d * 8, 8), 8)

    def quarter(q):
        return slice(128 * q, 128 * q + 128)

    def in_copies(d):
        copies = []
        for q in range(4):
            for src, dst, sem in ((conduct, cb, csem), (field, fb, fsem)):
                copies.append(
                    pltpu.make_async_copy(src.at[:, chunk(d), quarter(q)], dst.at[q, d], sem.at[d, q])
                )
        return copies

    def load4(ref, d, x):
        return jnp.concatenate([ref[q, d, x] for q in range(4)], axis=1)

    def order(t):
        u = 15 - t
        return lax.rem(me_x // 4 + u // 4, 4) * 4 + lax.rem(me_x + lax.rem(u, 4), 4)

    def start_in(t, carry):
        for copy in in_copies(order(t)):
            copy.start()
        return carry

    barrier = pltpu.get_barrier_semaphore()

    def greet_x(t, carry):
        pl.semaphore_signal(barrier, inc=1, device_id=(peer_x(t), me_y), device_id_type=MESH)
        return carry

    def greet_y(t, carry):
        pl.semaphore_signal(barrier, inc=1, device_id=(me_x, peer_y(t)), device_id_type=MESH)
        return carry

    lax.fori_loop(1, GX, greet_x, 0)
    lax.fori_loop(1, GY, greet_y, 0)
    lax.fori_loop(0, GX, start_in, 0)
    weights = pltpu.make_async_copy(coupling, cw, wsem)
    weights.start()
    smalls = [
        pltpu.make_async_copy(src, dst, small.at[i])
        for i, (src, dst) in enumerate(((cell_h, cell_v), (count_h, count_v), (cur_h, cur_v)))
    ]
    for copy in smalls:
        copy.start()

    def copy_x(src, dst, sems, slot, to, who):
        return pltpu.make_async_remote_copy(
            src_ref=src, dst_ref=dst, send_sem=sems.at[0, slot], recv_sem=sems.at[1, who],
            device_id=(to, me_y), device_id_type=MESH,
        )

    def copy_y(src, dst, sems, slot, to, who):
        return pltpu.make_async_remote_copy(
            src_ref=src, dst_ref=dst, send_sem=sems.at[0, slot], recv_sem=sems.at[1, who],
            device_id=(me_x, to), device_id_type=MESH,
        )

    lane_z = lax.broadcasted_iota(jnp.int32, (8, NZ), 1)
    scale_f = 1.0 / (KX * KY)

    def eliminate(ds):
        for d in ds:
            for copy in in_copies(d):
                copy.wait()

        def ground(d, x):
            return (1.0 / KX) + (0.5 / KX) * load4(cb, d, x)

        def source(d, x):
            value = load4(fb, d, x)
            up = jnp.where(lane_z == NZ - 1, 0.0, pltpu.roll(value, NZ - 1, 1))
            down = jnp.where(lane_z == 0, 0.0, pltpu.roll(value, 1, 1))
            return (0.5 * scale_f) * value + (0.25 * scale_f) * (up + down)

        blank4 = jnp.zeros((8, NZ), F32)
        states = [(jnp.ones((8, NZ), F32), ground(d, 0), source(d, 0), blank4, blank4) for d in ds]
        for x in range(CX - 1):
            for n, d in enumerate(ds):
                a, g, f, gp, fp = states[n]
                m = inverse(a + g + 1.0)
                am = a * m
                b = f * m
                gp = gp + am * g
                fp = fp + am * f
                f = source(d, x + 1) + b
                for q in range(4):
                    mx[q, d, x] = m[:, quarter(q)]
                    ax[q, d, x] = am[:, quarter(q)]
                    fb[q, d, x] = b[:, quarter(q)]
                states[n] = (am, ground(d, x + 1) + g * m, f, gp, fp)
        for n, d in enumerate(ds):
            for slot, value in enumerate(states[n]):
                for q in range(4):
                    xs[q, d, slot] = value[:, quarter(q)]

    def send_x(q, d):
        copy_x(xs.at[q, d], xr.at[q, me_x], xsem.at[q], d, d, me_x).start()

    def eliminate_and_send(t):
        d = order(t)
        eliminate([d])

        @pl.when(t < GX - 1)
        def _():
            send_x(0, d)

    each(EARLY, lambda t: eliminate([order(t)]), 0)
    pl.semaphore_wait(barrier, GX - 1 + GY - 1)
    each(EARLY, lambda t: send_x(0, order(t)), 0)
    each(GX, eliminate_and_send, EARLY)
    each(GX - 1, lambda t: send_x(1, order(t)), 0)
    each(AHEAD, lambda t: send_x(2, order(t)), 0)
    for q in range(4):
        xr[q, me_x] = xs[q, me_x]

    def respond(d):
        own = jnp.zeros((8, NZ), F32)
        west = jnp.zeros((8, NZ), F32)
        last = jnp.ones((8, NZ), F32)
        for x in range(CX - 1, -1, -1):
            if x < CX - 1:
                m = load4(mx, d, x)
                own = load4(fb, d, x) + m * own
                west = load4(ax, d, x) + m * west
                last = m * last
            for q in range(4):
                fb[q, d, x] = own[:, quarter(q)]
                ax[q, d, x] = west[:, quarter(q)]
                mx[q, d, x] = last[:, quarter(q)]

    each(GX, respond, 0)

    for copy in smalls:
        copy.wait()
    cells = cell_v[...]
    slot_of = lax.broadcasted_iota(jnp.int32, (CAP, 128), 0)
    filled = slot_of < count_v[...]
    at_x = cells >> 16
    place_z = jnp.where(filled, cells & (NZ - 1), -1)
    place_r = ((cells >> 9) & (CY - 1)) * CX + at_x
    rows_v[...] = ((cells >> 7) & 3) * PLANE + (at_x >> 3) * (8 * CY) + ((cells >> 9) & (CY - 1)) * 8 + (at_x & 7)
    rows_n[...] = ((cells >> 7) & 3) * PLANE + ((cells >> 12) & 15) * 128 + at_x * 8 + ((cells >> 9) & 7)
    rows_copies = [
        pltpu.make_async_copy(rows_n, rows_t, rsem.at[0]),
        pltpu.make_async_copy(rows_v, rows_s, rsem.at[1]),
    ]
    for copy in rows_copies:
        copy.start()
    zcol[...] = jnp.concatenate([place_z, jnp.full((128 - CAP, 128), -1, jnp.int32)], axis=0).T
    lanes = lax.broadcasted_iota(jnp.int32, (128, 128), 1)

    def hit_of(k):
        z = zcol[:, k : k + 1]
        return ((z & 127) == lanes) & (z >= 0)

    def pick(table, pairs):
        def run(n):
            for i in range(16):
                o = n * 16 + i
                for k in range(CAP):
                    row = table[k, o]
                    for src, dst in pairs:
                        dst[pl.ds(k * 128 + o, 1), :] = src[pl.ds(row, 1), :]

        each(128 // 16, run, 0)

    rows_copies[0].wait()
    pick(rows_t, [(ref.reshape(4 * PLANE, 128), dst) for ref, dst in ((fb, samp), (ax, samp2), (mx, samp3))])
    for k in range(CAP):
        hit = hit_of(k)
        rows = slice(128 * k, 128 * k + 128)
        for slot, ref in enumerate((samp, samp2, samp3)):
            chosen = jnp.where(hit, ref[rows, :], 0.0) * KY
            pas[slot * CAP + k : slot * CAP + k + 1, :] = jnp.sum(chosen.T, axis=0, keepdims=True)
    key = ((cells >> 12) & 15) * 32 + ((cells >> 7) & 3) * 8 + ((cells >> 9) & 7)
    pas[3 * CAP : 4 * CAP, :] = (key * 128 + (cells & 127)).astype(F32)

    def send_pa(t):
        to = order(t)
        copy_x(pas, par.at[me_x], spa, to, to, me_x).start()

    each(GX - 1, send_pa, 0)
    par[me_x] = pas[...]
    each(GX - 1, lambda t: send_x(2, order(t)), AHEAD)
    each(GX - 1, lambda t: send_x(3, order(t)), 0)

    cb2 = cb.reshape(4 * PLANE, 128)

    def spread_rows(y, u):
        return pl.ds((u // 2) * PLANE + (y // 8) * (8 * CX) + (u % 2) * 64 + lax.rem(y, 8), 8, stride=8)

    def ground_y(y):
        return [(1.0 / KY) + (0.5 / KY) * cb2[spread_rows(y, u), :] for u in range(UNITS)]

    def at_y(y, u):
        return pl.ds(pl.multiple_of(u * (8 * CY) + y * 8, 8), 8)

    def factor(y, state):
        a, g, gp = state
        after = ground_y(y + 1)
        a_new, g_new, gp_new = [], [], []
        for u in range(UNITS):
            m = inverse(a[u] + g[u] + 1.0)
            am = a[u] * m
            my[at_y(y, u), :] = m
            ay[at_y(y, u), :] = am
            gp_new.append(gp[u] + am * g[u])
            g_new.append(after[u] + g[u] * m)
            a_new.append(am)
        return a_new, g_new, gp_new

    ones = [jnp.ones((8, 128), F32) for _ in range(UNITS)]
    zeros = [jnp.zeros((8, 128), F32) for _ in range(UNITS)]
    a_y, g_y, gp_y = lax.fori_loop(0, CY - 1, factor, (ones, ground_y(0), zeros))
    for u in range(UNITS):
        for slot, value in enumerate((a_y, g_y, gp_y)):
            ycs[u, slot] = value[u]

    for u in range(UNITS):
        my[at_y(CY - 1, u), :] = jnp.ones((8, 128), F32)
        ay[at_y(CY - 1, u), :] = jnp.zeros((8, 128), F32)
        wv[at_y(CY - 1, u), :] = jnp.ones((8, 128), F32)
        wp[at_y(CY - 1, u), :] = jnp.zeros((8, 128), F32)

    def send_yc(t):
        to = peer_y(t)
        copy_y(ycs.at[to], ycr.at[me_y], syc, to, to, me_y).start()

    each(GY, send_yc)
    ycr[me_y] = ycs[me_y]

    def weigh(n, state):
        y = CY - 2 - n
        to_last, to_west = state
        last_new, west_new = [], []
        for u in range(UNITS):
            m = my[at_y(y, u), :]
            last_new.append(m * to_last[u])
            west_new.append(ay[at_y(y, u), :] + m * to_west[u])
            wv[at_y(y, u), :] = last_new[u]
            wp[at_y(y, u), :] = west_new[u]
        return last_new, west_new

    lax.fori_loop(0, CY - 1, weigh, (ones, zeros))

    rows_copies[1].wait()
    pick(rows_s, [(wv, samp), (wp, samp2)])
    for k in range(CAP):
        hit = hit_of(k)
        rows = slice(128 * k, 128 * k + 128)
        for slot, ref in enumerate((samp, samp2)):
            chosen = jnp.where(hit, ref[rows, :], 0.0) * (INJECT / KY)
            pks[slot * CAP + k : slot * CAP + k + 1, :] = jnp.sum(chosen.T, axis=0, keepdims=True)
    pks[2 * CAP : 3 * CAP, :] = at_x.astype(F32)
    pks[3 * CAP : 4 * CAP, :] = place_z.astype(F32)

    def send_pk(t):
        to = peer_y(t)
        copy_y(pks, pkr.at[me_y], spk, to, to, me_y).start()

    each(GY, send_pk)
    pkr[me_y] = pks[...]

    blank = jnp.zeros((8, 128), F32)

    def reduce_x(q):
        def arrive(t):
            frm = peer_x(t)
            copy_x(xs.at[q, frm], xr.at[q, frm], xsem.at[q], frm, frm, frm).wait_recv()

        each(GX, arrive)
        q_x = xr[q, 0, 0] + xr[q, 0, 1] + xr[q, 1, 3]
        phi = xr[q, 0, 2] + xr[q, 1, 4]
        kept = [None]
        for r in range(1, GX):
            a = xr[q, r, 0]
            m = inverse(a + q_x)
            am = a * m
            kept.append((am, m * phi))
            more_g, more_f = (xr[q, r + 1, 3], xr[q, r + 1, 4]) if r < GX - 1 else (1.0, 0.0)
            q_x = xr[q, r, 1] + more_g + am * q_x
            phi = xr[q, r, 2] + more_f + am * phi
        value = phi * inverse(q_x)
        for r in range(GX - 1, 0, -1):
            vs[q, r, 1] = value
            value = kept[r][1] + kept[r][0] * value
            vs[q, r, 0] = value
        vs[q, 0, 1] = value
        vs[q, 0, 0] = blank

    def send_back(q):
        def send(t):
            to = peer_x(t)
            copy_x(vs.at[q, to], vr.at[q, me_x], vsem.at[q], to, to, me_x).start()

        each(GX, send)
        vr[q, me_x] = vs[q, me_x]

    row_8 = lax.broadcasted_iota(jnp.int32, (8, 128), 0)
    row_128 = lax.broadcasted_iota(jnp.int32, (128, 128), 0)

    def build_lines(r):
        code = par[r, 3 * CAP : 4 * CAP, :].astype(jnp.int32)
        for k in range(CAP):
            match = jnp.where(row_128 == (code[k : k + 1, :] & 127), 1.0, 0.0)
            lines[r, :, quarter(k)] = match.astype(BF16)

    def gather_x(quarters, first):
        def one(r):
            info = par[r]
            code = info[3 * CAP : 4 * CAP, :].astype(jnp.int32)
            parts = []
            for q in quarters:
                value = vs[q, r].reshape(16, 128)
                high = value.astype(BF16).astype(F32)
                parts.extend((high, value - high))
            product = jnp.dot(jnp.concatenate(parts, axis=0).astype(BF16), lines[r], preferred_element_type=F32)
            for k in range(CAP):
                total = jnp.zeros((8, 128), F32) if first else acc[r, :, quarter(k)]
                for n, q in enumerate(quarters):
                    solved = product[32 * n : 32 * n + 16, quarter(k)] + product[32 * n + 16 : 32 * n + 32, quarter(k)]
                    match = (code[k : k + 1, :] >> 7) == me_x * 32 + q * 8 + row_8
                    value = (
                        info[k : k + 1, :]
                        + info[CAP + k : CAP + k + 1, :] * solved[0:8]
                        + info[2 * CAP + k : 2 * CAP + k + 1, :] * solved[8:16]
                    )
                    total = total + jnp.where(match, value, 0.0)
                acc[r, :, quarter(k)] = total

        def four(n):
            for i in range(4):
                one(n * 4 + i)

        each(4, four, 0)

    reduce_x(0)
    reduce_x(1)

    def arrive_pa(t):
        frm = peer_x(t)
        copy_x(pas, par.at[frm], spa, frm, frm, frm).wait_recv()

    each(GX, arrive_pa)
    each(GX, build_lines, 0)
    reduce_x(2)
    gather_x((0, 1, 2), True)
    reduce_x(3)
    gather_x((3,), False)

    tmat[...] = jnp.zeros_like(tmat)
    p2s[...] = jnp.zeros_like(p2s)
    ys[...] = jnp.zeros_like(ys)
    mine = lax.rem(me_x, 4) * 32 + me_y * CAP
    for r in range(GX):
        total = jnp.sum(acc[r], axis=0, keepdims=True)
        for k in range(CAP):
            tmat[pl.ds(lax.rem(me_y, 2) * 64 + CAP * r + k, 1), :] = total[:, quarter(k)]
    p1s[...] = tmat[...].T.reshape(GX, GY, 128)

    def send_1(t):
        to = peer_x(t)
        copy_x(p1s.at[to], p1r.at[me_x], s1, to, to, me_x).start()

    def arrive_1(t):
        frm = peer_x(t)
        copy_x(p1s.at[frm], p1r.at[frm], s1, frm, frm, frm).wait_recv()

    each(GX, send_1)
    p1r[me_x] = p1s[me_x]
    for q in range(4):
        send_back(q)

    row_m = lax.broadcasted_iota(jnp.int32, (128, WIRE), 0)
    lane_m = lax.broadcasted_iota(jnp.int32, (128, WIRE), 1)
    spread = [jnp.where(lane_m == row_m * CAP + k, 1.0, 0.0).astype(BF16) for k in range(CAP)]

    def three_rows(row):
        high, middle, low = split3(row)
        index = lax.broadcasted_iota(jnp.int32, (16, row.shape[1]), 0)
        stack = jnp.where(index == 0, high, jnp.where(index == 1, middle, jnp.where(index == 2, low, 0.0)))
        return stack.astype(BF16)

    def exact_dot(row, matrix, dims):
        product = lax.dot_general(three_rows(row), matrix, (dims, ((), ())), preferred_element_type=F32)
        return (product[2:3] + product[1:2]) + product[0:1]

    cur_row = jnp.zeros((1, WIRE), F32)
    for k in range(CAP):
        cur_row = cur_row + exact_dot(cur_v[k : k + 1, :], spread[k], ((1,), (0,)))
    lane_n = lax.broadcasted_iota(jnp.int32, (WIRE, WIRE), 1)
    source_n = ((lane_n >> 2) & 15) * 32 + (lane_n >> 6) * CAP + (lane_n & 3)
    shuffle = jnp.where(lax.broadcasted_iota(jnp.int32, (WIRE, WIRE), 0) == source_n, 1.0, 0.0).astype(BF16)
    weights.wait()
    cw2[...] = jnp.dot(cw[...], shuffle, preferred_element_type=F32).astype(BF16)

    def substitute(q):
        def arrive(t):
            frm = peer_x(t)
            copy_x(vs.at[q, frm], vr.at[q, frm], vsem.at[q], frm, frm, frm).wait_recv()

        def group(n):
            ds = [n * 4 + i for i in range(4)]
            west = [vr[q, d, 0] for d in ds]
            last = [vr[q, d, 1] for d in ds]
            for x in range(CX):
                value = [
                    (fb[q, d, x] + ax[q, d, x] * west[i]) + mx[q, d, x] * last[i] for i, d in enumerate(ds)
                ]
                for i, d in enumerate(ds):
                    ht[pl.ds((2 * q + x // 8) * (8 * CY) + d * 64 + x % 8, 8, stride=8), :] = value[i]

        each(GX, arrive)
        each(4, group, 0)

    each(GX, arrive_1)
    total = p1r[0]
    for i in range(1, GX):
        total = total + p1r[i]
    for j in range(GY):
        p2s[j, 0:1, :] = total[j : j + 1, :]

    def send_2(t):
        to = peer_y(t)
        copy_y(p2s.at[to], p2r.at[me_y], s2, to, to, me_y).start()

    def arrive_2(t):
        frm = peer_y(t)
        copy_y(p2s.at[frm], p2r.at[frm], s2, frm, frm, frm).wait_recv()

    each(GY, send_2)
    p2r[me_y] = p2s[me_y]
    def tree(terms):
        while len(terms) > 1:
            terms = [a + b for a, b in zip(terms[::2], terms[1::2])]
        return terms[0]

    def sum_up(q):
        def rows(n, state):
            new = []
            for i, u in enumerate((2 * q, 2 * q + 1)):
                values = [ht[at_y(n * 8 + step, u), :] for step in range(8)]
                for slot, ref in enumerate((wv, wp)):
                    terms = [value * ref[at_y(n * 8 + step, u), :] for step, value in enumerate(values)]
                    new.append(state[2 * i + slot] + tree(terms))
            return new

        sums = lax.fori_loop(0, CY // 8, rows, zeros[:4])
        for i, u in enumerate((2 * q, 2 * q + 1)):
            yrs[u, 0] = sums[2 * i]
            yrs[u, 1] = sums[2 * i + 1]

    substitute(0)
    sum_up(0)
    substitute(1)
    sum_up(1)
    each(GY, arrive_2)
    row = jnp.concatenate([p2r[2 * j, 0:1, :] + p2r[2 * j + 1, 0:1, :] for j in range(4)], axis=1)
    new_row = 0.5 * cur_row + exact_dot(row, cw2[...], ((1,), (1,)))
    for a in range(4):
        ys[a : a + 1, :] = new_row[:, 128 * a : 128 * a + 128]

    def send_a(t):
        to = peer_y(t)
        copy_y(ys, ga.at[me_y], sa, to, to, me_y).start()

    def arrive_a(t):
        frm = peer_y(t)
        copy_y(ys, ga.at[frm], sa, frm, frm, frm).wait_recv()

    each(GY, send_a)
    ga[me_y] = ys[...]
    for k in range(CAP):
        cur_out[k : k + 1, :] = exact_dot(new_row, spread[k], ((1,), (1,)))
    substitute(2)
    sum_up(2)
    substitute(3)
    sum_up(3)
    def send_yr(t):
        to = peer_y(t)
        copy_y(yrs.at[to], yrr.at[me_y], syr, to, to, me_y).start()

    each(GY, send_yr)
    yrr[me_y] = yrs[me_y]
    each(GY, arrive_a)
    for j in range(GY):
        part = ga[j]
        for a in range(4):
            gat[a, j : j + 1, :] = part[a : a + 1, :]

    def send_b(t):
        to = peer_x(t)
        copy_x(gat.at[to // 4], gb.at[me_x], sb, to, to, me_x).start()

    def arrive_b(t):
        frm = peer_x(t)
        copy_x(gat.at[0], gb.at[frm], sb, frm, frm, frm).wait_recv()

    each(GX, send_b)
    gb[me_x] = gat[me_x // 4]
    def drain_x(t):
        to = peer_x(t)
        for q in range(4):
            copy_x(xs.at[q, to], xr.at[q, me_x], xsem.at[q], to, to, me_x).wait_send()
            copy_x(vs.at[q, to], vr.at[q, me_x], vsem.at[q], to, to, me_x).wait_send()
        copy_x(p1s.at[to], p1r.at[me_x], s1, to, to, me_x).wait_send()
        copy_x(pas, par.at[me_x], spa, to, to, me_x).wait_send()

    def drain_y(t):
        to = peer_y(t)
        copy_y(p2s.at[to], p2r.at[me_y], s2, to, to, me_y).wait_send()
        copy_y(ycs.at[to], ycr.at[me_y], syc, to, to, me_y).wait_send()
        copy_y(yrs.at[to], yrr.at[me_y], syr, to, to, me_y).wait_send()
        copy_y(pks, pkr.at[me_y], spk, to, to, me_y).wait_send()

    def arrive_pk(t):
        frm = peer_y(t)
        copy_y(pks, pkr.at[frm], spk, frm, frm, frm).wait_recv()

    def arrive_yc(t):
        frm = peer_y(t)
        copy_y(ycs.at[frm], ycr.at[frm], syc, frm, frm, frm).wait_recv()

    each(GY, arrive_pk)
    each(GY, arrive_yc)
    share_z = ((me_y // 2) * 128 + lax.broadcasted_iota(jnp.int32, (128, 128), 0)).astype(F32)
    share_x = (lax.rem(me_y, 2) * 8 + lax.broadcasted_iota(jnp.int32, (8, 128), 0)).astype(F32)

    def build_share(r):
        info = pkr[r]
        for k in range(CAP):
            zhot[r, :, 128 * k : 128 * k + 128] = jnp.where(share_z == info[12 + k : 13 + k, :], 1.0, 0.0).astype(BF16)
            match = share_x == info[8 + k : 9 + k, :]
            for slot in range(2):
                weight = info[4 * slot + k : 4 * slot + k + 1, :]
                xmask[r, slot, :, 128 * k : 128 * k + 128] = jnp.where(match, weight, 0.0)

    each(GY, build_share, 0)
    q_y = ycr[0, 0] + ycr[0, 1] + ycr[1, 2]
    for r in range(1, GY):
        a = ycr[r, 0]
        m = inverse(a + q_y)
        yk[r, 0] = a * m
        yk[r, 1] = m
        more = ycr[r + 1, 2] if r < GY - 1 else 1.0
        q_y = ycr[r, 1] + more + a * m * q_y
    yk[0, 0] = inverse(q_y)
    row_16 = lax.broadcasted_iota(jnp.int32, (CX, 128), 0)

    def build_hot(y):
        rows = row_16 + y * CX
        for k in range(CAP):
            match = jnp.where(rows == place_r[k : k + 1, :], 1.0, 0.0)
            hot[pl.ds(pl.multiple_of(y * CX, CX), CX), quarter(k)] = match.astype(BF16)

    def build_some(n):
        for step in range(8):
            build_hot(n * 8 + step)

    each(CY // 8, build_some, 0)
    each(GX, drain_x)
    each(GY, drain_y)
    each(GX, arrive_b)

    back = gb[...].reshape(128, 128)
    gbt[...] = back.T
    mine_rows = gbt[pl.ds(pl.multiple_of(lax.rem(me_x, 4) * 32, 32), 32), :]
    extra = []
    for r in range(GY):
        values = jnp.concatenate([mine_rows[CAP * r + k : CAP * r + k + 1, :] for k in range(CAP)], axis=1)
        parts = jnp.concatenate([xmask[r, 0] * values, xmask[r, 1] * values], axis=0)
        high = parts.astype(BF16)
        low = (parts - high.astype(F32)).astype(BF16)
        product = lax.dot_general(
            jnp.concatenate([high, low], axis=0), zhot[r], (((1,), (1,)), ((), ())), preferred_element_type=F32
        )
        extra.append((product[0:8] + product[16:24], product[8:16] + product[24:32]))

    def arrive_yr(t):
        frm = peer_y(t)
        copy_y(yrs.at[frm], yrr.at[frm], syr, frm, frm, frm).wait_recv()

    each(GY, arrive_yr)
    phi = (yrr[0, 0] + extra[0][0]) + (yrr[1, 1] + extra[1][1])
    phis = [phi]
    for r in range(1, GY):
        phi = (yrr[r, 0] + extra[r][0]) + yk[r, 0] * phi
        if r < GY - 1:
            phi = phi + (yrr[r + 1, 1] + extra[r + 1][1])
        phis.append(phi)
    value = phi * yk[0, 0]
    for r in range(GY - 1, 0, -1):
        yvs[r, 1] = value
        value = yk[r, 1] * phis[r - 1] + yk[r, 0] * value
        yvs[r, 0] = value
    yvs[0, 1] = value
    yvs[0, 0] = jnp.zeros((8, 128), F32)

    def send_yv(t):
        to = peer_y(t)
        copy_y(yvs.at[to], yvr.at[me_y], syv, to, to, me_y).start()

    def arrive_yv(t):
        frm = peer_y(t)
        copy_y(yvs.at[frm], yvr.at[frm], syv, frm, frm, frm).wait_recv()

    each(GY, send_yv)
    yvr[me_y] = yvs[me_y]

    lane_k = lax.broadcasted_iota(jnp.int32, (128, NZ), 1)
    for k in range(CAP):
        value = jnp.sum(jnp.where(lanes == mine + k, back, 0.0), axis=1, keepdims=True) * (INJECT / KY)
        spot = jnp.where(lane_k == zcol[:, k : k + 1], value, 0.0)
        high = spot.astype(BF16)
        bhl[128 * k : 128 * k + 128, :] = high
        bhl[WIRE + 128 * k : WIRE + 128 * k + 128, :] = (spot - high.astype(F32)).astype(BF16)

    def scatter(n, added):
        part = hot[pl.ds(pl.multiple_of(n * 256, 256), 256), :]
        added[...] = jnp.dot(jnp.concatenate([part, part], axis=1), bhl[...], preferred_element_type=F32)

    def eliminate_y(n, added, state):
        for step in range(16):
            y = n * 16 + step
            new = []
            for u in range(UNITS):
                row = step * CX + (u % 2) * 8
                more = added[row : row + 8, quarter(u // 2)]
                b = ((ht[at_y(y, u), :] + more) + state[u]) * my[at_y(y, u), :]
                ht[at_y(y, u), :] = b
                new.append(b)
            state = new
        return state

    def forward_y(n, state):
        scatter(2 * n + 1, added1)
        state = eliminate_y(2 * n, added0, state)
        scatter(jnp.minimum(2 * n + 2, CY // 16 - 1), added0)
        return eliminate_y(2 * n + 1, added1, state)

    scatter(0, added0)
    lax.fori_loop(0, CY // 32, forward_y, zeros)
    each(GY, arrive_yv)

    ends[...] = yvr[...]

    def drain_late_x(t):
        copy_x(gat.at[0], gb.at[me_x], sb, peer_x(t), peer_x(t), me_x).wait_send()

    def drain_late_y(t):
        to = peer_y(t)
        copy_y(ys, ga.at[me_y], sa, to, to, me_y).wait_send()
        copy_y(yvs.at[to], yvr.at[me_y], syv, to, to, me_y).wait_send()

    each(GX, drain_late_x)
    each(GY, drain_late_y)


def deliver(ht, my, ay, ends, cur_in, out, cur_out, staged, sems):
    rows = staged.reshape(4 * PLANE, 128)
    west = [ends[u, 0] for u in range(UNITS)]
    last = [ends[u, 1] for u in range(UNITS)]

    def copies(c):
        place = pl.ds(pl.multiple_of(c * 8, 8), 8)
        return [
            pltpu.make_async_copy(staged.at[q, c], out.at[:, place, 128 * q : 128 * q + 128], sems.at[q, c])
            for q in range(4)
        ]

    def put(y, value):
        for u in range(UNITS):
            start = (u // 2) * PLANE + (y // 8) * (8 * CX) + (u % 2) * 64 + lax.rem(y, 8)
            rows[pl.ds(start, 8, stride=8), :] = value[u]

    def step(y, value):
        new = []
        for u in range(UNITS):
            at = pl.ds(pl.multiple_of(u * (8 * CY) + y * 8, 8), 8)
            new.append((ht[at, :] + ay[at, :] * west[u]) + my[at, :] * value[u])
        put(y, new)
        return new

    def send(c):
        for copy in copies(c):
            copy.start()

    def chunk(n, value):
        c = CY // 8 - 1 - n
        for back in range(8):
            value = step(c * 8 + 7 - back, value)
        send(c)
        return value

    put(CY - 1, last)
    value = last
    for back in range(1, 8):
        value = step(CY - 1 - back, value)
    send(CY // 8 - 1)
    lax.fori_loop(1, CY // 8, chunk, value)
    cur_out[...] = cur_in[...]

    def wait(c, carry):
        for copy in copies(c):
            copy.wait()
        return carry

    lax.fori_loop(0, CY // 8, wait, 0)


def local(field, conduct, seg_cell, seg_count, currents, coupling):
    hbm = pl.BlockSpec(memory_space=pltpu.HBM)
    vmem = pl.BlockSpec(memory_space=pltpu.VMEM)
    cells = seg_cell[0].T
    block = lambda *shape: pltpu.VMEM(shape, F32)
    sems = lambda count: pltpu.SemaphoreType.DMA((2, count))
    scratch = [
        block(4, GX, CX, 8, 128),
        block(4, GX, CX, 8, 128),
        block(4, GX, CX, 8, 128),
        block(4, GX, CX, 8, 128),
        block(4, GX, 5, 8, 128),
        block(4, GX, 5, 8, 128),
        block(4, GX, 2, 8, 128),
        block(4, GX, 2, 8, 128),
        pltpu.VMEM((WIRE, WIRE), BF16),
        pltpu.VMEM((PLANE, WIRE), BF16),
        pltpu.VMEM((2 * WIRE, NZ), BF16),
        block(WIRE, 128),
        pltpu.VMEM((128, 128), jnp.int32),
        pltpu.VMEM((CAP, 128), jnp.int32),
        pltpu.VMEM((1, 128), jnp.int32),
        block(CAP, 128),
        pltpu.VMEM((CAP, 128), jnp.int32),
        pltpu.SMEM((CAP, 128), jnp.int32),
        pltpu.VMEM((CAP, 128), jnp.int32),
        pltpu.SMEM((CAP, 128), jnp.int32),
        block(WIRE, 128),
        block(16, 128),
        block(GX, 16, 128),
        pltpu.VMEM((GX, 128, WIRE), BF16),
        block(GX, 8, WIRE),
        block(128, 128),
        pltpu.VMEM((WIRE, WIRE), BF16),
        block(4 * PLANE, 128),
        block(4 * PLANE, 128),
        block(WIRE, 128),
        block(16, 128),
        block(GY, 16, 128),
        pltpu.VMEM((GY, 128, WIRE), BF16),
        block(GY, 2, 8, WIRE),
        block(128, 128),
        block(GY, 2, 8, 128),
        block(256, NZ),
        block(256, NZ),
        block(GX, 8, 128),
        block(GX, 8, 128),
        block(GY, 8, 128),
        block(GY, 8, 128),
        block(8, 128),
        block(GY, 8, 128),
        block(4, 8, 128),
        block(GX, 8, 128),
        block(GY, 3, 8, 128),
        block(GY, 3, 8, 128),
        block(GY, 2, 8, 128),
        block(GY, 2, 8, 128),
        block(GY, 2, 8, 128),
        block(GY, 2, 8, 128),
        pltpu.SemaphoreType.DMA((GX, 4)),
        pltpu.SemaphoreType.DMA((GX, 4)),
        pltpu.SemaphoreType.DMA,
        pltpu.SemaphoreType.DMA((4, 2, GX)),
        pltpu.SemaphoreType.DMA((4, 2, GX)),
        sems(GX),
        sems(GY),
        sems(GY),
        sems(GX),
        sems(GY),
        sems(GY),
        sems(GY),
        sems(GY),
        sems(GX),
        pltpu.SemaphoreType.DMA((3,)),
        pltpu.SemaphoreType.DMA((2,)),
    ]
    rows = pltpu.VMEM((4 * PLANE, 128), F32)
    *parts, currents_next = pl.pallas_call(
        kernel,
        out_shape=(rows, rows, rows, pltpu.VMEM((GY, 2, 8, 128), F32), pltpu.VMEM((CAP, 128), F32)),
        in_specs=[hbm] * 6,
        out_specs=(vmem,) * 5,
        scratch_shapes=scratch,
        compiler_params=pltpu.CompilerParams(
            collective_id=0, has_side_effects=True, vmem_limit_bytes=49 * 1024 * 1024
        ),
    )(field, conduct, cells, seg_count, currents[0].T, coupling[0])
    field_next, currents_next = pl.pallas_call(
        deliver,
        out_shape=(
            jax.ShapeDtypeStruct((CX, CY, NZ), F32),
            jax.ShapeDtypeStruct((CAP, 128), F32),
        ),
        in_specs=[vmem] * 5,
        out_specs=(hbm, vmem),
        scratch_shapes=[block(4, GX, CX, 8, 128), pltpu.SemaphoreType.DMA((4, GX))],
        compiler_params=pltpu.CompilerParams(vmem_limit_bytes=6 * 1024 * 1024),
    )(*parts, currents_next)
    return field_next, currents_next.T[None]


def solution(mesh):
    placed = (
        P("gx", "gy", None),
        P("gx", "gy", None),
        P(("gx", "gy"), None, None),
        P(("gx", "gy"), None),
        P(("gx", "gy"), None, None),
        P(("gx", "gy"), None, None),
    )
    return jax.shard_map(
        local,
        mesh=mesh,
        in_specs=placed,
        out_specs=(P("gx", "gy", None), P(("gx", "gy"), None, None)),
        check_vma=False,
    )
```

```python
import functools

import jax
import jax.numpy as jnp
from jax import lax
from jax.experimental import pallas as pl
from jax.experimental.pallas import tpu as pltpu
from jax.sharding import PartitionSpec as P

MESH = pl.DeviceIdType.MESH
F32 = jnp.float32
BF16 = jnp.bfloat16

CX, CY, NZ, CAP = 16, 128, 512, 4
GX, GY = 16, 8
WIRE = 512
KX = 8.0 * CX * CX
KY = 8.0 * CY * CY
INJECT = 4.0 * KY**0.5
PLANE = CY * CX
UNITS = 8
EARLY = 2
AHEAD = 5


def inverse(value):
    return pl.reciprocal(value, approx=True)


def split3(value):
    high = value.astype(BF16).astype(F32)
    rest = value - high
    middle = rest.astype(BF16).astype(F32)
    return high, middle, rest - middle


def kernel(
    field,
    conduct,
    cell_h,
    count_h,
    cur_h,
    coupling,
    ht,
    my,
    ay,
    ends,
    cur_out,
    fb,
    cb,
    mx,
    ax,
    xs,
    xr,
    vs,
    vr,
    cw,
    hot,
    bhl,
    samp,
    zcol,
    cell_v,
    count_v,
    cur_v,
    rows_v,
    rows_s,
    rows_n,
    rows_t,
    samp3,
    pas,
    par,
    lines,
    acc,
    tmat,
    cw2,
    wv,
    wp,
    samp2,
    pks,
    pkr,
    zhot,
    xmask,
    gbt,
    yk,
    added0,
    added1,
    p1s,
    p1r,
    p2s,
    p2r,
    ys,
    ga,
    gat,
    gb,
    ycs,
    ycr,
    yrs,
    yrr,
    yvs,
    yvr,
    fsem,
    csem,
    wsem,
    xsem,
    vsem,
    s1,
    s2,
    sa,
    sb,
    syc,
    syr,
    syv,
    spk,
    spa,
    small,
    rsem,
):
    me_x = lax.axis_index("gx")
    me_y = lax.axis_index("gy")

    def peer_x(step):
        return lax.rem(me_x + step, GX)

    def peer_y(step):
        return lax.rem(me_y + step, GY)

    def each(count, body, start=1):
        def run(t, carry):
            body(t)
            return carry

        lax.fori_loop(start, count, run, 0)

    def chunk(d):
        return pl.ds(pl.multiple_of(d * 8, 8), 8)

    def quarter(q):
        return slice(128 * q, 128 * q + 128)

    def in_copies(d):
        copies = []
        for q in range(4):
            for src, dst, sem in ((conduct, cb, csem), (field, fb, fsem)):
                copies.append(
                    pltpu.make_async_copy(src.at[:, chunk(d), quarter(q)], dst.at[q, d], sem.at[d, q])
                )
        return copies

    def load4(ref, d, x):
        return jnp.concatenate([ref[q, d, x] for q in range(4)], axis=1)

    def order(t):
        u = 15 - t
        return lax.rem(me_x // 4 + lax.rem(u, 4), 4) * 4 + lax.rem(me_x + u // 4 + u, 4)

    def start_in(t, carry):
        for copy in in_copies(order(t)):
            copy.start()
        return carry

    barrier = pltpu.get_barrier_semaphore()

    def greet_x(t, carry):
        pl.semaphore_signal(barrier, inc=1, device_id=(peer_x(t), me_y), device_id_type=MESH)
        return carry

    def greet_y(t, carry):
        pl.semaphore_signal(barrier, inc=1, device_id=(me_x, peer_y(t)), device_id_type=MESH)
        return carry

    lax.fori_loop(1, GX, greet_x, 0)
    lax.fori_loop(1, GY, greet_y, 0)
    lax.fori_loop(0, GX, start_in, 0)
    weights = pltpu.make_async_copy(coupling, cw, wsem)
    weights.start()
    smalls = [
        pltpu.make_async_copy(src, dst, small.at[i])
        for i, (src, dst) in enumerate(((cell_h, cell_v), (count_h, count_v), (cur_h, cur_v)))
    ]
    for copy in smalls:
        copy.start()

    def copy_x(src, dst, sems, slot, to, who):
        return pltpu.make_async_remote_copy(
            src_ref=src, dst_ref=dst, send_sem=sems.at[0, slot], recv_sem=sems.at[1, who],
            device_id=(to, me_y), device_id_type=MESH,
        )

    def copy_y(src, dst, sems, slot, to, who):
        return pltpu.make_async_remote_copy(
            src_ref=src, dst_ref=dst, send_sem=sems.at[0, slot], recv_sem=sems.at[1, who],
            device_id=(me_x, to), device_id_type=MESH,
        )

    lane_z = lax.broadcasted_iota(jnp.int32, (8, NZ), 1)
    scale_f = 1.0 / (KX * KY)

    def eliminate(ds):
        for d in ds:
            for copy in in_copies(d):
                copy.wait()

        def ground(d, x):
            return (1.0 / KX) + (0.5 / KX) * load4(cb, d, x)

        def source(d, x):
            value = load4(fb, d, x)
            up = jnp.where(lane_z == NZ - 1, 0.0, pltpu.roll(value, NZ - 1, 1))
            down = jnp.where(lane_z == 0, 0.0, pltpu.roll(value, 1, 1))
            return (0.5 * scale_f) * value + (0.25 * scale_f) * (up + down)

        blank4 = jnp.zeros((8, NZ), F32)
        states = [(jnp.ones((8, NZ), F32), ground(d, 0), source(d, 0), blank4, blank4) for d in ds]
        for x in range(CX - 1):
            for n, d in enumerate(ds):
                a, g, f, gp, fp = states[n]
                m = inverse(a + g + 1.0)
                am = a * m
                b = f * m
                gp = gp + am * g
                fp = fp + am * f
                f = source(d, x + 1) + b
                for q in range(4):
                    mx[q, d, x] = m[:, quarter(q)]
                    ax[q, d, x] = am[:, quarter(q)]
                    fb[q, d, x] = b[:, quarter(q)]
                states[n] = (am, ground(d, x + 1) + g * m, f, gp, fp)
        for n, d in enumerate(ds):
            for slot, value in enumerate(states[n]):
                for q in range(4):
                    xs[q, d, slot] = value[:, quarter(q)]

    def send_x(q, d):
        copy_x(xs.at[q, d], xr.at[q, me_x], xsem.at[q], d, d, me_x).start()

    def eliminate_and_send(t):
        d = order(t)
        eliminate([d])

        @pl.when(t < GX - 1)
        def _():
            send_x(0, d)

    each(EARLY, lambda t: eliminate([order(t)]), 0)
    pl.semaphore_wait(barrier, GX - 1 + GY - 1)
    each(EARLY, lambda t: send_x(0, order(t)), 0)
    each(GX, eliminate_and_send, EARLY)
    each(GX - 1, lambda t: send_x(1, order(t)), 0)
    each(AHEAD, lambda t: send_x(2, order(t)), 0)
    for q in range(4):
        xr[q, me_x] = xs[q, me_x]

    def respond(d):
        own = jnp.zeros((8, NZ), F32)
        west = jnp.zeros((8, NZ), F32)
        last = jnp.ones((8, NZ), F32)
        for x in range(CX - 1, -1, -1):
            if x < CX - 1:
                m = load4(mx, d, x)
                own = load4(fb, d, x) + m * own
                west = load4(ax, d, x) + m * west
                last = m * last
            for q in range(4):
                fb[q, d, x] = own[:, quarter(q)]
                ax[q, d, x] = west[:, quarter(q)]
                mx[q, d, x] = last[:, quarter(q)]

    each(GX, respond, 0)

    for copy in smalls:
        copy.wait()
    cells = cell_v[...]
    slot_of = lax.broadcasted_iota(jnp.int32, (CAP, 128), 0)
    filled = slot_of < count_v[...]
    at_x = cells >> 16
    place_z = jnp.where(filled, cells & (NZ - 1), -1)
    place_r = ((cells >> 9) & (CY - 1)) * CX + at_x
    rows_v[...] = ((cells >> 7) & 3) * PLANE + (at_x >> 3) * (8 * CY) + ((cells >> 9) & (CY - 1)) * 8 + (at_x & 7)
    rows_n[...] = ((cells >> 7) & 3) * PLANE + ((cells >> 12) & 15) * 128 + at_x * 8 + ((cells >> 9) & 7)
    rows_copies = [
        pltpu.make_async_copy(rows_n, rows_t, rsem.at[0]),
        pltpu.make_async_copy(rows_v, rows_s, rsem.at[1]),
    ]
    for copy in rows_copies:
        copy.start()
    zcol[...] = jnp.concatenate([place_z, jnp.full((128 - CAP, 128), -1, jnp.int32)], axis=0).T
    lanes = lax.broadcasted_iota(jnp.int32, (128, 128), 1)

    def hit_of(k):
        z = zcol[:, k : k + 1]
        return ((z & 127) == lanes) & (z >= 0)

    def pick(table, pairs):
        def run(n):
            for i in range(16):
                o = n * 16 + i
                for k in range(CAP):
                    row = table[k, o]
                    for src, dst in pairs:
                        dst[pl.ds(k * 128 + o, 1), :] = src[pl.ds(row, 1), :]

        each(128 // 16, run, 0)

    rows_copies[0].wait()
    pick(rows_t, [(ref.reshape(4 * PLANE, 128), dst) for ref, dst in ((fb, samp), (ax, samp2), (mx, samp3))])
    for k in range(CAP):
        hit = hit_of(k)
        rows = slice(128 * k, 128 * k + 128)
        for slot, ref in enumerate((samp, samp2, samp3)):
            chosen = jnp.where(hit, ref[rows, :], 0.0) * KY
            pas[slot * CAP + k : slot * CAP + k + 1, :] = jnp.sum(chosen.T, axis=0, keepdims=True)
    key = ((cells >> 12) & 15) * 32 + ((cells >> 7) & 3) * 8 + ((cells >> 9) & 7)
    pas[3 * CAP : 4 * CAP, :] = (key * 128 + (cells & 127)).astype(F32)

    def send_pa(t):
        to = order(t)
        copy_x(pas, par.at[me_x], spa, to, to, me_x).start()

    each(GX - 1, send_pa, 0)
    par[me_x] = pas[...]
    each(GX - 1, lambda t: send_x(2, order(t)), AHEAD)
    each(GX - 1, lambda t: send_x(3, order(t)), 0)

    cb2 = cb.reshape(4 * PLANE, 128)

    def spread_rows(y, u):
        return pl.ds((u // 2) * PLANE + (y // 8) * (8 * CX) + (u % 2) * 64 + lax.rem(y, 8), 8, stride=8)

    def ground_y(y):
        return [(1.0 / KY) + (0.5 / KY) * cb2[spread_rows(y, u), :] for u in range(UNITS)]

    def at_y(y, u):
        return pl.ds(pl.multiple_of(u * (8 * CY) + y * 8, 8), 8)

    def factor(y, state):
        a, g, gp = state
        after = ground_y(y + 1)
        a_new, g_new, gp_new = [], [], []
        for u in range(UNITS):
            m = inverse(a[u] + g[u] + 1.0)
            am = a[u] * m
            my[at_y(y, u), :] = m
            ay[at_y(y, u), :] = am
            gp_new.append(gp[u] + am * g[u])
            g_new.append(after[u] + g[u] * m)
            a_new.append(am)
        return a_new, g_new, gp_new

    ones = [jnp.ones((8, 128), F32) for _ in range(UNITS)]
    zeros = [jnp.zeros((8, 128), F32) for _ in range(UNITS)]
    a_y, g_y, gp_y = lax.fori_loop(0, CY - 1, factor, (ones, ground_y(0), zeros))
    for u in range(UNITS):
        for slot, value in enumerate((a_y, g_y, gp_y)):
            ycs[u, slot] = value[u]

    for u in range(UNITS):
        my[at_y(CY - 1, u), :] = jnp.ones((8, 128), F32)
        ay[at_y(CY - 1, u), :] = jnp.zeros((8, 128), F32)
        wv[at_y(CY - 1, u), :] = jnp.ones((8, 128), F32)
        wp[at_y(CY - 1, u), :] = jnp.zeros((8, 128), F32)

    def send_yc(t):
        to = peer_y(t)
        copy_y(ycs.at[to], ycr.at[me_y], syc, to, to, me_y).start()

    each(GY, send_yc)
    ycr[me_y] = ycs[me_y]

    def weigh(n, state):
        y = CY - 2 - n
        to_last, to_west = state
        last_new, west_new = [], []
        for u in range(UNITS):
            m = my[at_y(y, u), :]
            last_new.append(m * to_last[u])
            west_new.append(ay[at_y(y, u), :] + m * to_west[u])
            wv[at_y(y, u), :] = last_new[u]
            wp[at_y(y, u), :] = west_new[u]
        return last_new, west_new

    lax.fori_loop(0, CY - 1, weigh, (ones, zeros))

    rows_copies[1].wait()
    pick(rows_s, [(wv, samp), (wp, samp2)])
    for k in range(CAP):
        hit = hit_of(k)
        rows = slice(128 * k, 128 * k + 128)
        for slot, ref in enumerate((samp, samp2)):
            chosen = jnp.where(hit, ref[rows, :], 0.0) * (INJECT / KY)
            pks[slot * CAP + k : slot * CAP + k + 1, :] = jnp.sum(chosen.T, axis=0, keepdims=True)
    pks[2 * CAP : 3 * CAP, :] = at_x.astype(F32)
    pks[3 * CAP : 4 * CAP, :] = place_z.astype(F32)

    def send_pk(t):
        to = peer_y(t)
        copy_y(pks, pkr.at[me_y], spk, to, to, me_y).start()

    each(GY, send_pk)
    pkr[me_y] = pks[...]

    blank = jnp.zeros((8, 128), F32)

    def reduce_x(q):
        def arrive(t):
            frm = peer_x(t)
            copy_x(xs.at[q, frm], xr.at[q, frm], xsem.at[q], frm, frm, frm).wait_recv()

        each(GX, arrive)
        q_x = xr[q, 0, 0] + xr[q, 0, 1] + xr[q, 1, 3]
        phi = xr[q, 0, 2] + xr[q, 1, 4]
        kept = [None]
        for r in range(1, GX):
            a = xr[q, r, 0]
            m = inverse(a + q_x)
            am = a * m
            kept.append((am, m * phi))
            more_g, more_f = (xr[q, r + 1, 3], xr[q, r + 1, 4]) if r < GX - 1 else (1.0, 0.0)
            q_x = xr[q, r, 1] + more_g + am * q_x
            phi = xr[q, r, 2] + more_f + am * phi
        value = phi * inverse(q_x)
        for r in range(GX - 1, 0, -1):
            vs[q, r, 1] = value
            value = kept[r][1] + kept[r][0] * value
            vs[q, r, 0] = value
        vs[q, 0, 1] = value
        vs[q, 0, 0] = blank

    def send_back(q):
        def send(t):
            to = peer_x(t)
            copy_x(vs.at[q, to], vr.at[q, me_x], vsem.at[q], to, to, me_x).start()

        each(GX, send)
        vr[q, me_x] = vs[q, me_x]

    row_8 = lax.broadcasted_iota(jnp.int32, (8, 128), 0)
    row_128 = lax.broadcasted_iota(jnp.int32, (128, 128), 0)

    def build_lines(r):
        code = par[r, 3 * CAP : 4 * CAP, :].astype(jnp.int32)
        for k in range(CAP):
            match = jnp.where(row_128 == (code[k : k + 1, :] & 127), 1.0, 0.0)
            lines[r, :, quarter(k)] = match.astype(BF16)

    def gather_x(quarters, first):
        def one(r):
            info = par[r]
            code = info[3 * CAP : 4 * CAP, :].astype(jnp.int32)
            parts = []
            for q in quarters:
                value = vs[q, r].reshape(16, 128)
                high = value.astype(BF16).astype(F32)
                parts.extend((high, value - high))
            product = jnp.dot(jnp.concatenate(parts, axis=0).astype(BF16), lines[r], preferred_element_type=F32)
            for k in range(CAP):
                total = jnp.zeros((8, 128), F32) if first else acc[r, :, quarter(k)]
                for n, q in enumerate(quarters):
                    solved = product[32 * n : 32 * n + 16, quarter(k)] + product[32 * n + 16 : 32 * n + 32, quarter(k)]
                    match = (code[k : k + 1, :] >> 7) == me_x * 32 + q * 8 + row_8
                    value = (
                        info[k : k + 1, :]
                        + info[CAP + k : CAP + k + 1, :] * solved[0:8]
                        + info[2 * CAP + k : 2 * CAP + k + 1, :] * solved[8:16]
                    )
                    total = total + jnp.where(match, value, 0.0)
                acc[r, :, quarter(k)] = total

        def four(n):
            for i in range(4):
                one(n * 4 + i)

        each(4, four, 0)

    reduce_x(0)
    reduce_x(1)

    def arrive_pa(t):
        frm = peer_x(t)
        copy_x(pas, par.at[frm], spa, frm, frm, frm).wait_recv()

    each(GX, arrive_pa)
    each(GX, build_lines, 0)
    reduce_x(2)
    gather_x((0, 1, 2), True)
    reduce_x(3)
    gather_x((3,), False)

    tmat[...] = jnp.zeros_like(tmat)
    p2s[...] = jnp.zeros_like(p2s)
    ys[...] = jnp.zeros_like(ys)
    mine = lax.rem(me_x, 4) * 32 + me_y * CAP
    for r in range(GX):
        total = jnp.sum(acc[r], axis=0, keepdims=True)
        for k in range(CAP):
            tmat[pl.ds(lax.rem(me_y, 2) * 64 + CAP * r + k, 1), :] = total[:, quarter(k)]
    p1s[...] = tmat[...].T.reshape(GX, GY, 128)

    def send_1(t):
        to = peer_x(t)
        copy_x(p1s.at[to], p1r.at[me_x], s1, to, to, me_x).start()

    def arrive_1(t):
        frm = peer_x(t)
        copy_x(p1s.at[frm], p1r.at[frm], s1, frm, frm, frm).wait_recv()

    each(GX, send_1)
    p1r[me_x] = p1s[me_x]
    for q in range(4):
        send_back(q)

    row_m = lax.broadcasted_iota(jnp.int32, (128, WIRE), 0)
    lane_m = lax.broadcasted_iota(jnp.int32, (128, WIRE), 1)
    spread = [jnp.where(lane_m == row_m * CAP + k, 1.0, 0.0).astype(BF16) for k in range(CAP)]

    def three_rows(row):
        high, middle, low = split3(row)
        index = lax.broadcasted_iota(jnp.int32, (16, row.shape[1]), 0)
        stack = jnp.where(index == 0, high, jnp.where(index == 1, middle, jnp.where(index == 2, low, 0.0)))
        return stack.astype(BF16)

    def exact_dot(row, matrix, dims):
        product = lax.dot_general(three_rows(row), matrix, (dims, ((), ())), preferred_element_type=F32)
        return (product[2:3] + product[1:2]) + product[0:1]

    cur_row = jnp.zeros((1, WIRE), F32)
    for k in range(CAP):
        cur_row = cur_row + exact_dot(cur_v[k : k + 1, :], spread[k], ((1,), (0,)))
    lane_n = lax.broadcasted_iota(jnp.int32, (WIRE, WIRE), 1)
    source_n = ((lane_n >> 2) & 15) * 32 + (lane_n >> 6) * CAP + (lane_n & 3)
    shuffle = jnp.where(lax.broadcasted_iota(jnp.int32, (WIRE, WIRE), 0) == source_n, 1.0, 0.0).astype(BF16)
    weights.wait()
    cw2[...] = jnp.dot(cw[...], shuffle, preferred_element_type=F32).astype(BF16)

    def substitute(q):
        def arrive(t):
            frm = peer_x(t)
            copy_x(vs.at[q, frm], vr.at[q, frm], vsem.at[q], frm, frm, frm).wait_recv()

        def group(n):
            ds = [n * 4 + i for i in range(4)]
            west = [vr[q, d, 0] for d in ds]
            last = [vr[q, d, 1] for d in ds]
            for x in range(CX):
                value = [
                    (fb[q, d, x] + ax[q, d, x] * west[i]) + mx[q, d, x] * last[i] for i, d in enumerate(ds)
                ]
                for i, d in enumerate(ds):
                    ht[pl.ds((2 * q + x // 8) * (8 * CY) + d * 64 + x % 8, 8, stride=8), :] = value[i]

        each(GX, arrive)
        each(4, group, 0)

    each(GX, arrive_1)
    total = p1r[0]
    for i in range(1, GX):
        total = total + p1r[i]
    for j in range(GY):
        p2s[j, 0:1, :] = total[j : j + 1, :]

    def send_2(t):
        to = peer_y(t)
        copy_y(p2s.at[to], p2r.at[me_y], s2, to, to, me_y).start()

    def arrive_2(t):
        frm = peer_y(t)
        copy_y(p2s.at[frm], p2r.at[frm], s2, frm, frm, frm).wait_recv()

    each(GY, send_2)
    p2r[me_y] = p2s[me_y]
    def tree(terms):
        while len(terms) > 1:
            terms = [a + b for a, b in zip(terms[::2], terms[1::2])]
        return terms[0]

    def sum_up(q):
        def rows(n, state):
            new = []
            for i, u in enumerate((2 * q, 2 * q + 1)):
                values = [ht[at_y(n * 8 + step, u), :] for step in range(8)]
                for slot, ref in enumerate((wv, wp)):
                    terms = [value * ref[at_y(n * 8 + step, u), :] for step, value in enumerate(values)]
                    new.append(state[2 * i + slot] + tree(terms))
            return new

        sums = lax.fori_loop(0, CY // 8, rows, zeros[:4])
        for i, u in enumerate((2 * q, 2 * q + 1)):
            yrs[u, 0] = sums[2 * i]
            yrs[u, 1] = sums[2 * i + 1]

    substitute(0)
    sum_up(0)
    each(GY, arrive_2)
    row = jnp.concatenate([p2r[2 * j, 0:1, :] + p2r[2 * j + 1, 0:1, :] for j in range(4)], axis=1)
    new_row = 0.5 * cur_row + exact_dot(row, cw2[...], ((1,), (1,)))
    for a in range(4):
        ys[a : a + 1, :] = new_row[:, 128 * a : 128 * a + 128]

    def send_a(t):
        to = peer_y(t)
        copy_y(ys, ga.at[me_y], sa, to, to, me_y).start()

    def arrive_a(t):
        frm = peer_y(t)
        copy_y(ys, ga.at[frm], sa, frm, frm, frm).wait_recv()

    each(GY, send_a)
    ga[me_y] = ys[...]
    for k in range(CAP):
        cur_out[k : k + 1, :] = exact_dot(new_row, spread[k], ((1,), (1,)))
    substitute(1)
    sum_up(1)
    substitute(2)
    sum_up(2)
    substitute(3)
    sum_up(3)
    def send_yr(t):
        to = peer_y(t)
        copy_y(yrs.at[to], yrr.at[me_y], syr, to, to, me_y).start()

    each(GY, send_yr)
    yrr[me_y] = yrs[me_y]
    each(GY, arrive_a)
    for j in range(GY):
        part = ga[j]
        for a in range(4):
            gat[a, j : j + 1, :] = part[a : a + 1, :]

    def send_b(t):
        to = peer_x(t)
        copy_x(gat.at[to // 4], gb.at[me_x], sb, to, to, me_x).start()

    def arrive_b(t):
        frm = peer_x(t)
        copy_x(gat.at[0], gb.at[frm], sb, frm, frm, frm).wait_recv()

    each(GX, send_b)
    gb[me_x] = gat[me_x // 4]
    def drain_x(t):
        to = peer_x(t)
        for q in range(4):
            copy_x(xs.at[q, to], xr.at[q, me_x], xsem.at[q], to, to, me_x).wait_send()
            copy_x(vs.at[q, to], vr.at[q, me_x], vsem.at[q], to, to, me_x).wait_send()
        copy_x(p1s.at[to], p1r.at[me_x], s1, to, to, me_x).wait_send()
        copy_x(pas, par.at[me_x], spa, to, to, me_x).wait_send()

    def drain_y(t):
        to = peer_y(t)
        copy_y(p2s.at[to], p2r.at[me_y], s2, to, to, me_y).wait_send()
        copy_y(ycs.at[to], ycr.at[me_y], syc, to, to, me_y).wait_send()
        copy_y(yrs.at[to], yrr.at[me_y], syr, to, to, me_y).wait_send()
        copy_y(pks, pkr.at[me_y], spk, to, to, me_y).wait_send()

    def arrive_pk(t):
        frm = peer_y(t)
        copy_y(pks, pkr.at[frm], spk, frm, frm, frm).wait_recv()

    def arrive_yc(t):
        frm = peer_y(t)
        copy_y(ycs.at[frm], ycr.at[frm], syc, frm, frm, frm).wait_recv()

    each(GY, arrive_pk)
    each(GY, arrive_yc)
    share_z = ((me_y // 2) * 128 + lax.broadcasted_iota(jnp.int32, (128, 128), 0)).astype(F32)
    share_x = (lax.rem(me_y, 2) * 8 + lax.broadcasted_iota(jnp.int32, (8, 128), 0)).astype(F32)

    def build_share(r):
        info = pkr[r]
        for k in range(CAP):
            zhot[r, :, 128 * k : 128 * k + 128] = jnp.where(share_z == info[12 + k : 13 + k, :], 1.0, 0.0).astype(BF16)
            match = share_x == info[8 + k : 9 + k, :]
            for slot in range(2):
                weight = info[4 * slot + k : 4 * slot + k + 1, :]
                xmask[r, slot, :, 128 * k : 128 * k + 128] = jnp.where(match, weight, 0.0)

    each(GY, build_share, 0)
    q_y = ycr[0, 0] + ycr[0, 1] + ycr[1, 2]
    for r in range(1, GY):
        a = ycr[r, 0]
        m = inverse(a + q_y)
        yk[r, 0] = a * m
        yk[r, 1] = m
        more = ycr[r + 1, 2] if r < GY - 1 else 1.0
        q_y = ycr[r, 1] + more + a * m * q_y
    yk[0, 0] = inverse(q_y)
    row_16 = lax.broadcasted_iota(jnp.int32, (CX, 128), 0)

    def build_hot(y):
        rows = row_16 + y * CX
        for k in range(CAP):
            match = jnp.where(rows == place_r[k : k + 1, :], 1.0, 0.0)
            hot[pl.ds(pl.multiple_of(y * CX, CX), CX), quarter(k)] = match.astype(BF16)

    def build_some(n):
        for step in range(8):
            build_hot(n * 8 + step)

    each(CY // 8, build_some, 0)
    each(GX, drain_x)
    each(GY, drain_y)
    each(GX, arrive_b)

    back = gb[...].reshape(128, 128)
    gbt[...] = back.T
    mine_rows = gbt[pl.ds(pl.multiple_of(lax.rem(me_x, 4) * 32, 32), 32), :]
    extra = []
    for r in range(GY):
        values = jnp.concatenate([mine_rows[CAP * r + k : CAP * r + k + 1, :] for k in range(CAP)], axis=1)
        parts = jnp.concatenate([xmask[r, 0] * values, xmask[r, 1] * values], axis=0)
        high = parts.astype(BF16)
        low = (parts - high.astype(F32)).astype(BF16)
        product = lax.dot_general(
            jnp.concatenate([high, low], axis=0), zhot[r], (((1,), (1,)), ((), ())), preferred_element_type=F32
        )
        extra.append((product[0:8] + product[16:24], product[8:16] + product[24:32]))

    def arrive_yr(t):
        frm = peer_y(t)
        copy_y(yrs.at[frm], yrr.at[frm], syr, frm, frm, frm).wait_recv()

    each(GY, arrive_yr)
    phi = (yrr[0, 0] + extra[0][0]) + (yrr[1, 1] + extra[1][1])
    phis = [phi]
    for r in range(1, GY):
        phi = (yrr[r, 0] + extra[r][0]) + yk[r, 0] * phi
        if r < GY - 1:
            phi = phi + (yrr[r + 1, 1] + extra[r + 1][1])
        phis.append(phi)
    value = phi * yk[0, 0]
    for r in range(GY - 1, 0, -1):
        yvs[r, 1] = value
        value = yk[r, 1] * phis[r - 1] + yk[r, 0] * value
        yvs[r, 0] = value
    yvs[0, 1] = value
    yvs[0, 0] = jnp.zeros((8, 128), F32)

    def send_yv(t):
        to = peer_y(t)
        copy_y(yvs.at[to], yvr.at[me_y], syv, to, to, me_y).start()

    def arrive_yv(t):
        frm = peer_y(t)
        copy_y(yvs.at[frm], yvr.at[frm], syv, frm, frm, frm).wait_recv()

    each(GY, send_yv)
    yvr[me_y] = yvs[me_y]

    lane_k = lax.broadcasted_iota(jnp.int32, (128, NZ), 1)
    for k in range(CAP):
        value = jnp.sum(jnp.where(lanes == mine + k, back, 0.0), axis=1, keepdims=True) * (INJECT / KY)
        spot = jnp.where(lane_k == zcol[:, k : k + 1], value, 0.0)
        high = spot.astype(BF16)
        bhl[128 * k : 128 * k + 128, :] = high
        bhl[WIRE + 128 * k : WIRE + 128 * k + 128, :] = (spot - high.astype(F32)).astype(BF16)

    def scatter(n, added):
        part = hot[pl.ds(pl.multiple_of(n * 256, 256), 256), :]
        added[...] = jnp.dot(jnp.concatenate([part, part], axis=1), bhl[...], preferred_element_type=F32)

    def eliminate_y(n, added, state):
        for step in range(16):
            y = n * 16 + step
            new = []
            for u in range(UNITS):
                row = step * CX + (u % 2) * 8
                more = added[row : row + 8, quarter(u // 2)]
                b = ((ht[at_y(y, u), :] + more) + state[u]) * my[at_y(y, u), :]
                ht[at_y(y, u), :] = b
                new.append(b)
            state = new
        return state

    def forward_y(n, state):
        scatter(2 * n + 1, added1)
        state = eliminate_y(2 * n, added0, state)
        scatter(jnp.minimum(2 * n + 2, CY // 16 - 1), added0)
        return eliminate_y(2 * n + 1, added1, state)

    scatter(0, added0)
    lax.fori_loop(0, CY // 32, forward_y, zeros)
    each(GY, arrive_yv)

    ends[...] = yvr[...]

    def drain_late_x(t):
        copy_x(gat.at[0], gb.at[me_x], sb, peer_x(t), peer_x(t), me_x).wait_send()

    def drain_late_y(t):
        to = peer_y(t)
        copy_y(ys, ga.at[me_y], sa, to, to, me_y).wait_send()
        copy_y(yvs.at[to], yvr.at[me_y], syv, to, to, me_y).wait_send()

    each(GX, drain_late_x)
    each(GY, drain_late_y)


def deliver(ht, my, ay, ends, cur_in, out, cur_out, staged, sems):
    rows = staged.reshape(4 * PLANE, 128)
    west = [ends[u, 0] for u in range(UNITS)]
    last = [ends[u, 1] for u in range(UNITS)]

    def copies(c):
        place = pl.ds(pl.multiple_of(c * 8, 8), 8)
        return [
            pltpu.make_async_copy(staged.at[q, c], out.at[:, place, 128 * q : 128 * q + 128], sems.at[q, c])
            for q in range(4)
        ]

    def put(y, value):
        for u in range(UNITS):
            start = (u // 2) * PLANE + (y // 8) * (8 * CX) + (u % 2) * 64 + lax.rem(y, 8)
            rows[pl.ds(start, 8, stride=8), :] = value[u]

    def step(y, value):
        new = []
        for u in range(UNITS):
            at = pl.ds(pl.multiple_of(u * (8 * CY) + y * 8, 8), 8)
            new.append((ht[at, :] + ay[at, :] * west[u]) + my[at, :] * value[u])
        put(y, new)
        return new

    def send(c):
        for copy in copies(c):
            copy.start()

    def chunk(n, value):
        c = CY // 8 - 1 - n
        for back in range(8):
            value = step(c * 8 + 7 - back, value)
        send(c)
        return value

    put(CY - 1, last)
    value = last
    for back in range(1, 8):
        value = step(CY - 1 - back, value)
    send(CY // 8 - 1)
    lax.fori_loop(1, CY // 8, chunk, value)
    cur_out[...] = cur_in[...]

    def wait(c, carry):
        for copy in copies(c):
            copy.wait()
        return carry

    lax.fori_loop(0, CY // 8, wait, 0)


def local(field, conduct, seg_cell, seg_count, currents, coupling):
    hbm = pl.BlockSpec(memory_space=pltpu.HBM)
    vmem = pl.BlockSpec(memory_space=pltpu.VMEM)
    cells = seg_cell[0].T
    block = lambda *shape: pltpu.VMEM(shape, F32)
    sems = lambda count: pltpu.SemaphoreType.DMA((2, count))
    scratch = [
        block(4, GX, CX, 8, 128),
        block(4, GX, CX, 8, 128),
        block(4, GX, CX, 8, 128),
        block(4, GX, CX, 8, 128),
        block(4, GX, 5, 8, 128),
        block(4, GX, 5, 8, 128),
        block(4, GX, 2, 8, 128),
        block(4, GX, 2, 8, 128),
        pltpu.VMEM((WIRE, WIRE), BF16),
        pltpu.VMEM((PLANE, WIRE), BF16),
        pltpu.VMEM((2 * WIRE, NZ), BF16),
        block(WIRE, 128),
        pltpu.VMEM((128, 128), jnp.int32),
        pltpu.VMEM((CAP, 128), jnp.int32),
        pltpu.VMEM((1, 128), jnp.int32),
        block(CAP, 128),
        pltpu.VMEM((CAP, 128), jnp.int32),
        pltpu.SMEM((CAP, 128), jnp.int32),
        pltpu.VMEM((CAP, 128), jnp.int32),
        pltpu.SMEM((CAP, 128), jnp.int32),
        block(WIRE, 128),
        block(16, 128),
        block(GX, 16, 128),
        pltpu.VMEM((GX, 128, WIRE), BF16),
        block(GX, 8, WIRE),
        block(128, 128),
        pltpu.VMEM((WIRE, WIRE), BF16),
        block(4 * PLANE, 128),
        block(4 * PLANE, 128),
        block(WIRE, 128),
        block(16, 128),
        block(GY, 16, 128),
        pltpu.VMEM((GY, 128, WIRE), BF16),
        block(GY, 2, 8, WIRE),
        block(128, 128),
        block(GY, 2, 8, 128),
        block(256, NZ),
        block(256, NZ),
        block(GX, 8, 128),
        block(GX, 8, 128),
        block(GY, 8, 128),
        block(GY, 8, 128),
        block(8, 128),
        block(GY, 8, 128),
        block(4, 8, 128),
        block(GX, 8, 128),
        block(GY, 3, 8, 128),
        block(GY, 3, 8, 128),
        block(GY, 2, 8, 128),
        block(GY, 2, 8, 128),
        block(GY, 2, 8, 128),
        block(GY, 2, 8, 128),
        pltpu.SemaphoreType.DMA((GX, 4)),
        pltpu.SemaphoreType.DMA((GX, 4)),
        pltpu.SemaphoreType.DMA,
        pltpu.SemaphoreType.DMA((4, 2, GX)),
        pltpu.SemaphoreType.DMA((4, 2, GX)),
        sems(GX),
        sems(GY),
        sems(GY),
        sems(GX),
        sems(GY),
        sems(GY),
        sems(GY),
        sems(GY),
        sems(GX),
        pltpu.SemaphoreType.DMA((3,)),
        pltpu.SemaphoreType.DMA((2,)),
    ]
    rows = pltpu.VMEM((4 * PLANE, 128), F32)
    *parts, currents_next = pl.pallas_call(
        kernel,
        out_shape=(rows, rows, rows, pltpu.VMEM((GY, 2, 8, 128), F32), pltpu.VMEM((CAP, 128), F32)),
        in_specs=[hbm] * 6,
        out_specs=(vmem,) * 5,
        scratch_shapes=scratch,
        compiler_params=pltpu.CompilerParams(
            collective_id=0, has_side_effects=True, vmem_limit_bytes=49 * 1024 * 1024
        ),
    )(field, conduct, cells, seg_count, currents[0].T, coupling[0])
    field_next, currents_next = pl.pallas_call(
        deliver,
        out_shape=(
            jax.ShapeDtypeStruct((CX, CY, NZ), F32),
            jax.ShapeDtypeStruct((CAP, 128), F32),
        ),
        in_specs=[vmem] * 5,
        out_specs=(hbm, vmem),
        scratch_shapes=[block(4, GX, CX, 8, 128), pltpu.SemaphoreType.DMA((4, GX))],
        compiler_params=pltpu.CompilerParams(vmem_limit_bytes=6 * 1024 * 1024),
    )(*parts, currents_next)
    return field_next, currents_next.T[None]


def solution(mesh):
    placed = (
        P("gx", "gy", None),
        P("gx", "gy", None),
        P(("gx", "gy"), None, None),
        P(("gx", "gy"), None),
        P(("gx", "gy"), None, None),
        P(("gx", "gy"), None, None),
    )
    return jax.shard_map(
        local,
        mesh=mesh,
        in_specs=placed,
        out_specs=(P("gx", "gy", None), P(("gx", "gy"), None, None)),
        check_vma=False,
    )
```

```python
import functools

import jax
import jax.numpy as jnp
from jax import lax
from jax.experimental import pallas as pl
from jax.experimental.pallas import tpu as pltpu
from jax.sharding import PartitionSpec as P

MESH = pl.DeviceIdType.MESH
F32 = jnp.float32
BF16 = jnp.bfloat16

CX, CY, NZ, CAP = 16, 128, 512, 4
GX, GY = 16, 8
WIRE = 512
KX = 8.0 * CX * CX
KY = 8.0 * CY * CY
INJECT = 4.0 * KY**0.5
PLANE = CY * CX
UNITS = 8
EARLY = 2
AHEAD = 5
SENT = 3 * CAP


def inverse(value):
    return pl.reciprocal(value, approx=True)


def split3(value):
    high = value.astype(BF16).astype(F32)
    rest = value - high
    middle = rest.astype(BF16).astype(F32)
    return high, middle, rest - middle


def kernel(
    field,
    conduct,
    cell_h,
    count_h,
    cur_h,
    coupling,
    ht,
    my,
    ay,
    ends,
    cur_out,
    fb,
    cb,
    mx,
    ax,
    xs,
    xr,
    vs,
    vr,
    cw,
    hot,
    bhl,
    samp,
    zcol,
    cell_v,
    count_v,
    cur_v,
    rows_v,
    rows_s,
    rows_n,
    rows_t,
    samp3,
    pas,
    par,
    lines,
    acc,
    tmat,
    cw2,
    wv,
    wp,
    samp2,
    pks,
    pkr,
    zhot,
    xmask,
    gbt,
    yk,
    added0,
    added1,
    p1s,
    p1r,
    p2s,
    p2r,
    ys,
    ga,
    gat,
    gb,
    ycs,
    ycr,
    yrs,
    yrr,
    yvs,
    yvr,
    fsem,
    csem,
    wsem,
    xsem,
    vsem,
    s1,
    s2,
    sa,
    sb,
    syc,
    syr,
    syv,
    spk,
    spa,
    small,
    rsem,
):
    me_x = lax.axis_index("gx")
    me_y = lax.axis_index("gy")

    def peer_x(step):
        return lax.rem(me_x + step, GX)

    def peer_y(step):
        return lax.rem(me_y + step, GY)

    def each(count, body, start=1):
        def run(t, carry):
            body(t)
            return carry

        lax.fori_loop(start, count, run, 0)

    def chunk(d):
        return pl.ds(pl.multiple_of(d * 8, 8), 8)

    def quarter(q):
        return slice(128 * q, 128 * q + 128)

    def in_copies(d):
        copies = []
        for q in range(4):
            for src, dst, sem in ((conduct, cb, csem), (field, fb, fsem)):
                copies.append(
                    pltpu.make_async_copy(src.at[:, chunk(d), quarter(q)], dst.at[q, d], sem.at[d, q])
                )
        return copies

    def load4(ref, d, x):
        return jnp.concatenate([ref[q, d, x] for q in range(4)], axis=1)

    def order(t):
        u = 15 - t
        return lax.rem(me_x // 4 + lax.rem(u, 4), 4) * 4 + lax.rem(me_x + u // 4 + u, 4)

    def start_in(t, carry):
        for copy in in_copies(order(t)):
            copy.start()
        return carry

    barrier = pltpu.get_barrier_semaphore()

    def greet_x(t, carry):
        pl.semaphore_signal(barrier, inc=1, device_id=(peer_x(t), me_y), device_id_type=MESH)
        return carry

    def greet_y(t, carry):
        pl.semaphore_signal(barrier, inc=1, device_id=(me_x, peer_y(t)), device_id_type=MESH)
        return carry

    lax.fori_loop(1, GX, greet_x, 0)
    lax.fori_loop(1, GY, greet_y, 0)
    lax.fori_loop(0, GX, start_in, 0)
    weights = pltpu.make_async_copy(coupling, cw, wsem)
    weights.start()
    smalls = [
        pltpu.make_async_copy(src, dst, small.at[i])
        for i, (src, dst) in enumerate(((cell_h, cell_v), (count_h, count_v), (cur_h, cur_v)))
    ]
    for copy in smalls:
        copy.start()

    def copy_x(src, dst, sems, slot, to, who):
        return pltpu.make_async_remote_copy(
            src_ref=src, dst_ref=dst, send_sem=sems.at[0, slot], recv_sem=sems.at[1, who],
            device_id=(to, me_y), device_id_type=MESH,
        )

    def copy_y(src, dst, sems, slot, to, who):
        return pltpu.make_async_remote_copy(
            src_ref=src, dst_ref=dst, send_sem=sems.at[0, slot], recv_sem=sems.at[1, who],
            device_id=(me_x, to), device_id_type=MESH,
        )

    lane_z = lax.broadcasted_iota(jnp.int32, (8, NZ), 1)
    scale_f = 1.0 / (KX * KY)

    def eliminate(ds):
        for d in ds:
            for copy in in_copies(d):
                copy.wait()

        def ground(d, x):
            return (1.0 / KX) + (0.5 / KX) * load4(cb, d, x)

        def source(d, x):
            value = load4(fb, d, x)
            up = jnp.where(lane_z == NZ - 1, 0.0, pltpu.roll(value, NZ - 1, 1))
            down = jnp.where(lane_z == 0, 0.0, pltpu.roll(value, 1, 1))
            return (0.5 * scale_f) * value + (0.25 * scale_f) * (up + down)

        blank4 = jnp.zeros((8, NZ), F32)
        states = [(jnp.ones((8, NZ), F32), ground(d, 0), source(d, 0), blank4, blank4) for d in ds]
        for x in range(CX - 1):
            for n, d in enumerate(ds):
                a, g, f, gp, fp = states[n]
                m = inverse(a + g + 1.0)
                am = a * m
                b = f * m
                gp = gp + am * g
                fp = fp + am * f
                f = source(d, x + 1) + b
                for q in range(4):
                    mx[q, d, x] = m[:, quarter(q)]
                    ax[q, d, x] = am[:, quarter(q)]
                    fb[q, d, x] = b[:, quarter(q)]
                states[n] = (am, ground(d, x + 1) + g * m, f, gp, fp)
        for n, d in enumerate(ds):
            for slot, value in enumerate(states[n]):
                for q in range(4):
                    xs[q, d, slot] = value[:, quarter(q)]

    def send_x(q, d):
        copy_x(xs.at[q, d], xr.at[q, me_x], xsem.at[q], d, d, me_x).start()

    def eliminate_and_send(t):
        d = order(t)
        eliminate([d])

        @pl.when(t < GX - 1)
        def _():
            send_x(0, d)

    each(EARLY, lambda t: eliminate([order(t)]), 0)
    pl.semaphore_wait(barrier, GX - 1 + GY - 1)
    each(EARLY, lambda t: send_x(0, order(t)), 0)
    each(GX, eliminate_and_send, EARLY)
    each(GX - 1, lambda t: send_x(1, order(t)), 0)
    each(AHEAD, lambda t: send_x(2, order(t)), 0)
    for q in range(4):
        xr[q, me_x] = xs[q, me_x]

    def respond(d):
        own = jnp.zeros((8, NZ), F32)
        west = jnp.zeros((8, NZ), F32)
        last = jnp.ones((8, NZ), F32)
        for x in range(CX - 1, -1, -1):
            if x < CX - 1:
                m = load4(mx, d, x)
                own = load4(fb, d, x) + m * own
                west = load4(ax, d, x) + m * west
                last = m * last
            for q in range(4):
                fb[q, d, x] = own[:, quarter(q)]
                ax[q, d, x] = west[:, quarter(q)]
                mx[q, d, x] = last[:, quarter(q)]

    each(GX, respond, 0)

    for copy in smalls:
        copy.wait()
    cells = cell_v[...]
    slot_of = lax.broadcasted_iota(jnp.int32, (CAP, 128), 0)
    filled = slot_of < count_v[...]
    at_x = cells >> 16
    place_z = jnp.where(filled, cells & (NZ - 1), -1)
    place_r = ((cells >> 9) & (CY - 1)) * CX + at_x
    rows_v[...] = ((cells >> 7) & 3) * PLANE + (at_x >> 3) * (8 * CY) + ((cells >> 9) & (CY - 1)) * 8 + (at_x & 7)
    rows_n[...] = ((cells >> 7) & 3) * PLANE + ((cells >> 12) & 15) * 128 + at_x * 8 + ((cells >> 9) & 7)
    rows_copies = [
        pltpu.make_async_copy(rows_n, rows_t, rsem.at[0]),
        pltpu.make_async_copy(rows_v, rows_s, rsem.at[1]),
    ]
    for copy in rows_copies:
        copy.start()
    zcol[...] = jnp.concatenate([place_z, jnp.full((128 - CAP, 128), -1, jnp.int32)], axis=0).T
    lanes = lax.broadcasted_iota(jnp.int32, (128, 128), 1)

    def hit_of(k):
        z = zcol[:, k : k + 1]
        return ((z & 127) == lanes) & (z >= 0)

    def pick(table, pairs):
        def run(n):
            for i in range(16):
                o = n * 16 + i
                for k in range(CAP):
                    row = table[k, o]
                    for src, dst in pairs:
                        dst[pl.ds(k * 128 + o, 1), :] = src[pl.ds(row, 1), :]

        each(128 // 16, run, 0)

    rows_copies[0].wait()
    pick(rows_t, [(ref.reshape(4 * PLANE, 128), dst) for ref, dst in ((fb, samp), (ax, samp2), (mx, samp3))])
    for k in range(CAP):
        hit = hit_of(k)
        rows = slice(128 * k, 128 * k + 128)
        for slot, ref in ((3, samp), (0, samp2), (1, samp3)):
            chosen = jnp.where(hit, ref[rows, :], 0.0) * KY
            pas[slot * CAP + k : slot * CAP + k + 1, :] = jnp.sum(chosen.T, axis=0, keepdims=True)
    key = ((cells >> 12) & 15) * 32 + ((cells >> 7) & 3) * 8 + ((cells >> 9) & 7)
    pas[2 * CAP : 3 * CAP, :] = (key * 128 + (cells & 127)).astype(F32)

    def send_pa(t):
        to = order(t)
        copy_x(pas.at[0:SENT], par.at[me_x, 0:SENT], spa, to, to, me_x).start()

    each(GX - 1, send_pa, 0)
    par[me_x] = pas[...]
    each(GX - 1, lambda t: send_x(2, order(t)), AHEAD)
    each(GX - 1, lambda t: send_x(3, order(t)), 0)

    cb2 = cb.reshape(4 * PLANE, 128)

    def spread_rows(y, u):
        return pl.ds((u // 2) * PLANE + (y // 8) * (8 * CX) + (u % 2) * 64 + lax.rem(y, 8), 8, stride=8)

    def ground_y(y):
        return [(1.0 / KY) + (0.5 / KY) * cb2[spread_rows(y, u), :] for u in range(UNITS)]

    def at_y(y, u):
        return pl.ds(pl.multiple_of(u * (8 * CY) + y * 8, 8), 8)

    def factor(y, state):
        a, g, gp = state
        after = ground_y(y + 1)
        a_new, g_new, gp_new = [], [], []
        for u in range(UNITS):
            m = inverse(a[u] + g[u] + 1.0)
            am = a[u] * m
            my[at_y(y, u), :] = m
            ay[at_y(y, u), :] = am
            gp_new.append(gp[u] + am * g[u])
            g_new.append(after[u] + g[u] * m)
            a_new.append(am)
        return a_new, g_new, gp_new

    ones = [jnp.ones((8, 128), F32) for _ in range(UNITS)]
    zeros = [jnp.zeros((8, 128), F32) for _ in range(UNITS)]
    a_y, g_y, gp_y = lax.fori_loop(0, CY - 1, factor, (ones, ground_y(0), zeros))
    for u in range(UNITS):
        for slot, value in enumerate((a_y, g_y, gp_y)):
            ycs[u, slot] = value[u]

    for u in range(UNITS):
        my[at_y(CY - 1, u), :] = jnp.ones((8, 128), F32)
        ay[at_y(CY - 1, u), :] = jnp.zeros((8, 128), F32)
        wv[at_y(CY - 1, u), :] = jnp.ones((8, 128), F32)
        wp[at_y(CY - 1, u), :] = jnp.zeros((8, 128), F32)

    def send_yc(t):
        to = peer_y(t)
        copy_y(ycs.at[to], ycr.at[me_y], syc, to, to, me_y).start()

    each(GY, send_yc)
    ycr[me_y] = ycs[me_y]

    def weigh(n, state):
        y = CY - 2 - n
        to_last, to_west = state
        last_new, west_new = [], []
        for u in range(UNITS):
            m = my[at_y(y, u), :]
            last_new.append(m * to_last[u])
            west_new.append(ay[at_y(y, u), :] + m * to_west[u])
            wv[at_y(y, u), :] = last_new[u]
            wp[at_y(y, u), :] = west_new[u]
        return last_new, west_new

    lax.fori_loop(0, CY - 1, weigh, (ones, zeros))

    rows_copies[1].wait()
    pick(rows_s, [(wv, samp), (wp, samp2)])
    for k in range(CAP):
        hit = hit_of(k)
        rows = slice(128 * k, 128 * k + 128)
        for slot, ref in enumerate((samp, samp2)):
            chosen = jnp.where(hit, ref[rows, :], 0.0) * (INJECT / KY)
            pks[slot * CAP + k : slot * CAP + k + 1, :] = jnp.sum(chosen.T, axis=0, keepdims=True)
    pks[2 * CAP : 3 * CAP, :] = at_x.astype(F32)
    pks[3 * CAP : 4 * CAP, :] = place_z.astype(F32)

    def send_pk(t):
        to = peer_y(t)
        copy_y(pks, pkr.at[me_y], spk, to, to, me_y).start()

    each(GY, send_pk)
    pkr[me_y] = pks[...]

    blank = jnp.zeros((8, 128), F32)

    def reduce_x(q):
        def arrive(t):
            frm = peer_x(t)
            copy_x(xs.at[q, frm], xr.at[q, frm], xsem.at[q], frm, frm, frm).wait_recv()

        each(GX, arrive)
        q_x = xr[q, 0, 0] + xr[q, 0, 1] + xr[q, 1, 3]
        phi = xr[q, 0, 2] + xr[q, 1, 4]
        kept = [None]
        for r in range(1, GX):
            a = xr[q, r, 0]
            m = inverse(a + q_x)
            am = a * m
            kept.append((am, m * phi))
            more_g, more_f = (xr[q, r + 1, 3], xr[q, r + 1, 4]) if r < GX - 1 else (1.0, 0.0)
            q_x = xr[q, r, 1] + more_g + am * q_x
            phi = xr[q, r, 2] + more_f + am * phi
        value = phi * inverse(q_x)
        for r in range(GX - 1, 0, -1):
            vs[q, r, 1] = value
            value = kept[r][1] + kept[r][0] * value
            vs[q, r, 0] = value
        vs[q, 0, 1] = value
        vs[q, 0, 0] = blank

    def send_back(q):
        def send(t):
            to = peer_x(t)
            copy_x(vs.at[q, to], vr.at[q, me_x], vsem.at[q], to, to, me_x).start()

        each(GX, send)
        vr[q, me_x] = vs[q, me_x]

    row_8 = lax.broadcasted_iota(jnp.int32, (8, 128), 0)
    row_128 = lax.broadcasted_iota(jnp.int32, (128, 128), 0)

    def build_lines(r):
        code = par[r, 2 * CAP : SENT, :].astype(jnp.int32)
        for k in range(CAP):
            match = jnp.where(row_128 == (code[k : k + 1, :] & 127), 1.0, 0.0)
            lines[r, :, quarter(k)] = match.astype(BF16)

    def gather_x(quarters, first):
        def one(r):
            info = par[r, 0 : 2 * CAP, :]
            code = par[r, 2 * CAP : SENT, :].astype(jnp.int32)
            parts = []
            for q in quarters:
                value = vs[q, r].reshape(16, 128)
                high = value.astype(BF16).astype(F32)
                parts.extend((high, value - high))
            product = jnp.dot(jnp.concatenate(parts, axis=0).astype(BF16), lines[r], preferred_element_type=F32)
            for k in range(CAP):
                total = jnp.zeros((8, 128), F32) if first else acc[r, :, quarter(k)]
                for n, q in enumerate(quarters):
                    solved = product[32 * n : 32 * n + 16, quarter(k)] + product[32 * n + 16 : 32 * n + 32, quarter(k)]
                    match = (code[k : k + 1, :] >> 7) == me_x * 32 + q * 8 + row_8
                    value = (
                        info[k : k + 1, :] * solved[0:8] + info[CAP + k : CAP + k + 1, :] * solved[8:16]
                    )
                    total = total + jnp.where(match, value, 0.0)
                acc[r, :, quarter(k)] = total

        def eight(n):
            for i in range(8):
                one(n * 8 + i)

        each(2, eight, 0)

    reduce_x(0)
    reduce_x(1)

    def arrive_pa(t):
        frm = peer_x(t)
        copy_x(pas.at[0:SENT], par.at[frm, 0:SENT], spa, frm, frm, frm).wait_recv()

    each(GX, arrive_pa)
    each(GX, build_lines, 0)
    reduce_x(2)
    gather_x((0, 1, 2), True)
    reduce_x(3)
    gather_x((3,), False)

    tmat[...] = jnp.zeros_like(tmat)
    p2s[...] = jnp.zeros_like(p2s)
    ys[...] = jnp.zeros_like(ys)
    mine = lax.rem(me_x, 4) * 32 + me_y * CAP
    for r in range(GX):
        total = jnp.sum(acc[r], axis=0, keepdims=True)
        for k in range(CAP):
            own = jnp.where(me_x == r, pas[3 * CAP + k : 3 * CAP + k + 1, :], 0.0)
            tmat[pl.ds(lax.rem(me_y, 2) * 64 + CAP * r + k, 1), :] = total[:, quarter(k)] + own
    p1s[...] = tmat[...].T.reshape(GX, GY, 128)

    def send_1(t):
        to = peer_x(t)
        copy_x(p1s.at[to], p1r.at[me_x], s1, to, to, me_x).start()

    def arrive_1(t):
        frm = peer_x(t)
        copy_x(p1s.at[frm], p1r.at[frm], s1, frm, frm, frm).wait_recv()

    each(GX, send_1)
    p1r[me_x] = p1s[me_x]
    for q in range(4):
        send_back(q)

    row_m = lax.broadcasted_iota(jnp.int32, (128, WIRE), 0)
    lane_m = lax.broadcasted_iota(jnp.int32, (128, WIRE), 1)
    spread = [jnp.where(lane_m == row_m * CAP + k, 1.0, 0.0).astype(BF16) for k in range(CAP)]

    def three_rows(row):
        high, middle, low = split3(row)
        index = lax.broadcasted_iota(jnp.int32, (16, row.shape[1]), 0)
        stack = jnp.where(index == 0, high, jnp.where(index == 1, middle, jnp.where(index == 2, low, 0.0)))
        return stack.astype(BF16)

    def exact_dot(row, matrix, dims):
        product = lax.dot_general(three_rows(row), matrix, (dims, ((), ())), preferred_element_type=F32)
        return (product[2:3] + product[1:2]) + product[0:1]

    cur_row = jnp.zeros((1, WIRE), F32)
    for k in range(CAP):
        cur_row = cur_row + exact_dot(cur_v[k : k + 1, :], spread[k], ((1,), (0,)))
    lane_n = lax.broadcasted_iota(jnp.int32, (WIRE, WIRE), 1)
    source_n = ((lane_n >> 2) & 15) * 32 + (lane_n >> 6) * CAP + (lane_n & 3)
    shuffle = jnp.where(lax.broadcasted_iota(jnp.int32, (WIRE, WIRE), 0) == source_n, 1.0, 0.0).astype(BF16)
    weights.wait()
    cw2[...] = jnp.dot(cw[...], shuffle, preferred_element_type=F32).astype(BF16)

    def substitute(q):
        def arrive(t):
            frm = peer_x(t)
            copy_x(vs.at[q, frm], vr.at[q, frm], vsem.at[q], frm, frm, frm).wait_recv()

        def group(n):
            ds = [n * 4 + i for i in range(4)]
            west = [vr[q, d, 0] for d in ds]
            last = [vr[q, d, 1] for d in ds]
            for x in range(CX):
                value = [
                    (fb[q, d, x] + ax[q, d, x] * west[i]) + mx[q, d, x] * last[i] for i, d in enumerate(ds)
                ]
                for i, d in enumerate(ds):
                    ht[pl.ds((2 * q + x // 8) * (8 * CY) + d * 64 + x % 8, 8, stride=8), :] = value[i]

        each(GX, arrive)
        each(4, group, 0)

    each(GX, arrive_1)
    total = p1r[0]
    for i in range(1, GX):
        total = total + p1r[i]
    for j in range(GY):
        p2s[j, 0:1, :] = total[j : j + 1, :]

    def send_2(t):
        to = peer_y(t)
        copy_y(p2s.at[to], p2r.at[me_y], s2, to, to, me_y).start()

    def arrive_2(t):
        frm = peer_y(t)
        copy_y(p2s.at[frm], p2r.at[frm], s2, frm, frm, frm).wait_recv()

    each(GY, send_2)
    p2r[me_y] = p2s[me_y]
    def tree(terms):
        while len(terms) > 1:
            terms = [a + b for a, b in zip(terms[::2], terms[1::2])]
        return terms[0]

    def sum_up(q):
        def rows(n, state):
            new = []
            for i, u in enumerate((2 * q, 2 * q + 1)):
                values = [ht[at_y(n * 8 + step, u), :] for step in range(8)]
                for slot, ref in enumerate((wv, wp)):
                    terms = [value * ref[at_y(n * 8 + step, u), :] for step, value in enumerate(values)]
                    new.append(state[2 * i + slot] + tree(terms))
            return new

        sums = lax.fori_loop(0, CY // 8, rows, zeros[:4])
        for i, u in enumerate((2 * q, 2 * q + 1)):
            yrs[u, 0] = sums[2 * i]
            yrs[u, 1] = sums[2 * i + 1]

    substitute(0)
    sum_up(0)
    each(GY, arrive_2)
    row = jnp.concatenate([p2r[2 * j, 0:1, :] + p2r[2 * j + 1, 0:1, :] for j in range(4)], axis=1)
    new_row = 0.5 * cur_row + exact_dot(row, cw2[...], ((1,), (1,)))
    for a in range(4):
        ys[a : a + 1, :] = new_row[:, 128 * a : 128 * a + 128]

    def send_a(t):
        to = peer_y(t)
        copy_y(ys, ga.at[me_y], sa, to, to, me_y).start()

    def arrive_a(t):
        frm = peer_y(t)
        copy_y(ys, ga.at[frm], sa, frm, frm, frm).wait_recv()

    each(GY, send_a)
    ga[me_y] = ys[...]
    for k in range(CAP):
        cur_out[k : k + 1, :] = exact_dot(new_row, spread[k], ((1,), (1,)))
    substitute(1)
    sum_up(1)
    substitute(2)
    sum_up(2)
    substitute(3)
    sum_up(3)
    def send_yr(t):
        to = peer_y(t)
        copy_y(yrs.at[to], yrr.at[me_y], syr, to, to, me_y).start()

    each(GY, send_yr)
    yrr[me_y] = yrs[me_y]
    each(GY, arrive_a)
    for j in range(GY):
        part = ga[j]
        for a in range(4):
            gat[a, j : j + 1, :] = part[a : a + 1, :]

    def send_b(t):
        to = peer_x(t)
        copy_x(gat.at[to // 4], gb.at[me_x], sb, to, to, me_x).start()

    def arrive_b(t):
        frm = peer_x(t)
        copy_x(gat.at[0], gb.at[frm], sb, frm, frm, frm).wait_recv()

    each(GX, send_b)
    gb[me_x] = gat[me_x // 4]
    def drain_x(t):
        to = peer_x(t)
        for q in range(4):
            copy_x(xs.at[q, to], xr.at[q, me_x], xsem.at[q], to, to, me_x).wait_send()
            copy_x(vs.at[q, to], vr.at[q, me_x], vsem.at[q], to, to, me_x).wait_send()
        copy_x(p1s.at[to], p1r.at[me_x], s1, to, to, me_x).wait_send()
        copy_x(pas.at[0:SENT], par.at[me_x, 0:SENT], spa, to, to, me_x).wait_send()

    def drain_y(t):
        to = peer_y(t)
        copy_y(p2s.at[to], p2r.at[me_y], s2, to, to, me_y).wait_send()
        copy_y(ycs.at[to], ycr.at[me_y], syc, to, to, me_y).wait_send()
        copy_y(yrs.at[to], yrr.at[me_y], syr, to, to, me_y).wait_send()
        copy_y(pks, pkr.at[me_y], spk, to, to, me_y).wait_send()

    def arrive_pk(t):
        frm = peer_y(t)
        copy_y(pks, pkr.at[frm], spk, frm, frm, frm).wait_recv()

    def arrive_yc(t):
        frm = peer_y(t)
        copy_y(ycs.at[frm], ycr.at[frm], syc, frm, frm, frm).wait_recv()

    each(GY, arrive_pk)
    each(GY, arrive_yc)
    share_z = ((me_y // 2) * 128 + lax.broadcasted_iota(jnp.int32, (128, 128), 0)).astype(F32)
    share_x = (lax.rem(me_y, 2) * 8 + lax.broadcasted_iota(jnp.int32, (8, 128), 0)).astype(F32)

    def build_share(r):
        info = pkr[r]
        for k in range(CAP):
            zhot[r, :, 128 * k : 128 * k + 128] = jnp.where(share_z == info[12 + k : 13 + k, :], 1.0, 0.0).astype(BF16)
            match = share_x == info[8 + k : 9 + k, :]
            for slot in range(2):
                weight = info[4 * slot + k : 4 * slot + k + 1, :]
                xmask[r, slot, :, 128 * k : 128 * k + 128] = jnp.where(match, weight, 0.0)

    each(GY, build_share, 0)
    q_y = ycr[0, 0] + ycr[0, 1] + ycr[1, 2]
    for r in range(1, GY):
        a = ycr[r, 0]
        m = inverse(a + q_y)
        yk[r, 0] = a * m
        yk[r, 1] = m
        more = ycr[r + 1, 2] if r < GY - 1 else 1.0
        q_y = ycr[r, 1] + more + a * m * q_y
    yk[0, 0] = inverse(q_y)
    row_16 = lax.broadcasted_iota(jnp.int32, (CX, 128), 0)

    def build_hot(y):
        rows = row_16 + y * CX
        for k in range(CAP):
            match = jnp.where(rows == place_r[k : k + 1, :], 1.0, 0.0)
            hot[pl.ds(pl.multiple_of(y * CX, CX), CX), quarter(k)] = match.astype(BF16)

    def build_some(n):
        for step in range(8):
            build_hot(n * 8 + step)

    each(CY // 8, build_some, 0)
    each(GX, drain_x)
    each(GY, drain_y)
    each(GX, arrive_b)

    back = gb[...].reshape(128, 128)
    gbt[...] = back.T
    mine_rows = gbt[pl.ds(pl.multiple_of(lax.rem(me_x, 4) * 32, 32), 32), :]
    extra = []
    for r in range(GY):
        values = jnp.concatenate([mine_rows[CAP * r + k : CAP * r + k + 1, :] for k in range(CAP)], axis=1)
        parts = jnp.concatenate([xmask[r, 0] * values, xmask[r, 1] * values], axis=0)
        high = parts.astype(BF16)
        low = (parts - high.astype(F32)).astype(BF16)
        product = lax.dot_general(
            jnp.concatenate([high, low], axis=0), zhot[r], (((1,), (1,)), ((), ())), preferred_element_type=F32
        )
        extra.append((product[0:8] + product[16:24], product[8:16] + product[24:32]))

    def arrive_yr(t):
        frm = peer_y(t)
        copy_y(yrs.at[frm], yrr.at[frm], syr, frm, frm, frm).wait_recv()

    each(GY, arrive_yr)
    phi = (yrr[0, 0] + extra[0][0]) + (yrr[1, 1] + extra[1][1])
    phis = [phi]
    for r in range(1, GY):
        phi = (yrr[r, 0] + extra[r][0]) + yk[r, 0] * phi
        if r < GY - 1:
            phi = phi + (yrr[r + 1, 1] + extra[r + 1][1])
        phis.append(phi)
    value = phi * yk[0, 0]
    for r in range(GY - 1, 0, -1):
        yvs[r, 1] = value
        value = yk[r, 1] * phis[r - 1] + yk[r, 0] * value
        yvs[r, 0] = value
    yvs[0, 1] = value
    yvs[0, 0] = jnp.zeros((8, 128), F32)

    def send_yv(t):
        to = peer_y(t)
        copy_y(yvs.at[to], yvr.at[me_y], syv, to, to, me_y).start()

    def arrive_yv(t):
        frm = peer_y(t)
        copy_y(yvs.at[frm], yvr.at[frm], syv, frm, frm, frm).wait_recv()

    each(GY, send_yv)
    yvr[me_y] = yvs[me_y]

    lane_k = lax.broadcasted_iota(jnp.int32, (128, NZ), 1)
    for k in range(CAP):
        value = jnp.sum(jnp.where(lanes == mine + k, back, 0.0), axis=1, keepdims=True) * (INJECT / KY)
        spot = jnp.where(lane_k == zcol[:, k : k + 1], value, 0.0)
        high = spot.astype(BF16)
        bhl[128 * k : 128 * k + 128, :] = high
        bhl[WIRE + 128 * k : WIRE + 128 * k + 128, :] = (spot - high.astype(F32)).astype(BF16)

    def scatter(n, added):
        part = hot[pl.ds(pl.multiple_of(n * 256, 256), 256), :]
        added[...] = jnp.dot(jnp.concatenate([part, part], axis=1), bhl[...], preferred_element_type=F32)

    def eliminate_y(n, added, state):
        for step in range(16):
            y = n * 16 + step
            new = []
            for u in range(UNITS):
                row = step * CX + (u % 2) * 8
                more = added[row : row + 8, quarter(u // 2)]
                b = ((ht[at_y(y, u), :] + more) + state[u]) * my[at_y(y, u), :]
                ht[at_y(y, u), :] = b
                new.append(b)
            state = new
        return state

    def forward_y(n, state):
        scatter(2 * n + 1, added1)
        state = eliminate_y(2 * n, added0, state)
        scatter(jnp.minimum(2 * n + 2, CY // 16 - 1), added0)
        return eliminate_y(2 * n + 1, added1, state)

    scatter(0, added0)
    lax.fori_loop(0, CY // 32, forward_y, zeros)
    each(GY, arrive_yv)

    ends[...] = yvr[...]

    def drain_late_x(t):
        copy_x(gat.at[0], gb.at[me_x], sb, peer_x(t), peer_x(t), me_x).wait_send()

    def drain_late_y(t):
        to = peer_y(t)
        copy_y(ys, ga.at[me_y], sa, to, to, me_y).wait_send()
        copy_y(yvs.at[to], yvr.at[me_y], syv, to, to, me_y).wait_send()

    each(GX, drain_late_x)
    each(GY, drain_late_y)


def deliver(ht, my, ay, ends, cur_in, out, cur_out, staged, sems):
    rows = staged.reshape(4 * PLANE, 128)
    west = [ends[u, 0] for u in range(UNITS)]
    last = [ends[u, 1] for u in range(UNITS)]

    def copies(c):
        place = pl.ds(pl.multiple_of(c * 8, 8), 8)
        return [
            pltpu.make_async_copy(staged.at[q, c], out.at[:, place, 128 * q : 128 * q + 128], sems.at[q, c])
            for q in range(4)
        ]

    def put(y, value):
        for u in range(UNITS):
            start = (u // 2) * PLANE + (y // 8) * (8 * CX) + (u % 2) * 64 + lax.rem(y, 8)
            rows[pl.ds(start, 8, stride=8), :] = value[u]

    def step(y, value):
        new = []
        for u in range(UNITS):
            at = pl.ds(pl.multiple_of(u * (8 * CY) + y * 8, 8), 8)
            new.append((ht[at, :] + ay[at, :] * west[u]) + my[at, :] * value[u])
        put(y, new)
        return new

    def send(c):
        for copy in copies(c):
            copy.start()

    def chunk(n, value):
        c = CY // 8 - 1 - n
        for back in range(8):
            value = step(c * 8 + 7 - back, value)
        send(c)
        return value

    put(CY - 1, last)
    value = last
    for back in range(1, 8):
        value = step(CY - 1 - back, value)
    send(CY // 8 - 1)
    lax.fori_loop(1, CY // 8, chunk, value)
    cur_out[...] = cur_in[...]

    def wait(c, carry):
        for copy in copies(c):
            copy.wait()
        return carry

    lax.fori_loop(0, CY // 8, wait, 0)


def local(field, conduct, seg_cell, seg_count, currents, coupling):
    hbm = pl.BlockSpec(memory_space=pltpu.HBM)
    vmem = pl.BlockSpec(memory_space=pltpu.VMEM)
    cells = seg_cell[0].T
    block = lambda *shape: pltpu.VMEM(shape, F32)
    sems = lambda count: pltpu.SemaphoreType.DMA((2, count))
    scratch = [
        block(4, GX, CX, 8, 128),
        block(4, GX, CX, 8, 128),
        block(4, GX, CX, 8, 128),
        block(4, GX, CX, 8, 128),
        block(4, GX, 5, 8, 128),
        block(4, GX, 5, 8, 128),
        block(4, GX, 2, 8, 128),
        block(4, GX, 2, 8, 128),
        pltpu.VMEM((WIRE, WIRE), BF16),
        pltpu.VMEM((PLANE, WIRE), BF16),
        pltpu.VMEM((2 * WIRE, NZ), BF16),
        block(WIRE, 128),
        pltpu.VMEM((128, 128), jnp.int32),
        pltpu.VMEM((CAP, 128), jnp.int32),
        pltpu.VMEM((1, 128), jnp.int32),
        block(CAP, 128),
        pltpu.VMEM((CAP, 128), jnp.int32),
        pltpu.SMEM((CAP, 128), jnp.int32),
        pltpu.VMEM((CAP, 128), jnp.int32),
        pltpu.SMEM((CAP, 128), jnp.int32),
        block(WIRE, 128),
        block(16, 128),
        block(GX, 16, 128),
        pltpu.VMEM((GX, 128, WIRE), BF16),
        block(GX, 8, WIRE),
        block(128, 128),
        pltpu.VMEM((WIRE, WIRE), BF16),
        block(4 * PLANE, 128),
        block(4 * PLANE, 128),
        block(WIRE, 128),
        block(16, 128),
        block(GY, 16, 128),
        pltpu.VMEM((GY, 128, WIRE), BF16),
        block(GY, 2, 8, WIRE),
        block(128, 128),
        block(GY, 2, 8, 128),
        block(256, NZ),
        block(256, NZ),
        block(GX, 8, 128),
        block(GX, 8, 128),
        block(GY, 8, 128),
        block(GY, 8, 128),
        block(8, 128),
        block(GY, 8, 128),
        block(4, 8, 128),
        block(GX, 8, 128),
        block(GY, 3, 8, 128),
        block(GY, 3, 8, 128),
        block(GY, 2, 8, 128),
        block(GY, 2, 8, 128),
        block(GY, 2, 8, 128),
        block(GY, 2, 8, 128),
        pltpu.SemaphoreType.DMA((GX, 4)),
        pltpu.SemaphoreType.DMA((GX, 4)),
        pltpu.SemaphoreType.DMA,
        pltpu.SemaphoreType.DMA((4, 2, GX)),
        pltpu.SemaphoreType.DMA((4, 2, GX)),
        sems(GX),
        sems(GY),
        sems(GY),
        sems(GX),
        sems(GY),
        sems(GY),
        sems(GY),
        sems(GY),
        sems(GX),
        pltpu.SemaphoreType.DMA((3,)),
        pltpu.SemaphoreType.DMA((2,)),
    ]
    rows = pltpu.VMEM((4 * PLANE, 128), F32)
    *parts, currents_next = pl.pallas_call(
        kernel,
        out_shape=(rows, rows, rows, pltpu.VMEM((GY, 2, 8, 128), F32), pltpu.VMEM((CAP, 128), F32)),
        in_specs=[hbm] * 6,
        out_specs=(vmem,) * 5,
        scratch_shapes=scratch,
        compiler_params=pltpu.CompilerParams(
            collective_id=0, has_side_effects=True, vmem_limit_bytes=49 * 1024 * 1024
        ),
    )(field, conduct, cells, seg_count, currents[0].T, coupling[0])
    field_next, currents_next = pl.pallas_call(
        deliver,
        out_shape=(
            jax.ShapeDtypeStruct((CX, CY, NZ), F32),
            jax.ShapeDtypeStruct((CAP, 128), F32),
        ),
        in_specs=[vmem] * 5,
        out_specs=(hbm, vmem),
        scratch_shapes=[block(4, GX, CX, 8, 128), pltpu.SemaphoreType.DMA((4, GX))],
        compiler_params=pltpu.CompilerParams(vmem_limit_bytes=6 * 1024 * 1024),
    )(*parts, currents_next)
    return field_next, currents_next.T[None]


def solution(mesh):
    placed = (
        P("gx", "gy", None),
        P("gx", "gy", None),
        P(("gx", "gy"), None, None),
        P(("gx", "gy"), None),
        P(("gx", "gy"), None, None),
        P(("gx", "gy"), None, None),
    )
    return jax.shard_map(
        local,
        mesh=mesh,
        in_specs=placed,
        out_specs=(P("gx", "gy", None), P(("gx", "gy"), None, None)),
        check_vma=False,
    )
```
